512 devices in a mesh: dp: 128 (over y_lo, z, x), mp: 4 (over y_hi, core).
Axes of the slice: x: 4, y: 4 (y_hi: 2, y_lo: 2; y = y_hi * 2 + y_lo), z: 16, core: 2. Of those that a mesh axis runs over, the one named last changes fastest.
Arguments:
- vision_encoder_output: bfloat16 [16384, 6144], P('dp', 'mp'), may hold values from -6 to 6
- sentence_encoder_output: bfloat16 [16384, 6144], P('dp', 'mp'), may hold values from -6 to 6
- vision_mapping_matrix: bfloat16 [6144, 512], P('mp'), may hold values from -0.078125 to 0.078125
- sentence_mapping_matrix: bfloat16 [6144, 512], P('mp'), may hold values from -0.078125 to 0.078125
- similarity_sharpness: float32 [1], replicated, may hold values from 20 to 60
- score_offset: float32 [1], replicated, may hold values from -4 to -1
Outputs:
- image_grad: bfloat16 [16384, 6144], P('dp', 'mp')
- text_grad: bfloat16 [16384, 6144], P('dp', 'mp')
The draws below stay inside these ranges and needn't reach their ends.
All inputs are finite; a program needn't handle non-finite values.
Results may differ from the reference program's by a relative error of at most 0.033.
Values may be sent and summed in bfloat16 or wider, within the bound.
No kernel may reach another device: no remote copies, remote signals or barrier semaphores. Data moves between devices by JAX's collectives and lax.ppermute only.
A program may use at most 64 MiB of HBM per device.

```python
import math
import jax
import jax.numpy as jnp
from jax import lax

D = 6144
E = 512
BATCH = 16384


def block_levels(own_key, shape, split, least, largest):
    def one(axis_at, shards_of):
        heights = jax.random.uniform(jax.random.fold_in(jax.random.fold_in(own_key, 6), axis_at), (shards_of,), jnp.float32, least / len(split), largest / len(split))
        return jnp.repeat(jnp.exp(heights), shape[axis_at] // shards_of).reshape((-1,) + (1,) * (len(shape) - axis_at - 1))

    level = one(*split[0])
    for cut in split[1:]:
        level = level * one(*cut)
    return level


def normal_values(rng, extent, deviation, limit, split=(), kind=jnp.bfloat16):
    drawn = jax.random.normal(rng, extent, jnp.float32) * deviation
    if len(split) > 0:
        drawn = block_levels(rng, extent, split, -0.22, 0.18) * drawn
    return jnp.clip(drawn, min=-limit, max=limit).astype(kind)


def setup_inputs(seed: int = 0) -> dict:
    seeds = jax.random.split(jax.random.key(seed), 7)
    return {
        "vision_encoder_output": normal_values(seeds[0], (BATCH, D), 1.0, 6.0, ((0, 128), (1, 4))),
        "sentence_encoder_output": normal_values(seeds[1], (BATCH, D), 1.0, 6.0, ((0, 128), (1, 4))),
        "vision_mapping_matrix": normal_values(seeds[2], (D, E), D ** -0.5, 0.078125, ((0, 4),)),
        "sentence_mapping_matrix": normal_values(seeds[3], (D, E), D ** -0.5, 0.078125, ((0, 4),)),
        "similarity_sharpness": jnp.clip(jnp.exp(jax.random.uniform(seeds[4], (1,), jnp.float32, math.log(20.0), math.log(60.0))), 20.0, 60.0),
        "score_offset": jnp.clip(jax.random.uniform(seeds[5], (1,), jnp.float32, -4.0, -1.0), -4.0, -1.0),
    }


EPS = 1e-06

def normalize(embed):
    inv = lax.rsqrt(lax.optimization_barrier(jnp.sum(embed * embed, axis=1, keepdims=True)) + EPS)
    return (inv, embed * inv)

def backward(grad, inv, unit):
    along = lax.optimization_barrier(jnp.sum(grad * unit, axis=1, keepdims=True))
    return (inv * (grad - along * unit)).astype(jnp.bfloat16)

def reference(vision_encoder_output, sentence_encoder_output, vision_mapping_matrix, sentence_mapping_matrix, similarity_sharpness, score_offset):
    img_embed = jnp.dot(vision_encoder_output, vision_mapping_matrix, preferred_element_type=jnp.float32)
    txt_embed = jnp.dot(sentence_encoder_output, sentence_mapping_matrix, preferred_element_type=jnp.float32)
    inv_img, picture_unit_rows = normalize(img_embed)
    inv_txt, unit_txt = normalize(txt_embed)
    img_b = picture_unit_rows.astype(jnp.bfloat16)
    txt_b = unit_txt.astype(jnp.bfloat16)
    score_multiplier = similarity_sharpness[0]
    shift = score_offset[0]
    block = math.gcd(512, BATCH)
    count = BATCH // block
    blocks = img_b.reshape(count, block, E)
    starts = jnp.arange(count, dtype=jnp.int32) * block
    columns = jnp.arange(BATCH, dtype=jnp.int32)
    local_rows = jnp.arange(block, dtype=jnp.int32)

    def step(caption_gradient, inputs):
        rows_blk, start = inputs
        logits = score_multiplier * lax.dot_general(rows_blk, txt_b, (((1,), (1,)), ((), ())), preferred_element_type=jnp.float32) + shift
        positive = (start + local_rows)[:, None] == columns[None, :]
        sign = jnp.where(positive, jnp.float32(1.0), jnp.float32(-1.0))
        coef = (score_multiplier * -sign * jax.nn.sigmoid(-sign * logits)).astype(jnp.bfloat16)
        grad_rows = jnp.dot(coef, txt_b, preferred_element_type=jnp.float32)
        caption_gradient = caption_gradient + lax.dot_general(coef, rows_blk, (((0,), (0,)), ((), ())), preferred_element_type=jnp.float32)
        return (caption_gradient, grad_rows)
    caption_gradient, grad_rows = lax.scan(step, jnp.zeros((BATCH, E), jnp.float32), (blocks, starts))
    grad_img = grad_rows.reshape(BATCH, E)
    delta_img = backward(grad_img, inv_img, picture_unit_rows)
    delta_txt = backward(caption_gradient, inv_txt, unit_txt)
    image_grad = lax.dot_general(delta_img, vision_mapping_matrix, (((1,), (1,)), ((), ())), preferred_element_type=jnp.float32).astype(jnp.bfloat16)
    text_grad = lax.dot_general(delta_txt, sentence_mapping_matrix, (((1,), (1,)), ((), ())), preferred_element_type=jnp.float32).astype(jnp.bfloat16)
    return (image_grad, text_grad)
```

```python
import jax
import jax.numpy as jnp
from jax import lax
from jax.sharding import Mesh
from jax.sharding import PartitionSpec as P

EPS = 1e-06
BF = jnp.bfloat16
F32 = jnp.float32
GROUP = ("yhi", "core")
LINE = "z"
PLANE = ("ylo", "x", "yhi", "core")


def normalize(embed):
    inv = lax.rsqrt(jnp.sum(embed * embed, axis=1, keepdims=True) + EPS)
    return (inv, embed * inv)


def backward(grad, inv, unit):
    along = jnp.sum(grad * unit, axis=1, keepdims=True)
    return (inv * (grad - along * unit)).astype(BF)


def exchange_sum(parts, axis):
    got = lax.all_to_all(parts.astype(BF), axis, 0, 0)
    return jnp.sum(got.astype(F32), axis=0)


def gather_rows(rows, axis):
    peers = lax.axis_size(axis)
    wide = jnp.broadcast_to(rows[None], (peers,) + rows.shape)
    return lax.all_to_all(wide, axis, 0, 0).reshape(peers * rows.shape[0], rows.shape[1])


def shards(vision, sentence, vision_map, sentence_map, sharpness, offset):
    rows = vision.shape[0]
    width = vision_map.shape[1]
    members = lax.axis_size(GROUP)
    quarter = rows // members
    t = sharpness[0]
    shift = offset[0]
    embed = jnp.concatenate(
        [
            jnp.dot(vision, vision_map, preferred_element_type=F32),
            jnp.dot(sentence, sentence_map, preferred_element_type=F32),
        ],
        axis=1,
    ).astype(BF)
    embed = exchange_sum(embed.reshape(members, quarter, 2 * width), GROUP)
    inv_img, unit_img = normalize(embed[:, :width])
    inv_txt, unit_txt = normalize(embed[:, width:])
    img_b = lax.all_gather(unit_img.astype(BF), LINE, axis=0, tiled=True)
    txt_b = gather_rows(unit_txt.astype(BF), PLANE)
    n_img, n_txt = img_b.shape[0], txt_b.shape[0]

    logits = t * lax.dot_general(img_b, txt_b, (((1,), (1,)), ((), ())), preferred_element_type=F32) + shift
    image_at = lax.broadcasted_iota(jnp.int32, (n_img, n_txt), 0) - lax.axis_index(LINE) * quarter
    text_at = lax.broadcasted_iota(jnp.int32, (n_img, n_txt), 1) - lax.axis_index(PLANE) * quarter
    own = (image_at == text_at) & (image_at >= 0) & (image_at < quarter)
    sign = jnp.where(own, F32(1.0), F32(-1.0))
    coef = (t * -sign * jax.nn.sigmoid(-sign * logits)).astype(BF)
    grad_img = jnp.dot(coef, txt_b, preferred_element_type=F32)
    grad_txt = lax.dot_general(coef, img_b, (((0,), (0,)), ((), ())), preferred_element_type=F32)

    grad_img = exchange_sum(grad_img.reshape(-1, quarter, width), LINE)
    grad_txt = exchange_sum(grad_txt.reshape(-1, quarter, width), PLANE)
    delta = jnp.concatenate(
        [backward(grad_img, inv_img, unit_img), backward(grad_txt, inv_txt, unit_txt)], axis=1
    )
    delta = lax.all_gather(delta, GROUP, axis=0, tiled=True)
    image_grad = lax.dot_general(
        delta[:, :width], vision_map, (((1,), (1,)), ((), ())), preferred_element_type=F32
    ).astype(BF)
    text_grad = lax.dot_general(
        delta[:, width:], sentence_map, (((1,), (1,)), ((), ())), preferred_element_type=F32
    ).astype(BF)
    return (image_grad, text_grad)


def solution(mesh):
    x, ylo = 4, 2
    z = mesh.shape["dp"] // (x * ylo)
    fine = Mesh(mesh.devices.reshape(ylo, z, x, 2, 2), ("ylo", "z", "x", "yhi", "core"))
    dp, mp = ("ylo", "z", "x"), ("yhi", "core")
    in_specs = (P(dp, mp), P(dp, mp), P(mp, None), P(mp, None), P(), P())
    out_specs = (P(dp, mp), P(dp, mp))
    return jax.shard_map(shards, mesh=fine, in_specs=in_specs, out_specs=out_specs, check_vma=False)
```

```python
import jax
import jax.numpy as jnp
from jax import lax
from jax.sharding import Mesh
from jax.sharding import PartitionSpec as P

EPS = 1e-06
BF = jnp.bfloat16
F32 = jnp.float32
GROUP = ("core", "yhi")


def normalize(embed):
    inv = lax.rsqrt(jnp.sum(embed * embed, axis=1, keepdims=True) + EPS)
    return (inv, embed * inv)


def backward(grad, inv, unit):
    along = jnp.sum(grad * unit, axis=1, keepdims=True)
    return (inv * (grad - along * unit)).astype(BF)


def shifted(x, axis, by):
    peers = lax.axis_size(axis)
    return lax.ppermute(x, axis, [(i, (i + by) % peers) for i in range(peers)])


def exchange_sum(parts, axis):
    got = lax.all_to_all(parts.astype(BF), axis, 0, 0)
    return jnp.sum(got.astype(F32), axis=0)


def mutual_sum(x, axis):
    x = x.astype(BF)
    return x.astype(F32) + shifted(x, axis, 1).astype(F32)


def other_half(x, core):
    return jnp.where(core == 0, x[1], x[0])


def own_half(x, core):
    return jnp.where(core == 0, x[0], x[1])


def gather_text(rows):
    rows = jnp.stack([rows, shifted(rows, "ylo", 1)])
    rows = jnp.stack([rows] + [shifted(rows, "x", k) for k in range(1, lax.axis_size("x"))])
    rows = jnp.stack([rows, shifted(rows, "core", 1)])
    return rows


def scatter_text(grad):
    grad = grad[0] + shifted(grad[1].astype(BF), "core", 1).astype(F32)
    back = [shifted(grad[k].astype(BF), "x", -k).astype(F32) for k in range(1, grad.shape[0])]
    grad = grad[0] + sum(back)
    grad = grad[0] + shifted(grad[1].astype(BF), "ylo", 1).astype(F32)
    return mutual_sum(grad, "yhi")


def shards(vision, sentence, vision_map, sentence_map, sharpness, offset):
    rows = vision.shape[0]
    width = vision_map.shape[1]
    quarter = rows // lax.axis_size(GROUP)
    half = 2 * quarter
    core, yhi, z = (lax.axis_index(a) for a in ("core", "yhi", "z"))
    depth = lax.axis_size("z")
    t = sharpness[0]
    shift = offset[0]

    img = jnp.dot(vision, vision_map, preferred_element_type=F32)
    img = exchange_sum(img.reshape(-1, quarter, width), GROUP)
    inv_img, unit_img = normalize(img)
    img_b = jnp.broadcast_to(unit_img.astype(BF)[None], (depth, quarter, width))
    img_b = lax.all_to_all(img_b, "z", 0, 0).reshape(depth * quarter, width)

    txt = jnp.dot(sentence, sentence_map, preferred_element_type=F32).reshape(2, half, width)
    txt = own_half(txt, core) + shifted(other_half(txt, core).astype(BF), "core", 1).astype(F32)
    txt = mutual_sum(txt, "yhi")
    inv_txt, unit_txt = normalize(txt)
    txt_b = gather_text(unit_txt.astype(BF))
    shape = txt_b.shape
    txt_b = txt_b.reshape(-1, width)
    n_img, n_txt = img_b.shape[0], txt_b.shape[0]

    logits = t * lax.dot_general(img_b, txt_b, (((1,), (1,)), ((), ())), preferred_element_type=F32) + shift
    image_at = lax.broadcasted_iota(jnp.int32, (n_img, n_txt), 0) - z * quarter
    text_at = lax.broadcasted_iota(jnp.int32, (n_img, n_txt), 1) - yhi * quarter
    own = (image_at == text_at) & (image_at >= 0) & (image_at < quarter)
    sign = jnp.where(own, F32(1.0), F32(-1.0))
    coef = (t * -sign * jax.nn.sigmoid(-sign * logits)).astype(BF)
    grad_img = jnp.dot(coef, txt_b, preferred_element_type=F32)
    grad_txt = lax.dot_general(coef, img_b, (((0,), (0,)), ((), ())), preferred_element_type=F32)

    grad_img = exchange_sum(grad_img.reshape(depth, quarter, width), "z")
    grad_txt = scatter_text(grad_txt.reshape(shape))
    delta_txt = lax.all_gather(backward(grad_txt, inv_txt, unit_txt), "core", axis=0, tiled=True)
    text_grad = lax.dot_general(
        delta_txt, sentence_map, (((1,), (1,)), ((), ())), preferred_element_type=F32
    ).astype(BF)
    delta_img = lax.all_gather(backward(grad_img, inv_img, unit_img), GROUP, axis=0, tiled=True)
    image_grad = lax.dot_general(
        delta_img, vision_map, (((1,), (1,)), ((), ())), preferred_element_type=F32
    ).astype(BF)
    return (image_grad, text_grad)


def solution(mesh):
    x, ylo = 4, 2
    z = mesh.shape["dp"] // (x * ylo)
    fine = Mesh(mesh.devices.reshape(ylo, z, x, 2, 2), ("ylo", "z", "x", "yhi", "core"))
    dp, mp = ("ylo", "z", "x"), ("yhi", "core")
    in_specs = (P(dp, mp), P(dp, mp), P(mp, None), P(mp, None), P(), P())
    out_specs = (P(dp, mp), P(dp, mp))
    return jax.shard_map(shards, mesh=fine, in_specs=in_specs, out_specs=out_specs, check_vma=False)
```

```python
import jax
import jax.numpy as jnp
from jax import lax
from jax.sharding import Mesh
from jax.sharding import PartitionSpec as P

EPS = 1e-06
BF = jnp.bfloat16
F32 = jnp.float32
AXES = ("ylo", "z", "x", "yhi", "core")
GROUP = ("yhi", "core")
PLANE = ("ylo", "x", "yhi")


def normalize(embed):
    inv = lax.rsqrt(jnp.sum(embed * embed, axis=1, keepdims=True) + EPS)
    return (inv, embed * inv)


def backward(grad, inv, unit):
    along = jnp.sum(grad * unit, axis=1, keepdims=True)
    return (inv * (grad - along * unit)).astype(BF)


def tower_groups(sizes):
    ylo, z, x, yhi, core = sizes

    def at(a, b, c, d, e):
        return (((a * z + b) * x + c) * yhi + d) * core + e

    lines = [[at(a, b, c, d, 0) for b in range(z)] for a in range(ylo) for c in range(x) for d in range(yhi)]
    planes = [[at(a, b, c, d, 1) for a in range(ylo) for c in range(x) for d in range(yhi)] for b in range(z)]
    return lines + planes


def shards(vision, sentence, vision_map, sentence_map, sharpness, offset):
    rows = vision.shape[0]
    width = vision_map.shape[1]
    own = rows // 2
    core, z, plane = (lax.axis_index(a) for a in ("core", "z", PLANE))
    groups = tower_groups([lax.axis_size(a) for a in AXES])
    peers = len(groups[0])
    t = sharpness[0]
    shift = offset[0]

    def meet(parts):
        return lax.all_to_all(parts, AXES, 0, 0, axis_index_groups=groups)

    parts = jnp.stack(
        [
            jnp.dot(vision, vision_map, preferred_element_type=F32).astype(BF).reshape(2, own, width),
            jnp.dot(sentence, sentence_map, preferred_element_type=F32).astype(BF).reshape(2, own, width),
        ],
        axis=1,
    ).reshape(4, own, width)
    embed = jnp.sum(lax.all_to_all(parts, GROUP, 0, 0).astype(F32), axis=0)
    inv, unit = normalize(embed)

    mine = meet(jnp.broadcast_to(unit.astype(BF)[None], (peers, own, width))).reshape(peers * own, width)
    other = lax.ppermute(mine, "core", [(0, 1), (1, 0)])
    logits = t * lax.dot_general(mine, other, (((1,), (1,)), ((), ())), preferred_element_type=F32) + shift
    mine_at = lax.broadcasted_iota(jnp.int32, logits.shape, 0) - jnp.where(core == 0, z, plane) * own
    other_at = lax.broadcasted_iota(jnp.int32, logits.shape, 1) - jnp.where(core == 0, plane, z) * own
    positive = (mine_at == other_at) & (mine_at >= 0) & (mine_at < own)
    sign = jnp.where(positive, F32(1.0), F32(-1.0))
    coef = (t * -sign * jax.nn.sigmoid(-sign * logits)).astype(BF)
    grad = jnp.dot(coef, other, preferred_element_type=F32).astype(BF)

    grad = jnp.sum(meet(grad.reshape(peers, own, width)).astype(F32), axis=0)
    delta = lax.all_gather(backward(grad, inv, unit), GROUP, axis=0).reshape(2, 2, own, width)
    image_grad = lax.dot_general(
        delta[:, 0].reshape(rows, width), vision_map, (((1,), (1,)), ((), ())), preferred_element_type=F32
    ).astype(BF)
    text_grad = lax.dot_general(
        delta[:, 1].reshape(rows, width), sentence_map, (((1,), (1,)), ((), ())), preferred_element_type=F32
    ).astype(BF)
    return (image_grad, text_grad)


def solution(mesh):
    x, ylo = 4, 2
    z = mesh.shape["dp"] // (x * ylo)
    fine = Mesh(mesh.devices.reshape(ylo, z, x, 2, 2), AXES)
    dp, mp = ("ylo", "z", "x"), ("yhi", "core")
    in_specs = (P(dp, mp), P(dp, mp), P(mp, None), P(mp, None), P(), P())
    out_specs = (P(dp, mp), P(dp, mp))
    return jax.shard_map(shards, mesh=fine, in_specs=in_specs, out_specs=out_specs, check_vma=False)
```

```python
import math

import jax
import jax.numpy as jnp
import numpy as np
from jax import lax
from jax.sharding import Mesh
from jax.sharding import PartitionSpec as P

EPS = 1e-06
BF = jnp.bfloat16
F32 = jnp.float32
AXES = ("ylo", "zhi", "zlo", "x", "yhi", "core")
GROUP = ("yhi", "core")
DEPTH = (("zhi",), ("zlo",))
PLANE = (("x",), ("ylo", "yhi"))


def normalize(embed):
    inv = lax.rsqrt(jnp.sum(embed * embed, axis=1, keepdims=True) + EPS)
    return (inv, embed * inv)


def backward(grad, inv, unit):
    along = jnp.sum(grad * unit, axis=1, keepdims=True)
    return (inv * (grad - along * unit)).astype(BF)


def tower_groups(sizes, axes_by_core):
    ids = np.arange(math.prod(sizes)).reshape(sizes)
    groups = []
    for core, axes in enumerate(axes_by_core):
        kept = [i for i, name in enumerate(AXES[:-1]) if name not in axes]
        moved = [AXES.index(name) for name in axes]
        members = math.prod(sizes[i] for i in moved)
        groups += ids[..., core].transpose(kept + moved).reshape(-1, members).tolist()
    return groups


def shards(vision, sentence, vision_map, sentence_map, sharpness, offset):
    rows = vision.shape[0]
    width = vision_map.shape[1]
    own = rows // 2
    core = lax.axis_index("core")
    place = [
        jnp.where(core == 0, lax.axis_index(axes[0]), lax.axis_index(axes[1])) for axes in (PLANE, DEPTH)
    ]
    there = [
        jnp.where(core == 0, lax.axis_index(axes[1]), lax.axis_index(axes[0])) for axes in (PLANE, DEPTH)
    ]
    sizes = [lax.axis_size(a) for a in AXES]
    depth, plane = (tower_groups(sizes, axes) for axes in (DEPTH, PLANE))
    deep, wide = len(depth[0]), len(plane[0])
    t = sharpness[0]
    shift = offset[0]

    def meet(parts, groups):
        return lax.all_to_all(parts, AXES, 0, 0, axis_index_groups=groups)

    def gather(block, groups):
        return meet(jnp.broadcast_to(block[None], (len(groups[0]),) + block.shape), groups)

    def scatter(parts, groups):
        return jnp.sum(meet(parts.astype(BF), groups).astype(F32), axis=0)

    parts = jnp.stack(
        [
            jnp.dot(vision, vision_map, preferred_element_type=F32).astype(BF).reshape(2, own, width),
            jnp.dot(sentence, sentence_map, preferred_element_type=F32).astype(BF).reshape(2, own, width),
        ],
        axis=1,
    ).reshape(4, own, width)
    embed = jnp.sum(lax.all_to_all(parts, GROUP, 0, 0).astype(F32), axis=0)
    inv, unit = normalize(embed)

    mine = gather(gather(unit.astype(BF), depth), plane).reshape(wide * deep * own, width)
    other = lax.ppermute(mine, "core", [(0, 1), (1, 0)])
    logits = t * lax.dot_general(mine, other, (((1,), (1,)), ((), ())), preferred_element_type=F32) + shift
    mine_at = lax.broadcasted_iota(jnp.int32, logits.shape, 0) - (place[0] * deep + place[1]) * own
    other_at = lax.broadcasted_iota(jnp.int32, logits.shape, 1) - (there[0] * deep + there[1]) * own
    positive = (mine_at == other_at) & (mine_at >= 0) & (mine_at < own)
    sign = jnp.where(positive, F32(1.0), F32(-1.0))
    coef = (t * -sign * jax.nn.sigmoid(-sign * logits)).astype(BF)
    grad = jnp.dot(coef, other, preferred_element_type=F32)

    grad = scatter(scatter(grad.reshape(wide, deep, own, width), plane), depth)
    delta = lax.all_gather(backward(grad, inv, unit), GROUP, axis=0).reshape(2, 2, own, width)
    image_grad = lax.dot_general(
        delta[:, 0].reshape(rows, width), vision_map, (((1,), (1,)), ((), ())), preferred_element_type=F32
    ).astype(BF)
    text_grad = lax.dot_general(
        delta[:, 1].reshape(rows, width), sentence_map, (((1,), (1,)), ((), ())), preferred_element_type=F32
    ).astype(BF)
    return (image_grad, text_grad)


def solution(mesh):
    x, ylo = 4, 2
    zlo = 4
    zhi = mesh.shape["dp"] // (x * ylo * zlo)
    fine = Mesh(mesh.devices.reshape(ylo, zhi, zlo, x, 2, 2), AXES)
    dp, mp = ("ylo", "zhi", "zlo", "x"), ("yhi", "core")
    in_specs = (P(dp, mp), P(dp, mp), P(mp, None), P(mp, None), P(), P())
    out_specs = (P(dp, mp), P(dp, mp))
    return jax.shard_map(shards, mesh=fine, in_specs=in_specs, out_specs=out_specs, check_vma=False)
```

```python
import math

import jax
import jax.numpy as jnp
import numpy as np
from jax import lax
from jax.experimental import pallas as pl
from jax.experimental.pallas import tpu as pltpu
from jax.sharding import Mesh
from jax.sharding import PartitionSpec as P

EPS = 1e-06
LOG2E = math.log2(math.e)
BF = jnp.bfloat16
F32 = jnp.float32
MIB = 2**20
AXES = ("ylo", "z", "x", "yhi", "core")
GROUP = ("yhi", "core")
MEET = (("z",), ("ylo", "x", "yhi"))

VMEM = pl.BlockSpec(memory_space=pltpu.VMEM)
SMEM = pl.BlockSpec(memory_space=pltpu.SMEM)
HBM = pl.BlockSpec(memory_space=pltpu.MemorySpace.HBM)


def normalize(embed):
    inv = lax.rsqrt(jnp.sum(embed * embed, axis=1, keepdims=True) + EPS)
    return (inv, embed * inv)


def backward(grad, inv, unit):
    along = jnp.sum(grad * unit, axis=1, keepdims=True)
    return (inv * (grad - along * unit)).astype(BF)


def tower_groups(sizes, axes_by_core):
    ids = np.arange(math.prod(sizes)).reshape(sizes)
    groups = []
    for core, axes in enumerate(axes_by_core):
        kept = [i for i, name in enumerate(AXES[:-1]) if name not in axes]
        moved = [AXES.index(name) for name in axes]
        members = math.prod(sizes[i] for i in moved)
        groups += ids[..., core].transpose(kept + moved).reshape(-1, members).tolist()
    return groups


def heads(vision, sentence, vision_map, sentence_map, chunks=3):
    rows, depth = vision.shape
    width = vision_map.shape[1]
    own, step = rows // 2, depth // chunks

    def kernel(v, s, wv, ws, out, vb, sb, wvb, wsb, sems):
        towers = ((v, wv, vb, wvb), (s, ws, sb, wsb))
        copies = []
        for tower, (x, w, xb, wb) in enumerate(towers):
            for c in range(chunks):
                cut = pl.ds(c * step, step)
                pair = (
                    pltpu.make_async_copy(x.at[:, cut], xb.at[:, cut], sems.at[tower, c, 0]),
                    pltpu.make_async_copy(w.at[cut], wb.at[cut], sems.at[tower, c, 1]),
                )
                for copy in pair:
                    copy.start()
                copies.append(pair)
        for tower, (_, _, xb, wb) in enumerate(towers):
            total = None
            for c in range(chunks):
                for copy in copies[tower * chunks + c]:
                    copy.wait()
                cut = slice(c * step, (c + 1) * step)
                part = jnp.dot(xb[:, cut], wb[cut], preferred_element_type=F32)
                total = part if total is None else total + part
            total = total.astype(BF)
            for half in range(2):
                out[2 * half + tower] = total[half * own : (half + 1) * own]

    return pl.pallas_call(
        kernel,
        out_shape=pltpu.VMEM((4, own, width), BF),
        in_specs=[HBM] * 4,
        out_specs=VMEM,
        scratch_shapes=[
            pltpu.VMEM((rows, depth), BF),
            pltpu.VMEM((rows, depth), BF),
            pltpu.VMEM((depth, width), BF),
            pltpu.VMEM((depth, width), BF),
            pltpu.SemaphoreType.DMA((2, chunks, 2)),
        ],
        compiler_params=pltpu.CompilerParams(vmem_limit_bytes=63 * MIB),
        name="heads",
    )(vision, sentence, vision_map, sentence_map)


def tile(mine, other, scale, place, own, block=256):
    n, width = mine.shape
    m = other.shape[0]
    blocks = n // block

    def kernel(scale_ref, place_ref, mine_ref, other_ref, out_ref):
        t, slope, start = scale_ref[0], scale_ref[1], scale_ref[2]
        first = place_ref[0] // block
        for i in range(blocks):
            at = pl.multiple_of(lax.rem(first + 1 + i, blocks) * block, block)
            dots = lax.dot_general(
                mine_ref[pl.ds(at, block)], other_ref[...], (((1,), (1,)), ((), ())), preferred_element_type=F32
            )
            e = jnp.exp2(dots * slope + start)
            coef = pl.reciprocal(1.0 + e, approx=True)
            if i == blocks - 1:
                col = lax.broadcasted_iota(jnp.int32, (1, m), 1) - place_ref[1]
                row = lax.broadcasted_iota(jnp.int32, (block, 1), 0) + (at - place_ref[0])
                row = jnp.where((row >= 0) & (row < own), row, -m)
                coef = jnp.where(row == col, -e, 1.0) * coef
            sums = jnp.dot(coef.astype(BF), other_ref[...], preferred_element_type=F32)
            out_ref[pl.ds(at, block)] = (t * sums).astype(BF)

    return pl.pallas_call(
        kernel,
        out_shape=pltpu.VMEM((n, width), BF),
        in_specs=[SMEM, SMEM, VMEM, VMEM],
        out_specs=VMEM,
        compiler_params=pltpu.CompilerParams(vmem_limit_bytes=40 * MIB),
        name="tile",
    )(scale, place, mine, other)


def heads_back(delta, vision_map, sentence_map, chunks=3):
    own, width = delta.shape[1:]
    rows, depth = 2 * own, vision_map.shape[0]
    step = depth // chunks

    def kernel(d, wv, ws, image, text, buf, sems):
        copies = []
        for tower, (w, out) in enumerate(((wv, image), (ws, text))):
            x = jnp.concatenate([d[tower], d[2 + tower]], axis=0)
            for c in range(chunks):
                cut = slice(c * step, (c + 1) * step)
                part = lax.dot_general(x, w[cut], (((1,), (1,)), ((), ())), preferred_element_type=F32)
                buf[tower, :, cut] = part.astype(BF)
                copy = pltpu.make_async_copy(buf.at[tower, :, cut], out.at[:, cut], sems.at[tower, c])
                copy.start()
                copies.append(copy)
        for copy in copies:
            copy.wait()

    return pl.pallas_call(
        kernel,
        out_shape=[jax.ShapeDtypeStruct((rows, depth), BF)] * 2,
        in_specs=[VMEM] * 3,
        out_specs=[HBM] * 2,
        scratch_shapes=[pltpu.VMEM((2, rows, depth), BF), pltpu.SemaphoreType.DMA((2, chunks))],
        compiler_params=pltpu.CompilerParams(vmem_limit_bytes=20 * MIB),
        name="heads_back",
    )(delta, vision_map, sentence_map)


def shards(vision, sentence, vision_map, sentence_map, sharpness, offset):
    width = vision_map.shape[1]
    own = vision.shape[0] // 2
    core = lax.axis_index("core")
    at_line, at_plane = (lax.axis_index(axes) * own for axes in MEET)
    place = jnp.where(core == 0, jnp.stack([at_line, at_plane]), jnp.stack([at_plane, at_line]))
    groups = tower_groups([lax.axis_size(a) for a in AXES], MEET)
    peers = len(groups[0])
    t = sharpness[0]
    scale = jnp.stack([t, -LOG2E * t, -LOG2E * offset[0]])

    def meet(parts):
        return lax.all_to_all(parts, AXES, 0, 0, axis_index_groups=groups)

    parts = heads(vision, sentence, vision_map, sentence_map)
    embed = jnp.sum(lax.all_to_all(parts, GROUP, 0, 0).astype(F32), axis=0)
    inv, unit = normalize(embed)

    mine = meet(jnp.broadcast_to(unit.astype(BF)[None], (peers, own, width))).reshape(peers * own, width)
    other = lax.ppermute(mine, "core", [(0, 1), (1, 0)])
    grad = tile(mine, other, scale, place, own)
    grad = jnp.sum(meet(grad.reshape(peers, own, width)).astype(F32), axis=0)
    delta = lax.all_gather(backward(grad, inv, unit), GROUP, axis=0)
    return tuple(heads_back(delta, vision_map, sentence_map))


def solution(mesh):
    x, ylo = 4, 2
    z = mesh.shape["dp"] // (x * ylo)
    fine = Mesh(mesh.devices.reshape(ylo, z, x, 2, 2), AXES)
    dp, mp = ("ylo", "z", "x"), ("yhi", "core")
    in_specs = (P(dp, mp), P(dp, mp), P(mp, None), P(mp, None), P(), P())
    out_specs = (P(dp, mp), P(dp, mp))
    return jax.shard_map(shards, mesh=fine, in_specs=in_specs, out_specs=out_specs, check_vma=False)
```

```python
import math

import jax
import jax.numpy as jnp
import numpy as np
from jax import lax
from jax.experimental import pallas as pl
from jax.experimental.pallas import tpu as pltpu
from jax.sharding import Mesh
from jax.sharding import PartitionSpec as P

EPS = 1e-06
LOG2E = math.log2(math.e)
BF = jnp.bfloat16
F32 = jnp.float32
MIB = 2**20
AXES = ("ylo", "z", "x", "yhi", "core")
GROUP = ("yhi", "core")
PLANE = ("ylo", "x", "yhi")
MEET = (("z",), PLANE)

VMEM = pl.BlockSpec(memory_space=pltpu.VMEM)
SMEM = pl.BlockSpec(memory_space=pltpu.SMEM)
HBM = pl.BlockSpec(memory_space=pltpu.MemorySpace.HBM)


def normalize(embed):
    inv = lax.rsqrt(jnp.sum(embed * embed, axis=1, keepdims=True) + EPS)
    return (inv, embed * inv)


def tower_groups(sizes, axes_by_core):
    ids = np.arange(math.prod(sizes)).reshape(sizes)
    groups = []
    for core, axes in enumerate(axes_by_core):
        kept = [i for i, name in enumerate(AXES[:-1]) if name not in axes]
        moved = [AXES.index(name) for name in axes]
        members = math.prod(sizes[i] for i in moved)
        groups += ids[..., core].transpose(kept + moved).reshape(-1, members).tolist()
    return groups


def heads(vision, sentence, vision_map, sentence_map, chunks=3):
    rows, depth = vision.shape
    width = vision_map.shape[1]
    own, step = rows // 4, depth // chunks

    def kernel(v, s, wv, ws, out, vb, sb, wvb, wsb, sems):
        towers = ((v, wv, vb, wvb), (s, ws, sb, wsb))
        copies = []
        for tower, (x, w, xb, wb) in enumerate(towers):
            for c in range(chunks):
                cut = pl.ds(c * step, step)
                pair = (
                    pltpu.make_async_copy(x.at[:, cut], xb.at[:, cut], sems.at[tower, c, 0]),
                    pltpu.make_async_copy(w.at[cut], wb.at[cut], sems.at[tower, c, 1]),
                )
                for copy in pair:
                    copy.start()
                copies.append(pair)
        for tower, (_, _, xb, wb) in enumerate(towers):
            total = None
            for c in range(chunks):
                for copy in copies[tower * chunks + c]:
                    copy.wait()
                cut = slice(c * step, (c + 1) * step)
                part = jnp.dot(xb[:, cut], wb[cut], preferred_element_type=F32)
                total = part if total is None else total + part
            total = total.astype(BF)
            for q in range(4):
                out[q, :, tower * width : (tower + 1) * width] = total[q * own : (q + 1) * own]

    return pl.pallas_call(
        kernel,
        out_shape=pltpu.VMEM((4, own, 2 * width), BF),
        in_specs=[HBM] * 4,
        out_specs=VMEM,
        scratch_shapes=[
            pltpu.VMEM((rows, depth), BF),
            pltpu.VMEM((rows, depth), BF),
            pltpu.VMEM((depth, width), BF),
            pltpu.VMEM((depth, width), BF),
            pltpu.SemaphoreType.DMA((2, chunks, 2)),
        ],
        compiler_params=pltpu.CompilerParams(vmem_limit_bytes=63 * MIB),
        name="heads",
    )(vision, sentence, vision_map, sentence_map)


def tile(sharpness, offset, near, far, text, own, block=256):
    half, width = near.shape
    n = text.shape[0]
    members = half // own

    def kernel(t_ref, b_ref, near_ref, far_ref, text_ref, out_ref):
        t = t_ref[0]
        slope, start = -LOG2E * t, -LOG2E * b_ref[0]
        z = lax.axis_index("z")
        plane = lax.axis_index(PLANE)

        def sums(rows, other, positive=None):
            dots = lax.dot_general(rows, other, (((1,), (1,)), ((), ())), preferred_element_type=F32)
            e = jnp.exp2(dots * slope + start)
            coef = pl.reciprocal(1.0 + e, approx=True)
            if positive is not None:
                row = lax.broadcasted_iota(jnp.int32, (block, 1), 0) - positive[0]
                row = jnp.where((row >= 0) & (row < own), row, -n)
                col = lax.broadcasted_iota(jnp.int32, (1, other.shape[0]), 1) - positive[1]
                coef = jnp.where(row == col, -e, 1.0) * coef
            return jnp.dot(coef.astype(BF), other, preferred_element_type=F32)

        def turn(blocks, place):
            for i in range(blocks):
                at = lax.rem(place // block + 1 + i, blocks) * block
                yield i == blocks - 1, pl.multiple_of(at, block)

        @pl.when(lax.axis_index("core") == 0)
        def _():
            for owner, rows_ref in enumerate((near_ref, far_ref)):
                for last, at in turn(half // block, z * own):
                    positive = (z * own - at, (2 * plane + owner) * own) if last else None
                    total = t * sums(rows_ref[pl.ds(at, block)], text_ref[...], positive)
                    some = block // own
                    out_ref[pl.ds(at // own, some), owner] = total.astype(BF).reshape(some, own, width)

        @pl.when(lax.axis_index("core") == 1)
        def _():
            for last, at in turn(n // block, 2 * plane * own):
                rows = text_ref[pl.ds(at, block)]
                total = 0.0
                for owner, other_ref in ((1, near_ref), (0, far_ref)):
                    positive = ((2 * plane + owner) * own - at, z * own) if last else None
                    total = total + sums(rows, other_ref[:half], positive)
                some = block // (2 * own)
                total = (t * total).astype(BF).reshape(some, 2, own, width)
                out_ref[pl.ds(at // (2 * own), some)] = total

    return pl.pallas_call(
        kernel,
        out_shape=pltpu.VMEM((members, 2, own, width), BF),
        in_specs=[SMEM, SMEM, VMEM, VMEM, VMEM],
        out_specs=VMEM,
        compiler_params=pltpu.CompilerParams(vmem_limit_bytes=40 * MIB),
        name="tile",
    )(sharpness, offset, near, far, text)


def finish(sums, embed, far, own):
    width = sums.shape[2]
    tail = far.shape[0] - 4 * own

    def kernel(sums_ref, embed_ref, far_ref, out_ref):
        def piece(i):
            return far_ref[tail + i * own : tail + (i + 1) * own].astype(F32)

        for core in range(2):

            @pl.when(lax.axis_index("core") == core)
            def _():
                for owner in range(2):
                    if owner == core:
                        rows = embed_ref[:, core * width : (core + 1) * width]
                    else:
                        rows = piece(2 * core) + piece(2 * core + 1)
                    inv, unit = normalize(rows)
                    at = slice(owner * own, (owner + 1) * own)
                    grad = jnp.sum(sums_ref[:, at].astype(F32), axis=0)
                    along = jnp.sum(grad * unit, axis=1, keepdims=True)
                    out_ref[at] = (inv * (grad - along * unit)).astype(BF)

    return pl.pallas_call(
        kernel,
        out_shape=pltpu.VMEM((2 * own, width), BF),
        in_specs=[VMEM] * 3,
        out_specs=VMEM,
        compiler_params=pltpu.CompilerParams(vmem_limit_bytes=20 * MIB),
        name="finish",
    )(sums, embed, far)


def heads_back(delta, vision_map, sentence_map, chunks=3):
    own, width = delta.shape[1:]
    rows, depth = 2 * own, vision_map.shape[0]
    step = depth // chunks

    def kernel(d, wv, ws, image, text, buf, sems):
        copies = []
        for tower, (w, out) in enumerate(((wv, image), (ws, text))):
            x = jnp.concatenate([d[tower], d[2 + tower]], axis=0)
            for c in range(chunks):
                cut = slice(c * step, (c + 1) * step)
                part = lax.dot_general(x, w[cut], (((1,), (1,)), ((), ())), preferred_element_type=F32)
                buf[tower, :, cut] = part.astype(BF)
                copy = pltpu.make_async_copy(buf.at[tower, :, cut], out.at[:, cut], sems.at[tower, c])
                copy.start()
                copies.append(copy)
        for copy in copies:
            copy.wait()

    return pl.pallas_call(
        kernel,
        out_shape=[jax.ShapeDtypeStruct((rows, depth), BF)] * 2,
        in_specs=[VMEM] * 3,
        out_specs=[HBM] * 2,
        scratch_shapes=[pltpu.VMEM((2, rows, depth), BF), pltpu.SemaphoreType.DMA((2, chunks))],
        compiler_params=pltpu.CompilerParams(vmem_limit_bytes=20 * MIB),
        name="heads_back",
    )(delta, vision_map, sentence_map)


def shards(vision, sentence, vision_map, sentence_map, sharpness, offset):
    width = vision_map.shape[1]
    own = vision.shape[0] // 4
    groups = tower_groups([lax.axis_size(a) for a in AXES], MEET)
    peers = len(groups[0])

    parts = heads(vision, sentence, vision_map, sentence_map)
    embed = jnp.sum(lax.all_to_all(parts, GROUP, 0, 0).astype(F32), axis=0)
    img, txt = embed[:, :width], embed[:, width:]
    img_b, txt_b = (normalize(e)[1].astype(BF) for e in (img, txt))

    text = jnp.broadcast_to(txt_b[None], (2 * peers, own, width))
    text, img_b = lax.optimization_barrier((text, img_b))
    text = lax.all_to_all(text, PLANE + ("core",), 0, 0).reshape(-1, width)
    near = lax.all_gather(img_b, "z", axis=0, tiled=True)
    terms = []
    for e in (img, txt):
        first = e.astype(BF)
        terms += [first, (e - first.astype(F32)).astype(BF)]
    far = lax.ppermute(jnp.concatenate([near] + terms), "core", [(0, 1), (1, 0)])
    grad = tile(sharpness, offset, near, far, text, own)

    grad = lax.all_to_all(grad.reshape(peers, 2 * own, width), AXES, 0, 0, axis_index_groups=groups)
    delta = lax.all_gather(finish(grad, embed, far, own), GROUP, axis=0)
    return tuple(heads_back(delta, vision_map, sentence_map))


def solution(mesh):
    x, ylo = 4, 2
    z = mesh.shape["dp"] // (x * ylo)
    fine = Mesh(mesh.devices.reshape(ylo, z, x, 2, 2), AXES)
    dp, mp = ("ylo", "z", "x"), ("yhi", "core")
    in_specs = (P(dp, mp), P(dp, mp), P(mp, None), P(mp, None), P(), P())
    out_specs = (P(dp, mp), P(dp, mp))
    return jax.shard_map(shards, mesh=fine, in_specs=in_specs, out_specs=out_specs, check_vma=False)
```

```python
import math

import jax
import jax.numpy as jnp
import numpy as np
from jax import lax
from jax.experimental import pallas as pl
from jax.experimental.pallas import tpu as pltpu
from jax.sharding import Mesh
from jax.sharding import PartitionSpec as P

EPS = 1e-06
LOG2E = math.log2(math.e)
BF = jnp.bfloat16
F32 = jnp.float32
MIB = 2**20
AXES = ("ylo", "zhi", "zlo", "x", "yhi", "core")
LINE = ("zhi", "zlo")
PLANE = ("ylo", "x", "yhi")
GROUP = ("yhi", "core")

VMEM = pl.BlockSpec(memory_space=pltpu.VMEM)
SMEM = pl.BlockSpec(memory_space=pltpu.SMEM)
HBM = pl.BlockSpec(memory_space=pltpu.MemorySpace.HBM)


def normalize(embed):
    inv = lax.rsqrt(jnp.sum(embed * embed, axis=1, keepdims=True) + EPS)
    return (inv, embed * inv)


def from_line(sizes, steps):
    ids = np.arange(math.prod(sizes)).reshape(sizes)
    pairs = []
    for core, step in enumerate(steps):
        target = ids[..., core].transpose(1, 2, 0, 3, 4).reshape(sizes[1] * sizes[2], -1)
        source = np.roll(target, -step, axis=0)
        pairs += zip(source.ravel().tolist(), target.ravel().tolist())
    return pairs


def heads(vision, sentence, vision_map, sentence_map, chunks=3):
    rows, depth = vision.shape
    width = vision_map.shape[1]
    own, step = rows // 2, depth // chunks

    def kernel(v, s, wv, ws, out, vb, sb, wvb, wsb, sems):
        towers = ((v, wv, vb, wvb), (s, ws, sb, wsb))
        copies = []
        for tower, (x, w, xb, wb) in enumerate(towers):
            for c in range(chunks):
                cut = pl.ds(c * step, step)
                pair = (
                    pltpu.make_async_copy(x.at[:, cut], xb.at[:, cut], sems.at[tower, c, 0]),
                    pltpu.make_async_copy(w.at[cut], wb.at[cut], sems.at[tower, c, 1]),
                )
                for copy in pair:
                    copy.start()
                copies.append(pair)
        for tower, (_, _, xb, wb) in enumerate(towers):
            total = None
            for c in range(chunks):
                for copy in copies[tower * chunks + c]:
                    copy.wait()
                cut = slice(c * step, (c + 1) * step)
                part = jnp.dot(xb[:, cut], wb[cut], preferred_element_type=F32)
                total = part if total is None else total + part
            total = total.astype(BF)
            for half in range(2):
                out[half, :, tower * width : (tower + 1) * width] = total[half * own : (half + 1) * own]

    return pl.pallas_call(
        kernel,
        out_shape=pltpu.VMEM((2, own, 2 * width), BF),
        in_specs=[HBM] * 4,
        out_specs=VMEM,
        scratch_shapes=[
            pltpu.VMEM((rows, depth), BF),
            pltpu.VMEM((rows, depth), BF),
            pltpu.VMEM((depth, width), BF),
            pltpu.VMEM((depth, width), BF),
            pltpu.SemaphoreType.DMA((2, chunks, 2)),
        ],
        compiler_params=pltpu.CompilerParams(vmem_limit_bytes=63 * MIB),
        name="heads",
    )(vision, sentence, vision_map, sentence_map)


def chip_sums(parts):
    _, _, own, width = parts.shape

    def kernel(parts_ref, given_ref, kept_ref):
        for yhi in range(2):

            @pl.when(lax.axis_index("yhi") == yhi)
            def _():
                total = [parts_ref[0, h].astype(F32) + parts_ref[1, h].astype(F32) for h in (yhi, 1 - yhi)]
                kept_ref[...] = total[0]
                given_ref[...] = total[1].astype(BF)

    return pl.pallas_call(
        kernel,
        out_shape=[pltpu.VMEM((own, width), BF), pltpu.VMEM((own, width), F32)],
        in_specs=[VMEM],
        out_specs=[VMEM, VMEM],
        compiler_params=pltpu.CompilerParams(vmem_limit_bytes=20 * MIB),
        name="chip_sums",
    )(parts)


def units(kept, got, peers):
    own, width = kept.shape[0], kept.shape[1] // 2

    def kernel(kept_ref, got_ref, wide_ref, line_ref, embed_ref):
        towers = [slice(0, width), slice(width, 2 * width)]
        for yhi in range(2):
            for core in range(2):

                @pl.when((lax.axis_index("yhi") == yhi) & (lax.axis_index("core") == core))
                def _():
                    embed = [kept_ref[:, cut] + got_ref[1 - yhi, :, cut].astype(F32) for cut in towers]
                    embed_ref[...] = embed[core]
                    mine = normalize(embed[core])[1].astype(BF)
                    for peer in range(peers):
                        wide_ref[peer] = mine
                    line_ref[...] = normalize(embed[1 - core])[1].astype(BF)

    return pl.pallas_call(
        kernel,
        out_shape=[
            pltpu.VMEM((peers, own, width), BF),
            pltpu.VMEM((own, width), BF),
            pltpu.VMEM((own, width), F32),
        ],
        in_specs=[VMEM] * 2,
        out_specs=[VMEM] * 3,
        compiler_params=pltpu.CompilerParams(vmem_limit_bytes=20 * MIB),
        name="units",
    )(kept, got)


def tile(sharpness, offset, mine, other, own, block=256):
    n, width = mine.shape
    m = other.shape[0]
    blocks = n // block

    def kernel(t_ref, b_ref, mine_ref, other_ref, out_ref):
        t = t_ref[0]
        slope, start = -LOG2E * t, -LOG2E * b_ref[0]
        mine_at, other_at = lax.axis_index(PLANE) * own, lax.axis_index("zhi") * own
        for i in range(blocks):
            at = pl.multiple_of(lax.rem(mine_at // block + 1 + i, blocks) * block, block)
            dots = lax.dot_general(
                mine_ref[pl.ds(at, block)], other_ref[...], (((1,), (1,)), ((), ())), preferred_element_type=F32
            )
            e = jnp.exp2(dots * slope + start)
            coef = pl.reciprocal(1.0 + e, approx=True)
            if i == blocks - 1:
                row = lax.broadcasted_iota(jnp.int32, (block, 1), 0) + (at - mine_at)
                row = jnp.where((row >= 0) & (row < own), row, -m)
                col = lax.broadcasted_iota(jnp.int32, (1, m), 1) - other_at
                coef = jnp.where(row == col, -e, 1.0) * coef
            sums = jnp.dot(coef.astype(BF), other_ref[...], preferred_element_type=F32)
            out_ref[pl.ds(at, block)] = (t * sums).astype(BF)

    return pl.pallas_call(
        kernel,
        out_shape=pltpu.VMEM((n, width), BF),
        in_specs=[SMEM, SMEM, VMEM, VMEM],
        out_specs=VMEM,
        compiler_params=pltpu.CompilerParams(vmem_limit_bytes=40 * MIB),
        name="tile",
    )(sharpness, offset, mine, other)


def finish(sums, embed):
    def kernel(sums_ref, embed_ref, out_ref):
        inv, unit = normalize(embed_ref[...])
        grad = jnp.sum(sums_ref[...].astype(F32), axis=0)
        along = jnp.sum(grad * unit, axis=1, keepdims=True)
        out_ref[...] = (inv * (grad - along * unit)).astype(BF)

    return pl.pallas_call(
        kernel,
        out_shape=pltpu.VMEM(embed.shape, BF),
        in_specs=[VMEM] * 2,
        out_specs=VMEM,
        compiler_params=pltpu.CompilerParams(vmem_limit_bytes=20 * MIB),
        name="finish",
    )(sums, embed)


def heads_back(delta, vision_map, sentence_map, chunks=3):
    own, width = delta.shape[1:]
    rows, depth = 2 * own, vision_map.shape[0]
    step = depth // chunks

    def kernel(d, wv, ws, image, text, buf, sems):
        copies = []
        for tower, (w, out) in enumerate(((wv, image), (ws, text))):
            x = jnp.concatenate([d[tower], d[2 + tower]], axis=0)
            for c in range(chunks):
                cut = slice(c * step, (c + 1) * step)
                part = lax.dot_general(x, w[cut], (((1,), (1,)), ((), ())), preferred_element_type=F32)
                buf[tower, :, cut] = part.astype(BF)
                copy = pltpu.make_async_copy(buf.at[tower, :, cut], out.at[:, cut], sems.at[tower, c])
                copy.start()
                copies.append(copy)
        for copy in copies:
            copy.wait()

    return pl.pallas_call(
        kernel,
        out_shape=[jax.ShapeDtypeStruct((rows, depth), BF)] * 2,
        in_specs=[VMEM] * 3,
        out_specs=[HBM] * 2,
        scratch_shapes=[pltpu.VMEM((2, rows, depth), BF), pltpu.SemaphoreType.DMA((2, chunks))],
        compiler_params=pltpu.CompilerParams(vmem_limit_bytes=20 * MIB),
        name="heads_back",
    )(delta, vision_map, sentence_map)


def shards(vision, sentence, vision_map, sentence_map, sharpness, offset):
    width = vision_map.shape[1]
    own = vision.shape[0] // 2
    sizes = [lax.axis_size(a) for a in AXES]
    peers = lax.axis_size(PLANE)

    parts = lax.all_gather(heads(vision, sentence, vision_map, sentence_map), "core", axis=0)
    given, kept = chip_sums(parts)
    wide, line, embed = units(kept, lax.all_gather(given, "yhi", axis=0), peers)

    wide, line = lax.optimization_barrier((wide, line))
    mine = lax.all_to_all(wide, PLANE, 0, 0).reshape(peers * own, width)
    line = lax.all_gather(line, "zhi", axis=0, tiled=True)
    near = [lax.ppermute(line, AXES, from_line(sizes, steps)) for steps in ((1, 1), (-1, -1), (2, -2))]
    grad = tile(sharpness, offset, mine, jnp.concatenate([line] + near), own)

    grad = lax.all_to_all(grad.reshape(peers, own, width), PLANE, 0, 0)
    delta = lax.all_gather(finish(grad, embed), GROUP, axis=0)
    return tuple(heads_back(delta, vision_map, sentence_map))


def solution(mesh):
    x, ylo, zlo = 4, 2, 4
    zhi = mesh.shape["dp"] // (x * ylo * zlo)
    fine = Mesh(mesh.devices.reshape(ylo, zhi, zlo, x, 2, 2), AXES)
    dp, mp = ("ylo", "zhi", "zlo", "x"), ("yhi", "core")
    in_specs = (P(dp, mp), P(dp, mp), P(mp, None), P(mp, None), P(), P())
    out_specs = (P(dp, mp), P(dp, mp))
    return jax.shard_map(shards, mesh=fine, in_specs=in_specs, out_specs=out_specs, check_vma=False)
```

```python
import math

import jax
import jax.numpy as jnp
import numpy as np
from jax import lax
from jax.experimental import pallas as pl
from jax.experimental.pallas import tpu as pltpu
from jax.sharding import Mesh
from jax.sharding import PartitionSpec as P

EPS = 1e-06
LOG2E = math.log2(math.e)
BF = jnp.bfloat16
F32 = jnp.float32
MIB = 2**20
AXES = ("ylo", "zhi", "zlo", "x", "yhi", "core")
GROUP = ("yhi", "core")
SUMS = (("ylo", "x", "yhi"), ("x", "zlo"))
RING = (("zhi", "zlo"), ("yhi", "ylo"))

VMEM = pl.BlockSpec(memory_space=pltpu.VMEM)
SMEM = pl.BlockSpec(memory_space=pltpu.SMEM)
HBM = pl.BlockSpec(memory_space=pltpu.MemorySpace.HBM)


def normalize(embed):
    inv = lax.rsqrt(jnp.sum(embed * embed, axis=1, keepdims=True) + EPS)
    return (inv, embed * inv)


def device_groups(sizes, axes_by_core, flip=False):
    ids = np.arange(math.prod(sizes)).reshape(sizes)
    groups = []
    for core, axes in enumerate(axes_by_core):
        kept = [i for i, name in enumerate(AXES[:-1]) if name not in axes]
        moved = [AXES.index(name) for name in axes]
        members = math.prod(sizes[i] for i in moved)
        part = ids[..., core].transpose(kept + moved).reshape(-1, members)
        groups += (part[:, ::-1] if flip and core == 1 else part).tolist()
    return groups


def from_ring(sizes, step):
    ids = np.arange(math.prod(sizes)).reshape(sizes)
    pairs = []
    for core, axes in enumerate(RING):
        kept = [i for i, name in enumerate(AXES[:-1]) if name not in axes]
        moved = [AXES.index(name) for name in axes]
        places = math.prod(sizes[i] for i in moved)
        target = ids[..., core].transpose(moved + kept).reshape(places, -1)
        for place in range(places):
            back = step == 2 and place % 2 == 1
            source = target[(place + (-step if back else step)) % places]
            pairs += zip(source.tolist(), target[place].tolist())
    return pairs


def heads(vision, sentence, vision_map, sentence_map, chunks=3):
    rows, depth = vision.shape
    width = vision_map.shape[1]
    own, step = rows // 2, depth // chunks

    def kernel(v, s, wv, ws, out, vb, sb, wvb, wsb, sems):
        towers = ((v, wv, vb, wvb), (s, ws, sb, wsb))
        copies = []
        for tower, (x, w, xb, wb) in enumerate(towers):
            for c in range(chunks):
                cut = pl.ds(c * step, step)
                pair = (
                    pltpu.make_async_copy(x.at[:, cut], xb.at[:, cut], sems.at[tower, c, 0]),
                    pltpu.make_async_copy(w.at[cut], wb.at[cut], sems.at[tower, c, 1]),
                )
                for copy in pair:
                    copy.start()
                copies.append(pair)
        for tower, (_, _, xb, wb) in enumerate(towers):
            total = None
            for c in range(chunks):
                for copy in copies[tower * chunks + c]:
                    copy.wait()
                cut = slice(c * step, (c + 1) * step)
                part = jnp.dot(xb[:, cut], wb[cut], preferred_element_type=F32)
                total = part if total is None else total + part
            total = total.astype(BF)
            for half in range(2):
                out[half, :, tower * width : (tower + 1) * width] = total[half * own : (half + 1) * own]

    return pl.pallas_call(
        kernel,
        out_shape=pltpu.VMEM((2, own, 2 * width), BF),
        in_specs=[HBM] * 4,
        out_specs=VMEM,
        scratch_shapes=[
            pltpu.VMEM((rows, depth), BF),
            pltpu.VMEM((rows, depth), BF),
            pltpu.VMEM((depth, width), BF),
            pltpu.VMEM((depth, width), BF),
            pltpu.SemaphoreType.DMA((2, chunks, 2)),
        ],
        compiler_params=pltpu.CompilerParams(vmem_limit_bytes=63 * MIB),
        name="heads",
    )(vision, sentence, vision_map, sentence_map)


def chip_sums(parts):
    _, _, own, width = parts.shape

    def kernel(parts_ref, given_ref, kept_ref):
        for yhi in range(2):

            @pl.when(lax.axis_index("yhi") == yhi)
            def _():
                total = [parts_ref[0, h].astype(F32) + parts_ref[1, h].astype(F32) for h in (yhi, 1 - yhi)]
                kept_ref[...] = total[0]
                given_ref[...] = total[1].astype(BF)

    return pl.pallas_call(
        kernel,
        out_shape=[pltpu.VMEM((own, width), BF), pltpu.VMEM((own, width), F32)],
        in_specs=[VMEM],
        out_specs=[VMEM, VMEM],
        compiler_params=pltpu.CompilerParams(vmem_limit_bytes=20 * MIB),
        name="chip_sums",
    )(parts)


def units(kept, got, peers):
    own, width = kept.shape[0], kept.shape[1] // 2

    def kernel(kept_ref, got_ref, wide_ref, line_ref, embed_ref):
        towers = [slice(0, width), slice(width, 2 * width)]
        for yhi in range(2):
            for core in range(2):

                @pl.when((lax.axis_index("yhi") == yhi) & (lax.axis_index("core") == core))
                def _():
                    embed = [kept_ref[:, cut] + got_ref[1 - yhi, :, cut].astype(F32) for cut in towers]
                    embed_ref[...] = embed[core]
                    mine = normalize(embed[core])[1].astype(BF)
                    for peer in range(peers):
                        wide_ref[peer] = mine
                    line_ref[...] = normalize(embed[1 - core])[1].astype(BF)

    return pl.pallas_call(
        kernel,
        out_shape=[
            pltpu.VMEM((peers, own, width), BF),
            pltpu.VMEM((own, width), BF),
            pltpu.VMEM((own, width), F32),
        ],
        in_specs=[VMEM] * 2,
        out_specs=[VMEM] * 3,
        compiler_params=pltpu.CompilerParams(vmem_limit_bytes=20 * MIB),
        name="units",
    )(kept, got)


def tile(sharpness, offset, mine, other, own, block=256):
    n, width = mine.shape
    m = other.shape[0]
    blocks = n // block

    def kernel(t_ref, b_ref, mine_ref, other_ref, out_ref):
        t = t_ref[0]
        slope, start = -LOG2E * t, -LOG2E * b_ref[0]
        zhi, last = lax.axis_index("zhi"), lax.axis_size("zhi") - 1
        first_core = lax.axis_index("core") == 0
        mine_at = jnp.where(first_core, lax.axis_index(SUMS[0]), lax.axis_index(SUMS[1])) * own
        other_at = jnp.where(first_core, zhi, last - zhi) * own
        for i in range(blocks):
            at = pl.multiple_of(lax.rem(mine_at // block + 1 + i, blocks) * block, block)
            dots = lax.dot_general(
                mine_ref[pl.ds(at, block)], other_ref[...], (((1,), (1,)), ((), ())), preferred_element_type=F32
            )
            e = jnp.exp2(dots * slope + start)
            coef = pl.reciprocal(1.0 + e, approx=True)
            if i == blocks - 1:
                row = lax.broadcasted_iota(jnp.int32, (block, 1), 0) + (at - mine_at)
                row = jnp.where((row >= 0) & (row < own), row, -m)
                col = lax.broadcasted_iota(jnp.int32, (1, m), 1) - other_at
                coef = jnp.where(row == col, -e, 1.0) * coef
            sums = jnp.dot(coef.astype(BF), other_ref[...], preferred_element_type=F32)
            out_ref[pl.ds(at, block)] = (t * sums).astype(BF)

    return pl.pallas_call(
        kernel,
        out_shape=pltpu.VMEM((n, width), BF),
        in_specs=[SMEM, SMEM, VMEM, VMEM],
        out_specs=VMEM,
        compiler_params=pltpu.CompilerParams(vmem_limit_bytes=40 * MIB),
        name="tile",
    )(sharpness, offset, mine, other)


def finish(sums, embed):
    def kernel(sums_ref, embed_ref, out_ref):
        inv, unit = normalize(embed_ref[...])
        grad = jnp.sum(sums_ref[...].astype(F32), axis=0)
        along = jnp.sum(grad * unit, axis=1, keepdims=True)
        out_ref[...] = (inv * (grad - along * unit)).astype(BF)

    return pl.pallas_call(
        kernel,
        out_shape=pltpu.VMEM(embed.shape, BF),
        in_specs=[VMEM] * 2,
        out_specs=VMEM,
        compiler_params=pltpu.CompilerParams(vmem_limit_bytes=20 * MIB),
        name="finish",
    )(sums, embed)


def heads_back(delta, vision_map, sentence_map, chunks=3):
    own, width = delta.shape[1:]
    rows, depth = 2 * own, vision_map.shape[0]
    step = depth // chunks

    def kernel(d, wv, ws, image, text, buf, sems):
        copies = []
        for tower, (w, out) in enumerate(((wv, image), (ws, text))):
            x = jnp.concatenate([d[tower], d[2 + tower]], axis=0)
            for c in range(chunks):
                cut = slice(c * step, (c + 1) * step)
                part = lax.dot_general(x, w[cut], (((1,), (1,)), ((), ())), preferred_element_type=F32)
                buf[tower, :, cut] = part.astype(BF)
                copy = pltpu.make_async_copy(buf.at[tower, :, cut], out.at[:, cut], sems.at[tower, c])
                copy.start()
                copies.append(copy)
        for copy in copies:
            copy.wait()

    return pl.pallas_call(
        kernel,
        out_shape=[jax.ShapeDtypeStruct((rows, depth), BF)] * 2,
        in_specs=[VMEM] * 3,
        out_specs=[HBM] * 2,
        scratch_shapes=[pltpu.VMEM((2, rows, depth), BF), pltpu.SemaphoreType.DMA((2, chunks))],
        compiler_params=pltpu.CompilerParams(vmem_limit_bytes=20 * MIB),
        name="heads_back",
    )(delta, vision_map, sentence_map)


def shards(vision, sentence, vision_map, sentence_map, sharpness, offset):
    width = vision_map.shape[1]
    own = vision.shape[0] // 2
    sizes = [lax.axis_size(a) for a in AXES]
    groups = device_groups(sizes, SUMS)
    peers = len(groups[0])

    def meet(x):
        return lax.all_to_all(x, AXES, 0, 0, axis_index_groups=groups)

    parts = lax.all_gather(heads(vision, sentence, vision_map, sentence_map), "core", axis=0)
    given, kept = chip_sums(parts)
    wide, line, embed = units(kept, lax.all_gather(given, "yhi", axis=0), peers)

    wide, line = lax.optimization_barrier((wide, line))
    mine = meet(wide).reshape(peers * own, width)
    far = device_groups(sizes, (("zhi",), ("zhi",)), flip=True)
    line = lax.all_gather(line, AXES, axis=0, tiled=True, axis_index_groups=far)
    near = [lax.ppermute(line, AXES, from_ring(sizes, step)) for step in (1, -1, 2)]
    grad = tile(sharpness, offset, mine, jnp.concatenate([line] + near), own)

    grad = meet(grad.reshape(peers, own, width))
    delta = lax.all_gather(finish(grad, embed), GROUP, axis=0)
    return tuple(heads_back(delta, vision_map, sentence_map))


def solution(mesh):
    x, ylo, zlo = 4, 2, 4
    zhi = mesh.shape["dp"] // (x * ylo * zlo)
    fine = Mesh(mesh.devices.reshape(ylo, zhi, zlo, x, 2, 2), AXES)
    dp, mp = ("ylo", "zhi", "zlo", "x"), ("yhi", "core")
    in_specs = (P(dp, mp), P(dp, mp), P(mp, None), P(mp, None), P(), P())
    out_specs = (P(dp, mp), P(dp, mp))
    return jax.shard_map(shards, mesh=fine, in_specs=in_specs, out_specs=out_specs, check_vma=False)
```

```python
import math

import jax
import jax.numpy as jnp
import numpy as np
from jax import lax
from jax.experimental import pallas as pl
from jax.experimental.pallas import tpu as pltpu
from jax.sharding import Mesh
from jax.sharding import PartitionSpec as P

EPS = 1e-06
LOG2E = math.log2(math.e)
BF = jnp.bfloat16
F32 = jnp.float32
MIB = 2**20
AXES = ("ylo", "zhi", "zlo", "x", "yhi", "core")
LINE = ("zhi", "zlo")
PLANE = ("ylo", "x", "yhi")
GROUP = ("yhi", "core")

VMEM = pl.BlockSpec(memory_space=pltpu.VMEM)
SMEM = pl.BlockSpec(memory_space=pltpu.SMEM)
HBM = pl.BlockSpec(memory_space=pltpu.MemorySpace.HBM)


def normalize(embed):
    inv = lax.rsqrt(jnp.sum(embed * embed, axis=1, keepdims=True) + EPS)
    return (inv, embed * inv)


def far_groups(sizes):
    ids = np.arange(math.prod(sizes)).reshape(sizes)
    groups = []
    for core in range(2):
        part = np.moveaxis(ids[..., core], 1, -1).reshape(-1, sizes[1])
        groups += (part[:, ::-1] if core == 1 else part).tolist()
    return groups


def from_line(sizes, steps):
    ids = np.arange(math.prod(sizes)).reshape(sizes)
    pairs = []
    for core, step in enumerate(steps):
        target = ids[..., core].transpose(1, 2, 0, 3, 4).reshape(sizes[1] * sizes[2], -1)
        source = np.roll(target, -step, axis=0)
        pairs += zip(source.ravel().tolist(), target.ravel().tolist())
    return pairs


def heads(vision, sentence, vision_map, sentence_map, chunks=3):
    rows, depth = vision.shape
    width = vision_map.shape[1]
    own, step = rows // 2, depth // chunks

    def kernel(v, s, wv, ws, out, vb, sb, wvb, wsb, sems):
        towers = ((v, wv, vb, wvb), (s, ws, sb, wsb))
        copies = []
        for tower, (x, w, xb, wb) in enumerate(towers):
            for c in range(chunks):
                cut = pl.ds(c * step, step)
                pair = (
                    pltpu.make_async_copy(x.at[:, cut], xb.at[:, cut], sems.at[tower, c, 0]),
                    pltpu.make_async_copy(w.at[cut], wb.at[cut], sems.at[tower, c, 1]),
                )
                for copy in pair:
                    copy.start()
                copies.append(pair)
        for tower, (_, _, xb, wb) in enumerate(towers):
            total = None
            for c in range(chunks):
                for copy in copies[tower * chunks + c]:
                    copy.wait()
                cut = slice(c * step, (c + 1) * step)
                part = jnp.dot(xb[:, cut], wb[cut], preferred_element_type=F32)
                total = part if total is None else total + part
            total = total.astype(BF)
            for half in range(2):
                out[half, :, tower * width : (tower + 1) * width] = total[half * own : (half + 1) * own]

    return pl.pallas_call(
        kernel,
        out_shape=pltpu.VMEM((2, own, 2 * width), BF),
        in_specs=[HBM] * 4,
        out_specs=VMEM,
        scratch_shapes=[
            pltpu.VMEM((rows, depth), BF),
            pltpu.VMEM((rows, depth), BF),
            pltpu.VMEM((depth, width), BF),
            pltpu.VMEM((depth, width), BF),
            pltpu.SemaphoreType.DMA((2, chunks, 2)),
        ],
        compiler_params=pltpu.CompilerParams(vmem_limit_bytes=63 * MIB),
        name="heads",
    )(vision, sentence, vision_map, sentence_map)


def chip_sums(parts):
    _, _, own, width = parts.shape

    def kernel(parts_ref, given_ref, kept_ref):
        for yhi in range(2):

            @pl.when(lax.axis_index("yhi") == yhi)
            def _():
                total = [parts_ref[0, h].astype(F32) + parts_ref[1, h].astype(F32) for h in (yhi, 1 - yhi)]
                kept_ref[...] = total[0]
                given_ref[...] = total[1].astype(BF)

    return pl.pallas_call(
        kernel,
        out_shape=[pltpu.VMEM((own, width), BF), pltpu.VMEM((own, width), F32)],
        in_specs=[VMEM],
        out_specs=[VMEM, VMEM],
        compiler_params=pltpu.CompilerParams(vmem_limit_bytes=20 * MIB),
        name="chip_sums",
    )(parts)


def units(kept, got, peers):
    own, width = kept.shape[0], kept.shape[1] // 2

    def kernel(kept_ref, got_ref, wide_ref, line_ref, embed_ref):
        towers = [slice(0, width), slice(width, 2 * width)]
        for yhi in range(2):
            for core in range(2):

                @pl.when((lax.axis_index("yhi") == yhi) & (lax.axis_index("core") == core))
                def _():
                    embed = [kept_ref[:, cut] + got_ref[1 - yhi, :, cut].astype(F32) for cut in towers]
                    embed_ref[...] = embed[core]
                    mine = normalize(embed[core])[1].astype(BF)
                    for peer in range(peers):
                        wide_ref[peer] = mine
                    line_ref[...] = normalize(embed[1 - core])[1].astype(BF)

    return pl.pallas_call(
        kernel,
        out_shape=[
            pltpu.VMEM((peers, own, width), BF),
            pltpu.VMEM((own, width), BF),
            pltpu.VMEM((own, width), F32),
        ],
        in_specs=[VMEM] * 2,
        out_specs=[VMEM] * 3,
        compiler_params=pltpu.CompilerParams(vmem_limit_bytes=20 * MIB),
        name="units",
    )(kept, got)


def tile(sharpness, offset, mine, other, total, own, final=False, block=256):
    n, width = mine.shape
    m = other.shape[0]
    blocks = n // block

    def kernel(t_ref, b_ref, mine_ref, other_ref, *rest):
        out_ref = rest[-1]
        t = t_ref[0]
        slope, start = -LOG2E * t, -LOG2E * b_ref[0]
        zhi, last = lax.axis_index("zhi"), lax.axis_size("zhi") - 1
        mine_at = lax.axis_index(PLANE) * own
        other_at = jnp.where(lax.axis_index("core") == 0, zhi, last - zhi) * own
        for i in range(blocks):
            at = pl.multiple_of(lax.rem(mine_at // block + 1 + i, blocks) * block, block)
            dots = lax.dot_general(
                mine_ref[pl.ds(at, block)], other_ref[...], (((1,), (1,)), ((), ())), preferred_element_type=F32
            )
            e = jnp.exp2(dots * slope + start)
            coef = pl.reciprocal(1.0 + e, approx=True)
            if total is None and i == blocks - 1:
                row = lax.broadcasted_iota(jnp.int32, (block, 1), 0) + (at - mine_at)
                row = jnp.where((row >= 0) & (row < own), row, -m)
                col = lax.broadcasted_iota(jnp.int32, (1, m), 1) - other_at
                coef = jnp.where(row == col, -e, 1.0) * coef
            sums = jnp.dot(coef.astype(BF), other_ref[...], preferred_element_type=F32)
            if total is not None:
                sums = sums + rest[0][pl.ds(at, block)]
            out_ref[pl.ds(at, block)] = (t * sums).astype(BF) if final else sums

    totals = [] if total is None else [total]
    return pl.pallas_call(
        kernel,
        out_shape=pltpu.VMEM((n, width), BF if final else F32),
        in_specs=[SMEM, SMEM, VMEM, VMEM] + [VMEM] * len(totals),
        out_specs=VMEM,
        compiler_params=pltpu.CompilerParams(vmem_limit_bytes=30 * MIB),
        cost_estimate=pl.CostEstimate(
            flops=4 * n * m * width, bytes_accessed=2 * width * (n + m), transcendentals=2 * n * m
        ),
        name="tile",
    )(sharpness, offset, mine, other, *totals)


def finish(sums, embed):
    def kernel(sums_ref, embed_ref, out_ref):
        inv, unit = normalize(embed_ref[...])
        grad = jnp.sum(sums_ref[...].astype(F32), axis=0)
        along = jnp.sum(grad * unit, axis=1, keepdims=True)
        out_ref[...] = (inv * (grad - along * unit)).astype(BF)

    return pl.pallas_call(
        kernel,
        out_shape=pltpu.VMEM(embed.shape, BF),
        in_specs=[VMEM] * 2,
        out_specs=VMEM,
        compiler_params=pltpu.CompilerParams(vmem_limit_bytes=20 * MIB),
        name="finish",
    )(sums, embed)


def heads_back(delta, vision_map, sentence_map, chunks=3):
    own, width = delta.shape[1:]
    rows, depth = 2 * own, vision_map.shape[0]
    step = depth // chunks

    def kernel(d, wv, ws, image, text, buf, sems):
        copies = []
        for tower, (w, out) in enumerate(((wv, image), (ws, text))):
            x = jnp.concatenate([d[tower], d[2 + tower]], axis=0)
            for c in range(chunks):
                cut = slice(c * step, (c + 1) * step)
                part = lax.dot_general(x, w[cut], (((1,), (1,)), ((), ())), preferred_element_type=F32)
                buf[tower, :, cut] = part.astype(BF)
                copy = pltpu.make_async_copy(buf.at[tower, :, cut], out.at[:, cut], sems.at[tower, c])
                copy.start()
                copies.append(copy)
        for copy in copies:
            copy.wait()

    return pl.pallas_call(
        kernel,
        out_shape=[jax.ShapeDtypeStruct((rows, depth), BF)] * 2,
        in_specs=[VMEM] * 3,
        out_specs=[HBM] * 2,
        scratch_shapes=[pltpu.VMEM((2, rows, depth), BF), pltpu.SemaphoreType.DMA((2, chunks))],
        compiler_params=pltpu.CompilerParams(vmem_limit_bytes=20 * MIB),
        name="heads_back",
    )(delta, vision_map, sentence_map)


def shards(vision, sentence, vision_map, sentence_map, sharpness, offset):
    width = vision_map.shape[1]
    own = vision.shape[0] // 2
    sizes = [lax.axis_size(a) for a in AXES]
    peers = lax.axis_size(PLANE)

    parts = lax.all_gather(heads(vision, sentence, vision_map, sentence_map), "core", axis=0)
    given, kept = chip_sums(parts)
    wide, line, embed = units(kept, lax.all_gather(given, "yhi", axis=0), peers)

    wide, line = lax.optimization_barrier((wide, line))
    mine = lax.all_to_all(wide, PLANE, 0, 0).reshape(peers * own, width)
    line = lax.all_gather(line, AXES, axis=0, tiled=True, axis_index_groups=far_groups(sizes))
    near = [lax.ppermute(line, AXES, from_line(sizes, steps)) for steps in ((1, 1), (-1, -1), (2, -2))]
    grad = tile(sharpness, offset, mine, line, None, own)
    for other in near:
        grad = tile(sharpness, offset, mine, other, grad, own, final=other is near[-1])

    grad = lax.all_to_all(grad.reshape(peers, own, width), PLANE, 0, 0)
    delta = lax.all_gather(finish(grad, embed), GROUP, axis=0)
    return tuple(heads_back(delta, vision_map, sentence_map))


def solution(mesh):
    x, ylo, zlo = 4, 2, 4
    zhi = mesh.shape["dp"] // (x * ylo * zlo)
    fine = Mesh(mesh.devices.reshape(ylo, zhi, zlo, x, 2, 2), AXES)
    dp, mp = ("ylo", "zhi", "zlo", "x"), ("yhi", "core")
    in_specs = (P(dp, mp), P(dp, mp), P(mp, None), P(mp, None), P(), P())
    out_specs = (P(dp, mp), P(dp, mp))
    return jax.shard_map(shards, mesh=fine, in_specs=in_specs, out_specs=out_specs, check_vma=False)
```

```python
import math

import jax
import jax.numpy as jnp
import numpy as np
from jax import lax
from jax.experimental import pallas as pl
from jax.experimental.pallas import tpu as pltpu
from jax.sharding import Mesh
from jax.sharding import PartitionSpec as P

EPS = 1e-06
LOG2E = math.log2(math.e)
BF = jnp.bfloat16
F32 = jnp.float32
MIB = 2**20
AXES = ("ylo", "zhi", "zlo", "x", "yhi", "core")
LINE = ("zhi", "zlo")
PLANE = ("ylo", "x", "yhi")
GROUP = ("yhi", "core")

VMEM = pl.BlockSpec(memory_space=pltpu.VMEM)
SMEM = pl.BlockSpec(memory_space=pltpu.SMEM)
HBM = pl.BlockSpec(memory_space=pltpu.MemorySpace.HBM)


def normalize(embed):
    inv = lax.rsqrt(jnp.sum(embed * embed, axis=1, keepdims=True) + EPS)
    return (inv, embed * inv)


def far_groups(sizes):
    ids = np.arange(math.prod(sizes)).reshape(sizes)
    groups = []
    for core in range(2):
        part = np.moveaxis(ids[..., core], 1, -1).reshape(-1, sizes[1])
        groups += (part[:, ::-1] if core == 1 else part).tolist()
    return groups


def from_line(sizes, steps):
    ids = np.arange(math.prod(sizes)).reshape(sizes)
    pairs = []
    for core, step in enumerate(steps):
        target, other = (
            ids[..., c].transpose(1, 2, 0, 3, 4).reshape(sizes[1] * sizes[2], -1) for c in (core, 1 - core)
        )
        pairs += zip(np.roll(other, -step, axis=0).ravel().tolist(), target.ravel().tolist())
    return pairs


def heads(vision, sentence, vision_map, sentence_map, chunks=3):
    rows, depth = vision.shape
    width = vision_map.shape[1]
    step = depth // chunks

    def kernel(v, s, wv, ws, given, kept, vb, sb, wvb, wsb, sems):
        towers = ((v, wv, vb, wvb), (s, ws, sb, wsb))
        copies = []
        for tower, (x, w, xb, wb) in enumerate(towers):
            for c in range(chunks):
                cut = pl.ds(c * step, step)
                pair = (
                    pltpu.make_async_copy(x.at[:, cut], xb.at[:, cut], sems.at[tower, c, 0]),
                    pltpu.make_async_copy(w.at[cut], wb.at[cut], sems.at[tower, c, 1]),
                )
                for copy in pair:
                    copy.start()
                copies.append(pair)
        for tower, (_, _, xb, wb) in enumerate(towers):
            total = None
            for c in range(chunks):
                for copy in copies[tower * chunks + c]:
                    copy.wait()
                cut = slice(c * step, (c + 1) * step)
                part = jnp.dot(xb[:, cut], wb[cut], preferred_element_type=F32)
                total = part if total is None else total + part

            @pl.when(lax.axis_index("core") == tower)
            def _():
                kept[...] = total

            @pl.when(lax.axis_index("core") != tower)
            def _():
                given[...] = total.astype(BF)

    return pl.pallas_call(
        kernel,
        out_shape=[pltpu.VMEM((rows, width), BF), pltpu.VMEM((rows, width), F32)],
        in_specs=[HBM] * 4,
        out_specs=[VMEM] * 2,
        scratch_shapes=[
            pltpu.VMEM((rows, depth), BF),
            pltpu.VMEM((rows, depth), BF),
            pltpu.VMEM((depth, width), BF),
            pltpu.VMEM((depth, width), BF),
            pltpu.SemaphoreType.DMA((2, chunks, 2)),
        ],
        compiler_params=pltpu.CompilerParams(vmem_limit_bytes=63 * MIB),
        name="heads",
    )(vision, sentence, vision_map, sentence_map)


def chip_sums(kept, got):
    own, width = kept.shape[0] // 2, kept.shape[1]

    def kernel(kept_ref, got_ref, given_ref, sums_ref):
        for core in range(2):
            for yhi in range(2):

                @pl.when((lax.axis_index("core") == core) & (lax.axis_index("yhi") == yhi))
                def _():
                    total = kept_ref[...] + got_ref[1 - core].astype(F32)
                    sums_ref[...] = total[yhi * own : (yhi + 1) * own]
                    given_ref[...] = total[(1 - yhi) * own : (2 - yhi) * own].astype(BF)

    return pl.pallas_call(
        kernel,
        out_shape=[pltpu.VMEM((own, width), BF), pltpu.VMEM((own, width), F32)],
        in_specs=[VMEM] * 2,
        out_specs=[VMEM] * 2,
        compiler_params=pltpu.CompilerParams(vmem_limit_bytes=20 * MIB),
        name="chip_sums",
    )(kept, got)


def units(sums, got, peers):
    own, width = sums.shape

    def kernel(sums_ref, got_ref, wide_ref, unit_ref, embed_ref):
        for yhi in range(2):

            @pl.when(lax.axis_index("yhi") == yhi)
            def _():
                embed = sums_ref[...] + got_ref[1 - yhi].astype(F32)
                embed_ref[...] = embed
                unit = normalize(embed)[1].astype(BF)
                unit_ref[...] = unit
                for peer in range(peers):
                    wide_ref[peer] = unit

    return pl.pallas_call(
        kernel,
        out_shape=[
            pltpu.VMEM((peers, own, width), BF),
            pltpu.VMEM((own, width), BF),
            pltpu.VMEM((own, width), F32),
        ],
        in_specs=[VMEM] * 2,
        out_specs=[VMEM] * 3,
        compiler_params=pltpu.CompilerParams(vmem_limit_bytes=20 * MIB),
        name="units",
    )(sums, got)


def tile(sharpness, offset, mine, others, total, own, positives=False, final=False, block=256):
    n, width = mine.shape
    m = others[0].shape[0]
    blocks = n // block

    def kernel(t_ref, b_ref, mine_ref, *rest):
        out_ref = rest[-1]
        t = t_ref[0]
        slope, start = -LOG2E * t, -LOG2E * b_ref[0]
        zhi, last = lax.axis_index("zhi"), lax.axis_size("zhi") - 1
        mine_at = lax.axis_index(PLANE) * own
        other_at = jnp.where(lax.axis_index("core") == 0, last - zhi, zhi) * own
        for i in range(blocks):
            at = pl.multiple_of(lax.rem(mine_at // block + 1 + i, blocks) * block, block)
            sums = None if total is None else rest[len(others)][pl.ds(at, block)]
            for other_ref in rest[: len(others)]:
                dots = lax.dot_general(
                    mine_ref[pl.ds(at, block)], other_ref[...], (((1,), (1,)), ((), ())), preferred_element_type=F32
                )
                e = jnp.exp2(dots * slope + start)
                coef = pl.reciprocal(1.0 + e, approx=True)
                if positives and i == blocks - 1:
                    row = lax.broadcasted_iota(jnp.int32, (block, 1), 0) + (at - mine_at)
                    row = jnp.where((row >= 0) & (row < own), row, -m)
                    col = lax.broadcasted_iota(jnp.int32, (1, m), 1) - other_at
                    coef = jnp.where(row == col, -e, 1.0) * coef
                part = jnp.dot(coef.astype(BF), other_ref[...], preferred_element_type=F32)
                sums = part if sums is None else sums + part
            out_ref[pl.ds(at, block)] = (t * sums).astype(BF) if final else sums

    totals = [] if total is None else [total]
    return pl.pallas_call(
        kernel,
        out_shape=pltpu.VMEM((n, width), BF if final else F32),
        in_specs=[SMEM, SMEM, VMEM] + [VMEM] * (len(others) + len(totals)),
        out_specs=VMEM,
        compiler_params=pltpu.CompilerParams(vmem_limit_bytes=30 * MIB),
        cost_estimate=pl.CostEstimate(
            flops=4 * n * m * width * len(others),
            bytes_accessed=2 * width * (n + m * len(others)),
            transcendentals=2 * n * m * len(others),
        ),
        name="tile",
    )(sharpness, offset, mine, *others, *totals)


def finish(sums, embed):
    def kernel(sums_ref, embed_ref, out_ref):
        inv, unit = normalize(embed_ref[...])
        grad = jnp.sum(sums_ref[...].astype(F32), axis=0)
        along = jnp.sum(grad * unit, axis=1, keepdims=True)
        out_ref[...] = (inv * (grad - along * unit)).astype(BF)

    return pl.pallas_call(
        kernel,
        out_shape=pltpu.VMEM(embed.shape, BF),
        in_specs=[VMEM] * 2,
        out_specs=VMEM,
        compiler_params=pltpu.CompilerParams(vmem_limit_bytes=20 * MIB),
        name="finish",
    )(sums, embed)


def heads_back(delta, vision_map, sentence_map, chunks=3):
    own, width = delta.shape[1:]
    rows, depth = 2 * own, vision_map.shape[0]
    step = depth // chunks

    def kernel(d, wv, ws, image, text, buf, sems):
        copies = []
        for tower, (w, out) in enumerate(((wv, image), (ws, text))):
            x = jnp.concatenate([d[tower], d[2 + tower]], axis=0)
            for c in range(chunks):
                cut = slice(c * step, (c + 1) * step)
                part = lax.dot_general(x, w[cut], (((1,), (1,)), ((), ())), preferred_element_type=F32)
                buf[tower, :, cut] = part.astype(BF)
                copy = pltpu.make_async_copy(buf.at[tower, :, cut], out.at[:, cut], sems.at[tower, c])
                copy.start()
                copies.append(copy)
        for copy in copies:
            copy.wait()

    return pl.pallas_call(
        kernel,
        out_shape=[jax.ShapeDtypeStruct((rows, depth), BF)] * 2,
        in_specs=[VMEM] * 3,
        out_specs=[HBM] * 2,
        scratch_shapes=[pltpu.VMEM((2, rows, depth), BF), pltpu.SemaphoreType.DMA((2, chunks))],
        compiler_params=pltpu.CompilerParams(vmem_limit_bytes=20 * MIB),
        name="heads_back",
    )(delta, vision_map, sentence_map)


def shards(vision, sentence, vision_map, sentence_map, sharpness, offset):
    width = vision_map.shape[1]
    own = vision.shape[0] // 2
    sizes = [lax.axis_size(a) for a in AXES]
    peers = lax.axis_size(PLANE)

    given, kept = heads(vision, sentence, vision_map, sentence_map)
    given, sums = chip_sums(kept, lax.all_gather(given, "core", axis=0))
    wide, unit, embed = units(sums, lax.all_gather(given, "yhi", axis=0), peers)

    wide, unit = lax.optimization_barrier((wide, unit))
    mine = lax.all_to_all(wide, PLANE, 0, 0).reshape(peers * own, width)
    line = lax.all_gather(unit, AXES, axis=0, tiled=True, axis_index_groups=far_groups(sizes))
    first, second, third, here = (
        lax.ppermute(line, AXES, from_line(sizes, steps)) for steps in ((1, 1), (-1, -1), (2, -2), (0, 0))
    )
    grad = tile(sharpness, offset, mine, [first], None, own)
    grad = tile(sharpness, offset, mine, [here], grad, own, positives=True)
    grad = tile(sharpness, offset, mine, [second, third], grad, own, final=True)

    grad = lax.all_to_all(grad.reshape(peers, own, width), PLANE, 0, 0)
    delta = lax.all_gather(finish(grad, embed), GROUP, axis=0)
    return tuple(heads_back(delta, vision_map, sentence_map))


def solution(mesh):
    x, ylo, zlo = 4, 2, 4
    zhi = mesh.shape["dp"] // (x * ylo * zlo)
    fine = Mesh(mesh.devices.reshape(ylo, zhi, zlo, x, 2, 2), AXES)
    dp, mp = ("ylo", "zhi", "zlo", "x"), ("yhi", "core")
    in_specs = (P(dp, mp), P(dp, mp), P(mp, None), P(mp, None), P(), P())
    out_specs = (P(dp, mp), P(dp, mp))
    return jax.shard_map(shards, mesh=fine, in_specs=in_specs, out_specs=out_specs, check_vma=False)
```

```python
import math

import jax
import jax.numpy as jnp
import numpy as np
from jax import lax
from jax.experimental import pallas as pl
from jax.experimental.pallas import tpu as pltpu
from jax.sharding import Mesh
from jax.sharding import PartitionSpec as P

EPS = 1e-06
LOG2E = math.log2(math.e)
BF = jnp.bfloat16
F32 = jnp.float32
MIB = 2**20
AXES = ("ylo", "zhi", "zlo", "x", "yhi", "core")
LINE = ("zhi", "zlo")
PLANE = ("ylo", "x", "yhi")
GROUP = ("yhi", "core")

VMEM = pl.BlockSpec(memory_space=pltpu.VMEM)
SMEM = pl.BlockSpec(memory_space=pltpu.SMEM)
HBM = pl.BlockSpec(memory_space=pltpu.MemorySpace.HBM)


def normalize(embed):
    inv = lax.rsqrt(jnp.sum(embed * embed, axis=1, keepdims=True) + EPS)
    return (inv, embed * inv)


def far_groups(sizes):
    ids = np.arange(math.prod(sizes)).reshape(sizes)
    groups = []
    for core in range(2):
        part = np.moveaxis(ids[..., core], 1, -1).reshape(-1, sizes[1])
        groups += (part[:, ::-1] if core == 1 else part).tolist()
    return groups


def from_line(sizes, steps):
    ids = np.arange(math.prod(sizes)).reshape(sizes)
    pairs = []
    for core, step in enumerate(steps):
        target = ids[..., core].transpose(1, 2, 0, 3, 4).reshape(sizes[1] * sizes[2], -1)
        source = np.roll(target, -step, axis=0)
        pairs += zip(source.ravel().tolist(), target.ravel().tolist())
    return pairs


def heads(vision, sentence, vision_map, sentence_map, chunks=3):
    rows, depth = vision.shape
    width = vision_map.shape[1]
    own, step = rows // 2, depth // chunks

    def kernel(v, s, wv, ws, out, vb, sb, wvb, wsb, sems):
        towers = ((v, wv, vb, wvb), (s, ws, sb, wsb))
        copies = []
        for tower, (x, w, xb, wb) in enumerate(towers):
            for c in range(chunks):
                cut = pl.ds(c * step, step)
                pair = (
                    pltpu.make_async_copy(x.at[:, cut], xb.at[:, cut], sems.at[tower, c, 0]),
                    pltpu.make_async_copy(w.at[cut], wb.at[cut], sems.at[tower, c, 1]),
                )
                for copy in pair:
                    copy.start()
                copies.append(pair)
        for tower, (_, _, xb, wb) in enumerate(towers):
            total = None
            for c in range(chunks):
                for copy in copies[tower * chunks + c]:
                    copy.wait()
                cut = slice(c * step, (c + 1) * step)
                part = jnp.dot(xb[:, cut], wb[cut], preferred_element_type=F32)
                total = part if total is None else total + part
            total = total.astype(BF)
            for half in range(2):
                out[half, :, tower * width : (tower + 1) * width] = total[half * own : (half + 1) * own]

    return pl.pallas_call(
        kernel,
        out_shape=pltpu.VMEM((2, own, 2 * width), BF),
        in_specs=[HBM] * 4,
        out_specs=VMEM,
        scratch_shapes=[
            pltpu.VMEM((rows, depth), BF),
            pltpu.VMEM((rows, depth), BF),
            pltpu.VMEM((depth, width), BF),
            pltpu.VMEM((depth, width), BF),
            pltpu.SemaphoreType.DMA((2, chunks, 2)),
        ],
        compiler_params=pltpu.CompilerParams(vmem_limit_bytes=63 * MIB),
        name="heads",
    )(vision, sentence, vision_map, sentence_map)


def chip_sums(parts):
    _, _, own, width = parts.shape

    def kernel(parts_ref, given_ref, kept_ref):
        for yhi in range(2):

            @pl.when(lax.axis_index("yhi") == yhi)
            def _():
                total = [parts_ref[0, h].astype(F32) + parts_ref[1, h].astype(F32) for h in (yhi, 1 - yhi)]
                kept_ref[...] = total[0]
                given_ref[...] = total[1].astype(BF)

    return pl.pallas_call(
        kernel,
        out_shape=[pltpu.VMEM((own, width), BF), pltpu.VMEM((own, width), F32)],
        in_specs=[VMEM],
        out_specs=[VMEM, VMEM],
        compiler_params=pltpu.CompilerParams(vmem_limit_bytes=20 * MIB),
        name="chip_sums",
    )(parts)


def units(kept, got, peers):
    own, width = kept.shape[0], kept.shape[1] // 2

    def kernel(kept_ref, got_ref, wide_ref, line_ref, embed_ref):
        towers = [slice(0, width), slice(width, 2 * width)]
        for yhi in range(2):
            for core in range(2):

                @pl.when((lax.axis_index("yhi") == yhi) & (lax.axis_index("core") == core))
                def _():
                    embed = [kept_ref[:, cut] + got_ref[1 - yhi, :, cut].astype(F32) for cut in towers]
                    embed_ref[...] = embed[core]
                    mine = normalize(embed[core])[1].astype(BF)
                    for peer in range(peers):
                        wide_ref[peer] = mine
                    line_ref[...] = normalize(embed[1 - core])[1].astype(BF)

    return pl.pallas_call(
        kernel,
        out_shape=[
            pltpu.VMEM((peers, own, width), BF),
            pltpu.VMEM((own, width), BF),
            pltpu.VMEM((own, width), F32),
        ],
        in_specs=[VMEM] * 2,
        out_specs=[VMEM] * 3,
        compiler_params=pltpu.CompilerParams(vmem_limit_bytes=20 * MIB),
        name="units",
    )(kept, got)


def tile(sharpness, offset, mine, others, total, own, positives=False, final=False, block=256):
    n, width = mine.shape
    m = others[0].shape[0]
    blocks = n // block

    def kernel(t_ref, b_ref, mine_ref, *rest):
        out_ref = rest[-1]
        t = t_ref[0]
        slope, start = -LOG2E * t, -LOG2E * b_ref[0]
        zhi, last = lax.axis_index("zhi"), lax.axis_size("zhi") - 1
        mine_at = lax.axis_index(PLANE) * own
        other_at = jnp.where(lax.axis_index("core") == 0, zhi, last - zhi) * own
        for i in range(blocks):
            at = pl.multiple_of(lax.rem(mine_at // block + 1 + i, blocks) * block, block)
            sums = None if total is None else rest[len(others)][pl.ds(at, block)]
            for other_ref in rest[: len(others)]:
                dots = lax.dot_general(
                    mine_ref[pl.ds(at, block)], other_ref[...], (((1,), (1,)), ((), ())), preferred_element_type=F32
                )
                e = jnp.exp2(dots * slope + start)
                coef = pl.reciprocal(1.0 + e, approx=True)
                if positives and i == blocks - 1:
                    row = lax.broadcasted_iota(jnp.int32, (block, 1), 0) + (at - mine_at)
                    row = jnp.where((row >= 0) & (row < own), row, -m)
                    col = lax.broadcasted_iota(jnp.int32, (1, m), 1) - other_at
                    coef = jnp.where(row == col, -e, 1.0) * coef
                part = jnp.dot(coef.astype(BF), other_ref[...], preferred_element_type=F32)
                sums = part if sums is None else sums + part
            out_ref[pl.ds(at, block)] = (t * sums).astype(BF) if final else sums

    totals = [] if total is None else [total]
    return pl.pallas_call(
        kernel,
        out_shape=pltpu.VMEM((n, width), BF if final else F32),
        in_specs=[SMEM, SMEM, VMEM] + [VMEM] * (len(others) + len(totals)),
        out_specs=VMEM,
        compiler_params=pltpu.CompilerParams(vmem_limit_bytes=30 * MIB),
        cost_estimate=pl.CostEstimate(
            flops=4 * n * m * width * len(others),
            bytes_accessed=2 * width * (n + m * len(others)),
            transcendentals=2 * n * m * len(others),
        ),
        name="tile",
    )(sharpness, offset, mine, *others, *totals)


def finish(sums, embed):
    def kernel(sums_ref, embed_ref, out_ref):
        inv, unit = normalize(embed_ref[...])
        grad = jnp.sum(sums_ref[...].astype(F32), axis=0)
        along = jnp.sum(grad * unit, axis=1, keepdims=True)
        out_ref[...] = (inv * (grad - along * unit)).astype(BF)

    return pl.pallas_call(
        kernel,
        out_shape=pltpu.VMEM(embed.shape, BF),
        in_specs=[VMEM] * 2,
        out_specs=VMEM,
        compiler_params=pltpu.CompilerParams(vmem_limit_bytes=20 * MIB),
        name="finish",
    )(sums, embed)


def heads_back(delta, vision_map, sentence_map, chunks=3):
    own, width = delta.shape[1:]
    rows, depth = 2 * own, vision_map.shape[0]
    step = depth // chunks

    def kernel(d, wv, ws, image, text, buf, sems):
        copies = []
        for tower, (w, out) in enumerate(((wv, image), (ws, text))):
            x = jnp.concatenate([d[tower], d[2 + tower]], axis=0)
            for c in range(chunks):
                cut = slice(c * step, (c + 1) * step)
                part = lax.dot_general(x, w[cut], (((1,), (1,)), ((), ())), preferred_element_type=F32)
                buf[tower, :, cut] = part.astype(BF)
                copy = pltpu.make_async_copy(buf.at[tower, :, cut], out.at[:, cut], sems.at[tower, c])
                copy.start()
                copies.append(copy)
        for copy in copies:
            copy.wait()

    return pl.pallas_call(
        kernel,
        out_shape=[jax.ShapeDtypeStruct((rows, depth), BF)] * 2,
        in_specs=[VMEM] * 3,
        out_specs=[HBM] * 2,
        scratch_shapes=[pltpu.VMEM((2, rows, depth), BF), pltpu.SemaphoreType.DMA((2, chunks))],
        compiler_params=pltpu.CompilerParams(vmem_limit_bytes=20 * MIB),
        name="heads_back",
    )(delta, vision_map, sentence_map)


def shards(vision, sentence, vision_map, sentence_map, sharpness, offset):
    width = vision_map.shape[1]
    own = vision.shape[0] // 2
    sizes = [lax.axis_size(a) for a in AXES]
    peers = lax.axis_size(PLANE)

    parts = lax.all_gather(heads(vision, sentence, vision_map, sentence_map), "core", axis=0)
    given, kept = chip_sums(parts)
    wide, line, embed = units(kept, lax.all_gather(given, "yhi", axis=0), peers)

    wide, line = lax.optimization_barrier((wide, line))
    mine = lax.all_to_all(wide, PLANE, 0, 0).reshape(peers * own, width)
    line = lax.all_gather(line, AXES, axis=0, tiled=True, axis_index_groups=far_groups(sizes))
    first, second, third = (
        lax.ppermute(line, AXES, from_line(sizes, steps)) for steps in ((1, 1), (-1, -1), (2, -2))
    )
    grad = tile(sharpness, offset, mine, [line], None, own, positives=True)
    grad = tile(sharpness, offset, mine, [first], grad, own)
    grad = tile(sharpness, offset, mine, [second, third], grad, own, final=True)

    grad = lax.all_to_all(grad.reshape(peers, own, width), PLANE, 0, 0)
    delta = lax.all_gather(finish(grad, embed), GROUP, axis=0)
    return tuple(heads_back(delta, vision_map, sentence_map))


def solution(mesh):
    x, ylo, zlo = 4, 2, 4
    zhi = mesh.shape["dp"] // (x * ylo * zlo)
    fine = Mesh(mesh.devices.reshape(ylo, zhi, zlo, x, 2, 2), AXES)
    dp, mp = ("ylo", "zhi", "zlo", "x"), ("yhi", "core")
    in_specs = (P(dp, mp), P(dp, mp), P(mp, None), P(mp, None), P(), P())
    out_specs = (P(dp, mp), P(dp, mp))
    return jax.shard_map(shards, mesh=fine, in_specs=in_specs, out_specs=out_specs, check_vma=False)
```

```python
import math

import jax
import jax.numpy as jnp
import numpy as np
from jax import lax
from jax.experimental import pallas as pl
from jax.experimental.pallas import tpu as pltpu
from jax.sharding import Mesh
from jax.sharding import PartitionSpec as P

EPS = 1e-06
LOG2E = math.log2(math.e)
BF = jnp.bfloat16
F32 = jnp.float32
MIB = 2**20
AXES = ("ylo", "zhi", "zlo", "x", "yhi", "core")
LINE = ("zhi", "zlo")
PLANE = ("ylo", "x", "yhi")
GROUP = ("yhi", "core")

VMEM = pl.BlockSpec(memory_space=pltpu.VMEM)
SMEM = pl.BlockSpec(memory_space=pltpu.SMEM)
HBM = pl.BlockSpec(memory_space=pltpu.MemorySpace.HBM)


def normalize(embed):
    inv = lax.rsqrt(jnp.sum(embed * embed, axis=1, keepdims=True) + EPS)
    return (inv, embed * inv)


def far_groups(sizes):
    ids = np.arange(math.prod(sizes)).reshape(sizes)
    groups = []
    for core in range(2):
        part = np.moveaxis(ids[..., core], 1, -1).reshape(-1, sizes[1])
        groups += (part[:, ::-1] if core == 1 else part).tolist()
    return groups


def from_line(sizes, steps):
    ids = np.arange(math.prod(sizes)).reshape(sizes)
    pairs = []
    for core, step in enumerate(steps):
        target = ids[..., core].transpose(1, 2, 0, 3, 4).reshape(sizes[1] * sizes[2], -1)
        source = np.roll(target, -step, axis=0)
        pairs += zip(source.ravel().tolist(), target.ravel().tolist())
    return pairs


def heads(vision, sentence, vision_map, sentence_map, chunks=3):
    rows, depth = vision.shape
    width = vision_map.shape[1]
    own, step = rows // 2, depth // chunks

    def kernel(v, s, wv, ws, out, vb, sb, wvb, wsb, sems):
        towers = ((v, wv, vb, wvb), (s, ws, sb, wsb))
        copies = []
        for tower, (x, w, xb, wb) in enumerate(towers):
            for c in range(chunks):
                cut = pl.ds(c * step, step)
                pair = (
                    pltpu.make_async_copy(x.at[:, cut], xb.at[:, cut], sems.at[tower, c, 0]),
                    pltpu.make_async_copy(w.at[cut], wb.at[cut], sems.at[tower, c, 1]),
                )
                for copy in pair:
                    copy.start()
                copies.append(pair)
        for tower, (_, _, xb, wb) in enumerate(towers):
            total = None
            for c in range(chunks):
                for copy in copies[tower * chunks + c]:
                    copy.wait()
                cut = slice(c * step, (c + 1) * step)
                part = jnp.dot(xb[:, cut], wb[cut], preferred_element_type=F32)
                total = part if total is None else total + part
            total = total.astype(BF)
            for half in range(2):
                out[half, :, tower * width : (tower + 1) * width] = total[half * own : (half + 1) * own]

    return pl.pallas_call(
        kernel,
        out_shape=pltpu.VMEM((2, own, 2 * width), BF),
        in_specs=[HBM] * 4,
        out_specs=VMEM,
        scratch_shapes=[
            pltpu.VMEM((rows, depth), BF),
            pltpu.VMEM((rows, depth), BF),
            pltpu.VMEM((depth, width), BF),
            pltpu.VMEM((depth, width), BF),
            pltpu.SemaphoreType.DMA((2, chunks, 2)),
        ],
        compiler_params=pltpu.CompilerParams(vmem_limit_bytes=63 * MIB),
        name="heads",
    )(vision, sentence, vision_map, sentence_map)


def chip_sums(parts):
    _, _, own, width = parts.shape

    def kernel(parts_ref, given_ref, kept_ref):
        for yhi in range(2):

            @pl.when(lax.axis_index("yhi") == yhi)
            def _():
                total = [parts_ref[0, h].astype(F32) + parts_ref[1, h].astype(F32) for h in (yhi, 1 - yhi)]
                kept_ref[...] = total[0]
                given_ref[...] = total[1].astype(BF)

    return pl.pallas_call(
        kernel,
        out_shape=[pltpu.VMEM((own, width), BF), pltpu.VMEM((own, width), F32)],
        in_specs=[VMEM],
        out_specs=[VMEM, VMEM],
        compiler_params=pltpu.CompilerParams(vmem_limit_bytes=20 * MIB),
        name="chip_sums",
    )(parts)


def units(kept, got, peers):
    own, width = kept.shape[0], kept.shape[1] // 2

    def kernel(kept_ref, got_ref, wide_ref, line_ref, embed_ref, mine, sems):
        towers = [slice(0, width), slice(width, 2 * width)]
        for yhi in range(2):
            for core in range(2):

                @pl.when((lax.axis_index("yhi") == yhi) & (lax.axis_index("core") == core))
                def _():
                    embed = [kept_ref[:, cut] + got_ref[1 - yhi, :, cut].astype(F32) for cut in towers]
                    embed_ref[...] = embed[core]
                    mine[...] = normalize(embed[core])[1].astype(BF)
                    line_ref[...] = normalize(embed[1 - core])[1].astype(BF)

        copies = [pltpu.make_async_copy(mine, wide_ref.at[peer], sems.at[peer]) for peer in range(peers)]
        for copy in copies:
            copy.start()
        for copy in copies:
            copy.wait()

    return pl.pallas_call(
        kernel,
        out_shape=[
            jax.ShapeDtypeStruct((peers, own, width), BF),
            pltpu.VMEM((own, width), BF),
            pltpu.VMEM((own, width), F32),
        ],
        in_specs=[VMEM] * 2,
        out_specs=[HBM, VMEM, VMEM],
        scratch_shapes=[pltpu.VMEM((own, width), BF), pltpu.SemaphoreType.DMA((peers,))],
        compiler_params=pltpu.CompilerParams(vmem_limit_bytes=20 * MIB),
        name="units",
    )(kept, got)


def tile(sharpness, offset, mine, others, total, own, positives=False, final=False, block=256):
    n, width = mine.shape
    m = others[0].shape[0]
    blocks = n // block

    def kernel(t_ref, b_ref, mine_ref, *rest):
        out_ref = rest[-1]
        t = t_ref[0]
        slope, start = -LOG2E * t, -LOG2E * b_ref[0]
        zhi, last = lax.axis_index("zhi"), lax.axis_size("zhi") - 1
        mine_at = lax.axis_index(PLANE) * own
        other_at = jnp.where(lax.axis_index("core") == 0, zhi, last - zhi) * own
        for i in range(blocks):
            at = pl.multiple_of(lax.rem(mine_at // block + 1 + i, blocks) * block, block)
            sums = None if total is None else rest[len(others)][pl.ds(at, block)]
            for other_ref in rest[: len(others)]:
                dots = lax.dot_general(
                    mine_ref[pl.ds(at, block)], other_ref[...], (((1,), (1,)), ((), ())), preferred_element_type=F32
                )
                e = jnp.exp2(dots * slope + start)
                coef = pl.reciprocal(1.0 + e)
                if positives and i == blocks - 1:
                    row = lax.broadcasted_iota(jnp.int32, (block, 1), 0) + (at - mine_at)
                    row = jnp.where((row >= 0) & (row < own), row, -m)
                    col = lax.broadcasted_iota(jnp.int32, (1, m), 1) - other_at
                    coef = jnp.where(row == col, -e, 1.0) * coef
                part = jnp.dot(coef.astype(BF), other_ref[...], preferred_element_type=F32)
                sums = part if sums is None else sums + part
            out_ref[pl.ds(at, block)] = (t * sums).astype(BF) if final else sums

    totals = [] if total is None else [total]
    return pl.pallas_call(
        kernel,
        out_shape=pltpu.VMEM((n, width), BF if final else F32),
        in_specs=[SMEM, SMEM, VMEM] + [VMEM] * (len(others) + len(totals)),
        out_specs=VMEM,
        compiler_params=pltpu.CompilerParams(vmem_limit_bytes=30 * MIB),
        cost_estimate=pl.CostEstimate(
            flops=4 * n * m * width * len(others),
            bytes_accessed=2 * width * (n + m * len(others)),
            transcendentals=2 * n * m * len(others),
        ),
        name="tile",
    )(sharpness, offset, mine, *others, *totals)


def finish(sums, embed):
    def kernel(sums_ref, embed_ref, out_ref):
        inv, unit = normalize(embed_ref[...])
        grad = jnp.sum(sums_ref[...].astype(F32), axis=0)
        along = jnp.sum(grad * unit, axis=1, keepdims=True)
        out_ref[...] = (inv * (grad - along * unit)).astype(BF)

    return pl.pallas_call(
        kernel,
        out_shape=pltpu.VMEM(embed.shape, BF),
        in_specs=[VMEM] * 2,
        out_specs=VMEM,
        compiler_params=pltpu.CompilerParams(vmem_limit_bytes=20 * MIB),
        name="finish",
    )(sums, embed)


def heads_back(delta, vision_map, sentence_map, chunks=3):
    own, width = delta.shape[1:]
    rows, depth = 2 * own, vision_map.shape[0]
    step = depth // chunks

    def kernel(d, wv, ws, image, text, buf, sems):
        copies = []
        for tower, (w, out) in enumerate(((wv, image), (ws, text))):
            x = jnp.concatenate([d[tower], d[2 + tower]], axis=0)
            for c in range(chunks):
                cut = slice(c * step, (c + 1) * step)
                part = lax.dot_general(x, w[cut], (((1,), (1,)), ((), ())), preferred_element_type=F32)
                buf[tower, :, cut] = part.astype(BF)
                copy = pltpu.make_async_copy(buf.at[tower, :, cut], out.at[:, cut], sems.at[tower, c])
                copy.start()
                copies.append(copy)
        for copy in copies:
            copy.wait()

    return pl.pallas_call(
        kernel,
        out_shape=[jax.ShapeDtypeStruct((rows, depth), BF)] * 2,
        in_specs=[VMEM] * 3,
        out_specs=[HBM] * 2,
        scratch_shapes=[pltpu.VMEM((2, rows, depth), BF), pltpu.SemaphoreType.DMA((2, chunks))],
        compiler_params=pltpu.CompilerParams(vmem_limit_bytes=20 * MIB),
        name="heads_back",
    )(delta, vision_map, sentence_map)


def shards(vision, sentence, vision_map, sentence_map, sharpness, offset):
    width = vision_map.shape[1]
    own = vision.shape[0] // 2
    sizes = [lax.axis_size(a) for a in AXES]
    peers = lax.axis_size(PLANE)

    parts = lax.all_gather(heads(vision, sentence, vision_map, sentence_map), "core", axis=0)
    given, kept = chip_sums(parts)
    wide, line, embed = units(kept, lax.all_gather(given, "yhi", axis=0), peers)

    wide, line = lax.optimization_barrier((wide, line))
    mine = lax.all_to_all(wide, PLANE, 0, 0).reshape(peers * own, width)
    line = lax.all_gather(line, AXES, axis=0, tiled=True, axis_index_groups=far_groups(sizes))
    first, second, third = (
        lax.ppermute(line, AXES, from_line(sizes, steps)) for steps in ((1, 1), (-1, -1), (2, -2))
    )
    grad = tile(sharpness, offset, mine, [line], None, own, positives=True)
    grad = tile(sharpness, offset, mine, [third], grad, own)
    grad = tile(sharpness, offset, mine, [first, second], grad, own, final=True)

    grad = lax.all_to_all(grad.reshape(peers, own, width), PLANE, 0, 0)
    delta = lax.all_gather(finish(grad, embed), GROUP, axis=0)
    return tuple(heads_back(delta, vision_map, sentence_map))


def solution(mesh):
    x, ylo, zlo = 4, 2, 4
    zhi = mesh.shape["dp"] // (x * ylo * zlo)
    fine = Mesh(mesh.devices.reshape(ylo, zhi, zlo, x, 2, 2), AXES)
    dp, mp = ("ylo", "zhi", "zlo", "x"), ("yhi", "core")
    in_specs = (P(dp, mp), P(dp, mp), P(mp, None), P(mp, None), P(), P())
    out_specs = (P(dp, mp), P(dp, mp))
    return jax.shard_map(shards, mesh=fine, in_specs=in_specs, out_specs=out_specs, check_vma=False)
```

```python
import math

import jax
import jax.numpy as jnp
import numpy as np
from jax import lax
from jax.experimental import pallas as pl
from jax.experimental.pallas import tpu as pltpu
from jax.sharding import Mesh
from jax.sharding import PartitionSpec as P

EPS = 1e-06
LOG2E = math.log2(math.e)
BF = jnp.bfloat16
F32 = jnp.float32
MIB = 2**20
AXES = ("ylo", "zhi", "zlo", "x", "yhi", "core")
LINE = ("zhi", "zlo")
PLANE = ("ylo", "x", "yhi")
GROUP = ("yhi", "core")

VMEM = pl.BlockSpec(memory_space=pltpu.VMEM)
SMEM = pl.BlockSpec(memory_space=pltpu.SMEM)
HBM = pl.BlockSpec(memory_space=pltpu.MemorySpace.HBM)


def normalize(embed):
    inv = lax.rsqrt(jnp.sum(embed * embed, axis=1, keepdims=True) + EPS)
    return (inv, embed * inv)


def opposite_groups(sizes, axis):
    ids = np.arange(math.prod(sizes)).reshape(sizes)
    groups = []
    for core in range(2):
        part = np.moveaxis(ids[..., core], AXES.index(axis), -1).reshape(-1, sizes[AXES.index(axis)])
        groups += (part[:, ::-1] if core == 1 else part).tolist()
    return groups


def from_line(sizes, steps):
    ids = np.arange(math.prod(sizes)).reshape(sizes)
    pairs = []
    for core, step in enumerate(steps):
        target = ids[..., core].transpose(1, 2, 0, 3, 4).reshape(sizes[1] * sizes[2], -1)
        source = np.roll(target, -step, axis=0)
        pairs += zip(source.ravel().tolist(), target.ravel().tolist())
    return pairs


def heads(vision, sentence, vision_map, sentence_map, chunks=3):
    rows, depth = vision.shape
    width = vision_map.shape[1]
    own, step = rows // 2, depth // chunks

    def kernel(v, s, wv, ws, out, vb, sb, wvb, wsb, sems):
        towers = ((v, wv, vb, wvb), (s, ws, sb, wsb))
        copies = []
        for tower, (x, w, xb, wb) in enumerate(towers):
            for c in range(chunks):
                cut = pl.ds(c * step, step)
                pair = (
                    pltpu.make_async_copy(x.at[:, cut], xb.at[:, cut], sems.at[tower, c, 0]),
                    pltpu.make_async_copy(w.at[cut], wb.at[cut], sems.at[tower, c, 1]),
                )
                for copy in pair:
                    copy.start()
                copies.append(pair)
        for tower, (_, _, xb, wb) in enumerate(towers):
            total = None
            for c in range(chunks):
                for copy in copies[tower * chunks + c]:
                    copy.wait()
                cut = slice(c * step, (c + 1) * step)
                part = jnp.dot(xb[:, cut], wb[cut], preferred_element_type=F32)
                total = part if total is None else total + part
            total = total.astype(BF)
            for half in range(2):
                out[half, :, tower * width : (tower + 1) * width] = total[half * own : (half + 1) * own]

    return pl.pallas_call(
        kernel,
        out_shape=pltpu.VMEM((2, own, 2 * width), BF),
        in_specs=[HBM] * 4,
        out_specs=VMEM,
        scratch_shapes=[
            pltpu.VMEM((rows, depth), BF),
            pltpu.VMEM((rows, depth), BF),
            pltpu.VMEM((depth, width), BF),
            pltpu.VMEM((depth, width), BF),
            pltpu.SemaphoreType.DMA((2, chunks, 2)),
        ],
        compiler_params=pltpu.CompilerParams(vmem_limit_bytes=63 * MIB),
        name="heads",
    )(vision, sentence, vision_map, sentence_map)


def chip_sums(parts):
    _, _, own, width = parts.shape

    def kernel(parts_ref, given_ref, kept_ref):
        for yhi in range(2):

            @pl.when(lax.axis_index("yhi") == yhi)
            def _():
                total = [parts_ref[0, h].astype(F32) + parts_ref[1, h].astype(F32) for h in (yhi, 1 - yhi)]
                kept_ref[...] = total[0]
                given_ref[...] = total[1].astype(BF)

    return pl.pallas_call(
        kernel,
        out_shape=[pltpu.VMEM((own, width), BF), pltpu.VMEM((own, width), F32)],
        in_specs=[VMEM],
        out_specs=[VMEM, VMEM],
        compiler_params=pltpu.CompilerParams(vmem_limit_bytes=20 * MIB),
        name="chip_sums",
    )(parts)


def units(kept, got, peers):
    own, width = kept.shape[0], kept.shape[1] // 2

    def kernel(kept_ref, got_ref, wide_ref, line_ref, embed_ref):
        towers = [slice(0, width), slice(width, 2 * width)]
        for yhi in range(2):
            for core in range(2):

                @pl.when((lax.axis_index("yhi") == yhi) & (lax.axis_index("core") == core))
                def _():
                    other = 1 - yhi if core == 0 else yhi
                    embed = [kept_ref[:, cut] + got_ref[other, :, cut].astype(F32) for cut in towers]
                    embed_ref[...] = embed[core]
                    mine = normalize(embed[core])[1].astype(BF)
                    for peer in range(peers):
                        wide_ref[peer] = mine
                    line_ref[...] = normalize(embed[1 - core])[1].astype(BF)

    return pl.pallas_call(
        kernel,
        out_shape=[
            pltpu.VMEM((peers, own, width), BF),
            pltpu.VMEM((own, width), BF),
            pltpu.VMEM((own, width), F32),
        ],
        in_specs=[VMEM] * 2,
        out_specs=[VMEM] * 3,
        compiler_params=pltpu.CompilerParams(vmem_limit_bytes=20 * MIB),
        name="units",
    )(kept, got)


def tile(sharpness, offset, mine, others, total, own, positives=False, final=False, block=256):
    n, width = mine.shape
    m = others[0].shape[0]
    blocks = n // block

    def kernel(t_ref, b_ref, mine_ref, *rest):
        out_ref = rest[-1]
        t = t_ref[0]
        slope, start = -LOG2E * t, -LOG2E * b_ref[0]
        zhi, last = lax.axis_index("zhi"), lax.axis_size("zhi") - 1
        mine_at = lax.axis_index(PLANE) * own
        other_at = jnp.where(lax.axis_index("core") == 0, zhi, last - zhi) * own
        for i in range(blocks):
            at = pl.multiple_of(lax.rem(mine_at // block + 1 + i, blocks) * block, block)
            sums = None if total is None else rest[len(others)][pl.ds(at, block)]
            for other_ref in rest[: len(others)]:
                dots = lax.dot_general(
                    mine_ref[pl.ds(at, block)], other_ref[...], (((1,), (1,)), ((), ())), preferred_element_type=F32
                )
                e = jnp.exp2(dots * slope + start)
                coef = pl.reciprocal(1.0 + e)
                if positives and i == blocks - 1:
                    row = lax.broadcasted_iota(jnp.int32, (block, 1), 0) + (at - mine_at)
                    row = jnp.where((row >= 0) & (row < own), row, -m)
                    col = lax.broadcasted_iota(jnp.int32, (1, m), 1) - other_at
                    coef = jnp.where(row == col, -e, 1.0) * coef
                part = jnp.dot(coef.astype(BF), other_ref[...], preferred_element_type=F32)
                sums = part if sums is None else sums + part
            out_ref[pl.ds(at, block)] = (t * sums).astype(BF) if final else sums

    totals = [] if total is None else [total]
    return pl.pallas_call(
        kernel,
        out_shape=pltpu.VMEM((n, width), BF if final else F32),
        in_specs=[SMEM, SMEM, VMEM] + [VMEM] * (len(others) + len(totals)),
        out_specs=VMEM,
        compiler_params=pltpu.CompilerParams(vmem_limit_bytes=30 * MIB),
        cost_estimate=pl.CostEstimate(
            flops=4 * n * m * width * len(others),
            bytes_accessed=2 * width * (n + m * len(others)),
            transcendentals=2 * n * m * len(others),
        ),
        name="tile",
    )(sharpness, offset, mine, *others, *totals)


def finish(sums, embed):
    def kernel(sums_ref, embed_ref, out_ref):
        inv, unit = normalize(embed_ref[...])
        grad = jnp.sum(sums_ref[...].astype(F32), axis=0)
        along = jnp.sum(grad * unit, axis=1, keepdims=True)
        out_ref[...] = (inv * (grad - along * unit)).astype(BF)

    return pl.pallas_call(
        kernel,
        out_shape=pltpu.VMEM(embed.shape, BF),
        in_specs=[VMEM] * 2,
        out_specs=VMEM,
        compiler_params=pltpu.CompilerParams(vmem_limit_bytes=20 * MIB),
        name="finish",
    )(sums, embed)


def heads_back(delta, vision_map, sentence_map, chunks=3):
    own, width = delta.shape[1:]
    rows, depth = 2 * own, vision_map.shape[0]
    step = depth // chunks

    def kernel(d, wv, ws, image, text, buf, sems):
        copies = []
        for tower, (w, out) in enumerate(((wv, image), (ws, text))):
            x = jnp.concatenate([d[tower], d[2 + tower]], axis=0)
            for c in range(chunks):
                cut = slice(c * step, (c + 1) * step)
                part = lax.dot_general(x, w[cut], (((1,), (1,)), ((), ())), preferred_element_type=F32)
                buf[tower, :, cut] = part.astype(BF)
                copy = pltpu.make_async_copy(buf.at[tower, :, cut], out.at[:, cut], sems.at[tower, c])
                copy.start()
                copies.append(copy)
        for copy in copies:
            copy.wait()

    return pl.pallas_call(
        kernel,
        out_shape=[jax.ShapeDtypeStruct((rows, depth), BF)] * 2,
        in_specs=[VMEM] * 3,
        out_specs=[HBM] * 2,
        scratch_shapes=[pltpu.VMEM((2, rows, depth), BF), pltpu.SemaphoreType.DMA((2, chunks))],
        compiler_params=pltpu.CompilerParams(vmem_limit_bytes=20 * MIB),
        name="heads_back",
    )(delta, vision_map, sentence_map)


def shards(vision, sentence, vision_map, sentence_map, sharpness, offset):
    width = vision_map.shape[1]
    own = vision.shape[0] // 2
    sizes = [lax.axis_size(a) for a in AXES]
    peers = lax.axis_size(PLANE)

    def gather(x, axis):
        return lax.all_gather(x, AXES, axis=0, axis_index_groups=opposite_groups(sizes, axis))

    parts = lax.all_gather(heads(vision, sentence, vision_map, sentence_map), "core", axis=0)
    given, kept = chip_sums(parts)
    wide, line, embed = units(kept, gather(given, "yhi"), peers)

    wide, line = lax.optimization_barrier((wide, line))
    mine = lax.all_to_all(wide, PLANE, 0, 0).reshape(peers * own, width)
    line = gather(line, "zhi").reshape(-1, width)
    first, second, third = (
        lax.ppermute(line, AXES, from_line(sizes, steps)) for steps in ((2, -2), (-1, 1), (1, -1))
    )
    grad = tile(sharpness, offset, mine, [line], None, own, positives=True)
    grad = tile(sharpness, offset, mine, [first], grad, own)
    grad = tile(sharpness, offset, mine, [second, third], grad, own, final=True)

    grad = lax.all_to_all(grad.reshape(peers, own, width), PLANE, 0, 0)
    delta = lax.all_gather(finish(grad, embed), GROUP, axis=0)
    return tuple(heads_back(delta, vision_map, sentence_map))


def solution(mesh):
    x, ylo, zlo = 4, 2, 4
    zhi = mesh.shape["dp"] // (x * ylo * zlo)
    fine = Mesh(mesh.devices.reshape(ylo, zhi, zlo, x, 2, 2), AXES)
    dp, mp = ("ylo", "zhi", "zlo", "x"), ("yhi", "core")
    in_specs = (P(dp, mp), P(dp, mp), P(mp, None), P(mp, None), P(), P())
    out_specs = (P(dp, mp), P(dp, mp))
    return jax.shard_map(shards, mesh=fine, in_specs=in_specs, out_specs=out_specs, check_vma=False)
```

```python
import math

import jax
import jax.numpy as jnp
import numpy as np
from jax import lax
from jax.experimental import pallas as pl
from jax.experimental.pallas import tpu as pltpu
from jax.sharding import Mesh
from jax.sharding import PartitionSpec as P

EPS = 1e-06
LOG2E = math.log2(math.e)
BF = jnp.bfloat16
F32 = jnp.float32
MIB = 2**20
AXES = ("ylo", "zhi", "zlo", "x", "yhi", "core")
LINE = ("zhi", "zlo")
PLANE = ("ylo", "x", "yhi")
GROUP = ("yhi", "core")

VMEM = pl.BlockSpec(memory_space=pltpu.VMEM)
SMEM = pl.BlockSpec(memory_space=pltpu.SMEM)
HBM = pl.BlockSpec(memory_space=pltpu.MemorySpace.HBM)


def normalize(embed):
    inv = lax.rsqrt(jnp.sum(embed * embed, axis=1, keepdims=True) + EPS)
    return (inv, embed * inv)


def far_groups(sizes):
    ids = np.arange(math.prod(sizes)).reshape(sizes)
    groups = []
    for core in range(2):
        part = np.moveaxis(ids[..., core], 1, -1).reshape(-1, sizes[1])
        groups += (part[:, ::-1] if core == 1 else part).tolist()
    return groups


def from_line(sizes, steps):
    ids = np.arange(math.prod(sizes)).reshape(sizes)
    pairs = []
    for core, step in enumerate(steps):
        target = ids[..., core].transpose(1, 2, 0, 3, 4).reshape(sizes[1] * sizes[2], -1)
        source = np.roll(target, -step, axis=0)
        pairs += zip(source.ravel().tolist(), target.ravel().tolist())
    return pairs


def heads(vision, sentence, vision_map, sentence_map, chunks=3):
    rows, depth = vision.shape
    width = vision_map.shape[1]
    own, step = rows // 2, depth // chunks

    def kernel(v, s, wv, ws, out, vb, sb, wvb, wsb, sems):
        towers = ((v, wv, vb, wvb), (s, ws, sb, wsb))
        copies = []
        for tower, (x, w, xb, wb) in enumerate(towers):
            for c in range(chunks):
                cut = pl.ds(c * step, step)
                pair = (
                    pltpu.make_async_copy(x.at[:, cut], xb.at[:, cut], sems.at[tower, c, 0]),
                    pltpu.make_async_copy(w.at[cut], wb.at[cut], sems.at[tower, c, 1]),
                )
                for copy in pair:
                    copy.start()
                copies.append(pair)
        for tower, (_, _, xb, wb) in enumerate(towers):
            total = None
            for c in range(chunks):
                for copy in copies[tower * chunks + c]:
                    copy.wait()
                cut = slice(c * step, (c + 1) * step)
                part = jnp.dot(xb[:, cut], wb[cut], preferred_element_type=F32)
                total = part if total is None else total + part
            total = total.astype(BF)
            for half in range(2):
                out[half, :, tower * width : (tower + 1) * width] = total[half * own : (half + 1) * own]

    return pl.pallas_call(
        kernel,
        out_shape=pltpu.VMEM((2, own, 2 * width), BF),
        in_specs=[HBM] * 4,
        out_specs=VMEM,
        scratch_shapes=[
            pltpu.VMEM((rows, depth), BF),
            pltpu.VMEM((rows, depth), BF),
            pltpu.VMEM((depth, width), BF),
            pltpu.VMEM((depth, width), BF),
            pltpu.SemaphoreType.DMA((2, chunks, 2)),
        ],
        compiler_params=pltpu.CompilerParams(vmem_limit_bytes=63 * MIB),
        name="heads",
    )(vision, sentence, vision_map, sentence_map)


def chip_sums(parts):
    _, _, own, width = parts.shape

    def kernel(parts_ref, given_ref, kept_ref):
        for yhi in range(2):

            @pl.when(lax.axis_index("yhi") == yhi)
            def _():
                total = [parts_ref[0, h].astype(F32) + parts_ref[1, h].astype(F32) for h in (yhi, 1 - yhi)]
                kept_ref[...] = total[0]
                given_ref[...] = total[1].astype(BF)

    return pl.pallas_call(
        kernel,
        out_shape=[pltpu.VMEM((own, width), BF), pltpu.VMEM((own, width), F32)],
        in_specs=[VMEM],
        out_specs=[VMEM, VMEM],
        compiler_params=pltpu.CompilerParams(vmem_limit_bytes=20 * MIB),
        name="chip_sums",
    )(parts)


def units(kept, got, peers):
    own, width = kept.shape[0], kept.shape[1] // 2

    def kernel(kept_ref, got_ref, wide_ref, line_ref, embed_ref):
        towers = [slice(0, width), slice(width, 2 * width)]
        for yhi in range(2):
            for core in range(2):

                @pl.when((lax.axis_index("yhi") == yhi) & (lax.axis_index("core") == core))
                def _():
                    embed = [kept_ref[:, cut] + got_ref[1 - yhi, :, cut].astype(F32) for cut in towers]
                    embed_ref[...] = embed[core]
                    mine = normalize(embed[core])[1].astype(BF)
                    for peer in range(peers):
                        wide_ref[peer] = mine
                    line_ref[...] = normalize(embed[1 - core])[1].astype(BF)

    return pl.pallas_call(
        kernel,
        out_shape=[
            pltpu.VMEM((peers, own, width), BF),
            pltpu.VMEM((own, width), BF),
            pltpu.VMEM((own, width), F32),
        ],
        in_specs=[VMEM] * 2,
        out_specs=[VMEM] * 3,
        compiler_params=pltpu.CompilerParams(vmem_limit_bytes=20 * MIB),
        name="units",
    )(kept, got)


def tile(sharpness, offset, mine, others, total, own, positives=False, final=False, block=256):
    n, width = mine.shape
    m = others[0].shape[0]
    blocks = n // block

    def kernel(t_ref, b_ref, mine_ref, *rest):
        out_ref = rest[-1]
        t = t_ref[0]
        slope, start = -LOG2E * t, -LOG2E * b_ref[0]
        zhi, last = lax.axis_index("zhi"), lax.axis_size("zhi") - 1
        mine_at = lax.axis_index(PLANE) * own
        other_at = jnp.where(lax.axis_index("core") == 0, zhi, last - zhi) * own
        for i in range(blocks):
            at = pl.multiple_of(lax.rem(mine_at // block + 1 + i, blocks) * block, block)
            sums = None if total is None else rest[len(others)][pl.ds(at, block)]
            for other_ref in rest[: len(others)]:
                dots = lax.dot_general(
                    mine_ref[pl.ds(at, block)], other_ref[...], (((1,), (1,)), ((), ())), preferred_element_type=F32
                )
                e = jnp.exp2(dots * slope + start)
                coef = pl.reciprocal(1.0 + e)
                if positives and i == blocks - 1:
                    row = lax.broadcasted_iota(jnp.int32, (block, 1), 0) + (at - mine_at)
                    row = jnp.where((row >= 0) & (row < own), row, -m)
                    col = lax.broadcasted_iota(jnp.int32, (1, m), 1) - other_at
                    coef = jnp.where(row == col, -e, 1.0) * coef
                part = jnp.dot(coef.astype(BF), other_ref[...], preferred_element_type=F32)
                sums = part if sums is None else sums + part
            out_ref[pl.ds(at, block)] = (t * sums).astype(BF) if final else sums

    totals = [] if total is None else [total]
    return pl.pallas_call(
        kernel,
        out_shape=pltpu.VMEM((n, width), BF if final else F32),
        in_specs=[SMEM, SMEM, VMEM] + [VMEM] * (len(others) + len(totals)),
        out_specs=VMEM,
        compiler_params=pltpu.CompilerParams(vmem_limit_bytes=30 * MIB),
        cost_estimate=pl.CostEstimate(
            flops=4 * n * m * width * len(others),
            bytes_accessed=2 * width * (n + m * len(others)),
            transcendentals=2 * n * m * len(others),
        ),
        name="tile",
    )(sharpness, offset, mine, *others, *totals)


def finish(sums, embed):
    def kernel(sums_ref, embed_ref, out_ref):
        inv, unit = normalize(embed_ref[...])
        grad = jnp.sum(sums_ref[...].astype(F32), axis=0)
        along = jnp.sum(grad * unit, axis=1, keepdims=True)
        out_ref[...] = (inv * (grad - along * unit)).astype(BF)

    return pl.pallas_call(
        kernel,
        out_shape=pltpu.VMEM(embed.shape, BF),
        in_specs=[VMEM] * 2,
        out_specs=VMEM,
        compiler_params=pltpu.CompilerParams(vmem_limit_bytes=20 * MIB),
        name="finish",
    )(sums, embed)


def heads_back(delta, vision_map, sentence_map, chunks=3):
    own, width = delta.shape[1:]
    rows, depth = 2 * own, vision_map.shape[0]
    step = depth // chunks

    def kernel(d, wv, ws, image, text, buf, sems):
        copies = []
        for tower, (w, out) in enumerate(((wv, image), (ws, text))):
            x = jnp.concatenate([d[tower], d[2 + tower]], axis=0)
            for c in range(chunks):
                cut = slice(c * step, (c + 1) * step)
                part = lax.dot_general(x, w[cut], (((1,), (1,)), ((), ())), preferred_element_type=F32)
                buf[tower, :, cut] = part.astype(BF)
                copy = pltpu.make_async_copy(buf.at[tower, :, cut], out.at[:, cut], sems.at[tower, c])
                copy.start()
                copies.append(copy)
        for copy in copies:
            copy.wait()

    return pl.pallas_call(
        kernel,
        out_shape=[jax.ShapeDtypeStruct((rows, depth), BF)] * 2,
        in_specs=[VMEM] * 3,
        out_specs=[HBM] * 2,
        scratch_shapes=[pltpu.VMEM((2, rows, depth), BF), pltpu.SemaphoreType.DMA((2, chunks))],
        compiler_params=pltpu.CompilerParams(vmem_limit_bytes=20 * MIB),
        name="heads_back",
    )(delta, vision_map, sentence_map)


def shards(vision, sentence, vision_map, sentence_map, sharpness, offset):
    width = vision_map.shape[1]
    own = vision.shape[0] // 2
    sizes = [lax.axis_size(a) for a in AXES]
    peers = lax.axis_size(PLANE)

    parts = lax.all_gather(heads(vision, sentence, vision_map, sentence_map), "core", axis=0)
    given, kept = chip_sums(parts)
    wide, line, embed = units(kept, lax.all_gather(given, "yhi", axis=0), peers)

    wide, line = lax.optimization_barrier((wide, line))
    mine = lax.all_to_all(wide, PLANE, 0, 0).reshape(peers * own, width)
    line = lax.all_gather(line, AXES, axis=0, tiled=True, axis_index_groups=far_groups(sizes))
    first, second, third = (
        lax.ppermute(line, AXES, from_line(sizes, steps)) for steps in ((1, 1), (-1, -1), (2, -2))
    )
    grad = tile(sharpness, offset, mine, [line], None, own, positives=True)
    grad = tile(sharpness, offset, mine, [third], grad, own)
    grad = tile(sharpness, offset, mine, [second, first], grad, own, final=True)

    grad = lax.all_to_all(grad.reshape(peers, own, width), PLANE, 0, 0)
    delta = lax.all_gather(finish(grad, embed), GROUP, axis=0)
    return tuple(heads_back(delta, vision_map, sentence_map))


def solution(mesh):
    x, ylo, zlo = 4, 2, 4
    zhi = mesh.shape["dp"] // (x * ylo * zlo)
    fine = Mesh(mesh.devices.reshape(ylo, zhi, zlo, x, 2, 2), AXES)
    dp, mp = ("ylo", "zhi", "zlo", "x"), ("yhi", "core")
    in_specs = (P(dp, mp), P(dp, mp), P(mp, None), P(mp, None), P(), P())
    out_specs = (P(dp, mp), P(dp, mp))
    return jax.shard_map(shards, mesh=fine, in_specs=in_specs, out_specs=out_specs, check_vma=False)
```

```python
import math

import jax
import jax.numpy as jnp
import numpy as np
from jax import lax
from jax.experimental import pallas as pl
from jax.experimental.pallas import tpu as pltpu
from jax.sharding import Mesh
from jax.sharding import PartitionSpec as P

EPS = 1e-06
LOG2E = math.log2(math.e)
BF = jnp.bfloat16
F32 = jnp.float32
MIB = 2**20
AXES = ("ylo", "zhi", "zlo", "x", "yhi", "core")
LINE = ("zhi", "zlo")
PLANE = ("ylo", "x", "yhi")
GROUP = ("yhi", "core")

VMEM = pl.BlockSpec(memory_space=pltpu.VMEM)
SMEM = pl.BlockSpec(memory_space=pltpu.SMEM)
HBM = pl.BlockSpec(memory_space=pltpu.MemorySpace.HBM)


def normalize(embed):
    inv = lax.rsqrt(jnp.sum(embed * embed, axis=1, keepdims=True) + EPS)
    return (inv, embed * inv)


def far_groups(sizes):
    ids = np.arange(math.prod(sizes)).reshape(sizes)
    groups = []
    for core in range(2):
        part = np.moveaxis(ids[..., core], 1, -1).reshape(-1, sizes[1])
        groups += (part[:, ::-1] if core == 1 else part).tolist()
    return groups


def from_line(sizes, steps):
    ids = np.arange(math.prod(sizes)).reshape(sizes)
    pairs = []
    for core, step in enumerate(steps):
        target = ids[..., core].transpose(1, 2, 0, 3, 4).reshape(sizes[1] * sizes[2], -1)
        source = np.roll(target, -step, axis=0)
        pairs += zip(source.ravel().tolist(), target.ravel().tolist())
    return pairs


def heads(vision, sentence, vision_map, sentence_map, chunks=3):
    rows, depth = vision.shape
    width = vision_map.shape[1]
    own, step = rows // 2, depth // chunks

    def kernel(v, s, wv, ws, out, vb, sb, wvb, wsb, sems):
        towers = ((v, wv, vb, wvb), (s, ws, sb, wsb))
        copies = []
        for tower, (x, w, xb, wb) in enumerate(towers):
            for c in range(chunks):
                cut = pl.ds(c * step, step)
                pair = (
                    pltpu.make_async_copy(x.at[:, cut], xb.at[:, cut], sems.at[tower, c, 0]),
                    pltpu.make_async_copy(w.at[cut], wb.at[cut], sems.at[tower, c, 1]),
                )
                for copy in pair:
                    copy.start()
                copies.append(pair)
        for tower, (_, _, xb, wb) in enumerate(towers):
            total = None
            for c in range(chunks):
                for copy in copies[tower * chunks + c]:
                    copy.wait()
                cut = slice(c * step, (c + 1) * step)
                part = jnp.dot(xb[:, cut], wb[cut], preferred_element_type=F32)
                total = part if total is None else total + part
            total = total.astype(BF)
            for half in range(2):
                out[half, :, tower * width : (tower + 1) * width] = total[half * own : (half + 1) * own]

    return pl.pallas_call(
        kernel,
        out_shape=pltpu.VMEM((2, own, 2 * width), BF),
        in_specs=[HBM] * 4,
        out_specs=VMEM,
        scratch_shapes=[
            pltpu.VMEM((rows, depth), BF),
            pltpu.VMEM((rows, depth), BF),
            pltpu.VMEM((depth, width), BF),
            pltpu.VMEM((depth, width), BF),
            pltpu.SemaphoreType.DMA((2, chunks, 2)),
        ],
        compiler_params=pltpu.CompilerParams(vmem_limit_bytes=63 * MIB),
        name="heads",
    )(vision, sentence, vision_map, sentence_map)


def chip_sums(parts):
    _, _, own, width = parts.shape

    def kernel(parts_ref, given_ref, kept_ref):
        for yhi in range(2):

            @pl.when(lax.axis_index("yhi") == yhi)
            def _():
                total = [parts_ref[0, h].astype(F32) + parts_ref[1, h].astype(F32) for h in (yhi, 1 - yhi)]
                kept_ref[...] = total[0]
                given_ref[...] = total[1].astype(BF)

    return pl.pallas_call(
        kernel,
        out_shape=[pltpu.VMEM((own, width), BF), pltpu.VMEM((own, width), F32)],
        in_specs=[VMEM],
        out_specs=[VMEM, VMEM],
        compiler_params=pltpu.CompilerParams(vmem_limit_bytes=20 * MIB),
        name="chip_sums",
    )(parts)


def units(kept, got, peers):
    own, width = kept.shape[0], kept.shape[1] // 2

    def kernel(kept_ref, got_ref, wide_ref, line_ref, embed_ref, mine, sems):
        towers = [slice(0, width), slice(width, 2 * width)]
        for yhi in range(2):
            for core in range(2):

                @pl.when((lax.axis_index("yhi") == yhi) & (lax.axis_index("core") == core))
                def _():
                    embed = [kept_ref[:, cut] + got_ref[1 - yhi, :, cut].astype(F32) for cut in towers]
                    embed_ref[...] = embed[core]
                    mine[...] = normalize(embed[core])[1].astype(BF)
                    line_ref[...] = normalize(embed[1 - core])[1].astype(BF)

        copies = [pltpu.make_async_copy(mine, wide_ref.at[peer], sems.at[peer]) for peer in range(peers)]
        for copy in copies:
            copy.start()
        for copy in copies:
            copy.wait()

    return pl.pallas_call(
        kernel,
        out_shape=[
            jax.ShapeDtypeStruct((peers, own, width), BF),
            pltpu.VMEM((own, width), BF),
            pltpu.VMEM((own, width), F32),
        ],
        in_specs=[VMEM] * 2,
        out_specs=[HBM, VMEM, VMEM],
        scratch_shapes=[pltpu.VMEM((own, width), BF), pltpu.SemaphoreType.DMA((peers,))],
        compiler_params=pltpu.CompilerParams(vmem_limit_bytes=20 * MIB),
        name="units",
    )(kept, got)


def tile(sharpness, offset, mine, others, total, own, positives=False, final=False, block=256):
    n, width = mine.shape
    m = others[0].shape[0]
    blocks = n // block

    def kernel(t_ref, b_ref, mine_ref, *rest):
        out_ref = rest[-1]
        t = t_ref[0]
        slope, start = -LOG2E * t, -LOG2E * b_ref[0]
        zhi, last = lax.axis_index("zhi"), lax.axis_size("zhi") - 1
        mine_at = lax.axis_index(PLANE) * own
        other_at = jnp.where(lax.axis_index("core") == 0, zhi, last - zhi) * own
        for i in range(blocks):
            at = pl.multiple_of(lax.rem(mine_at // block + 1 + i, blocks) * block, block)
            sums = None if total is None else rest[len(others)][pl.ds(at, block)]
            for other_ref in rest[: len(others)]:
                dots = lax.dot_general(
                    mine_ref[pl.ds(at, block)], other_ref[...], (((1,), (1,)), ((), ())), preferred_element_type=F32
                )
                e = jnp.exp2(dots * slope + start)
                coef = pl.reciprocal(1.0 + e)
                if positives and i == blocks - 1:
                    row = lax.broadcasted_iota(jnp.int32, (block, 1), 0) + (at - mine_at)
                    row = jnp.where((row >= 0) & (row < own), row, -m)
                    col = lax.broadcasted_iota(jnp.int32, (1, m), 1) - other_at
                    coef = jnp.where(row == col, -e, 1.0) * coef
                part = jnp.dot(coef.astype(BF), other_ref[...], preferred_element_type=F32)
                sums = part if sums is None else sums + part
            out_ref[pl.ds(at, block)] = (t * sums).astype(BF) if final else sums

    totals = [] if total is None else [total]
    return pl.pallas_call(
        kernel,
        out_shape=pltpu.VMEM((n, width), BF if final else F32),
        in_specs=[SMEM, SMEM, VMEM] + [VMEM] * (len(others) + len(totals)),
        out_specs=VMEM,
        compiler_params=pltpu.CompilerParams(vmem_limit_bytes=30 * MIB),
        cost_estimate=pl.CostEstimate(
            flops=4 * n * m * width * len(others),
            bytes_accessed=2 * width * (n + m * len(others)),
            transcendentals=2 * n * m * len(others),
        ),
        name="tile",
    )(sharpness, offset, mine, *others, *totals)


def finish(sums, embed):
    def kernel(sums_ref, embed_ref, out_ref):
        inv, unit = normalize(embed_ref[...])
        grad = jnp.sum(sums_ref[...].astype(F32), axis=0)
        along = jnp.sum(grad * unit, axis=1, keepdims=True)
        out_ref[...] = (inv * (grad - along * unit)).astype(BF)

    return pl.pallas_call(
        kernel,
        out_shape=pltpu.VMEM(embed.shape, BF),
        in_specs=[VMEM] * 2,
        out_specs=VMEM,
        compiler_params=pltpu.CompilerParams(vmem_limit_bytes=20 * MIB),
        name="finish",
    )(sums, embed)


def heads_back(delta, vision_map, sentence_map, chunks=3):
    own, width = delta.shape[1:]
    rows, depth = 2 * own, vision_map.shape[0]
    step = depth // chunks

    def kernel(d, wv, ws, image, text, buf, sems):
        copies = []
        for tower, (w, out) in enumerate(((wv, image), (ws, text))):
            x = jnp.concatenate([d[tower], d[2 + tower]], axis=0)
            for c in range(chunks):
                cut = slice(c * step, (c + 1) * step)
                part = lax.dot_general(x, w[cut], (((1,), (1,)), ((), ())), preferred_element_type=F32)
                buf[tower, :, cut] = part.astype(BF)
                copy = pltpu.make_async_copy(buf.at[tower, :, cut], out.at[:, cut], sems.at[tower, c])
                copy.start()
                copies.append(copy)
        for copy in copies:
            copy.wait()

    return pl.pallas_call(
        kernel,
        out_shape=[jax.ShapeDtypeStruct((rows, depth), BF)] * 2,
        in_specs=[VMEM] * 3,
        out_specs=[HBM] * 2,
        scratch_shapes=[pltpu.VMEM((2, rows, depth), BF), pltpu.SemaphoreType.DMA((2, chunks))],
        compiler_params=pltpu.CompilerParams(vmem_limit_bytes=20 * MIB),
        name="heads_back",
    )(delta, vision_map, sentence_map)


def shards(vision, sentence, vision_map, sentence_map, sharpness, offset):
    width = vision_map.shape[1]
    own = vision.shape[0] // 2
    sizes = [lax.axis_size(a) for a in AXES]
    peers = lax.axis_size(PLANE)

    parts = lax.all_gather(heads(vision, sentence, vision_map, sentence_map), "core", axis=0)
    given, kept = chip_sums(parts)
    wide, line, embed = units(kept, lax.all_gather(given, "yhi", axis=0), peers)

    wide, line = lax.optimization_barrier((wide, line))
    mine = lax.all_to_all(wide, PLANE, 0, 0).reshape(peers * own, width)
    line = lax.all_gather(line, AXES, axis=0, tiled=True, axis_index_groups=far_groups(sizes))
    first, second, third = (
        lax.ppermute(line, AXES, from_line(sizes, steps)) for steps in ((1, -1), (-1, 1), (2, -2))
    )
    grad = tile(sharpness, offset, mine, [line], None, own, positives=True)
    grad = tile(sharpness, offset, mine, [third], grad, own)
    grad = tile(sharpness, offset, mine, [first, second], grad, own, final=True)

    grad = lax.all_to_all(grad.reshape(peers, own, width), PLANE, 0, 0)
    delta = lax.all_gather(finish(grad, embed), GROUP, axis=0)
    return tuple(heads_back(delta, vision_map, sentence_map))


def solution(mesh):
    x, ylo, zlo = 4, 2, 4
    zhi = mesh.shape["dp"] // (x * ylo * zlo)
    fine = Mesh(mesh.devices.reshape(ylo, zhi, zlo, x, 2, 2), AXES)
    dp, mp = ("ylo", "zhi", "zlo", "x"), ("yhi", "core")
    in_specs = (P(dp, mp), P(dp, mp), P(mp, None), P(mp, None), P(), P())
    out_specs = (P(dp, mp), P(dp, mp))
    return jax.shard_map(shards, mesh=fine, in_specs=in_specs, out_specs=out_specs, check_vma=False)
```

```python
import math

import jax
import jax.numpy as jnp
import numpy as np
from jax import lax
from jax.experimental import pallas as pl
from jax.experimental.pallas import tpu as pltpu
from jax.sharding import Mesh
from jax.sharding import PartitionSpec as P

EPS = 1e-06
LOG2E = math.log2(math.e)
BF = jnp.bfloat16
F32 = jnp.float32
MIB = 2**20
AXES = ("ylo", "zhi", "zlo", "x", "yhi", "core")
LINE = ("zhi", "zlo")
PLANE = ("ylo", "x", "yhi")
GROUP = ("yhi", "core")

VMEM = pl.BlockSpec(memory_space=pltpu.VMEM)
SMEM = pl.BlockSpec(memory_space=pltpu.SMEM)
HBM = pl.BlockSpec(memory_space=pltpu.MemorySpace.HBM)


def normalize(embed):
    inv = lax.rsqrt(jnp.sum(embed * embed, axis=1, keepdims=True) + EPS)
    return (inv, embed * inv)


def opposite_groups(sizes, axes):
    ids = np.arange(math.prod(sizes)).reshape(sizes)
    kept = [i for i, name in enumerate(AXES[:-1]) if name not in axes]
    moved = [AXES.index(name) for name in axes]
    members = math.prod(sizes[i] for i in moved)
    groups = []
    for core in range(2):
        part = ids[..., core].transpose(kept + moved).reshape(-1, members)
        groups += (part[:, ::-1] if core == 1 else part).tolist()
    return groups


def from_line(sizes, steps):
    ids = np.arange(math.prod(sizes)).reshape(sizes)
    pairs = []
    for core, step in enumerate(steps):
        target = ids[..., core].transpose(1, 2, 0, 3, 4).reshape(sizes[1] * sizes[2], -1)
        source = np.roll(target, -step, axis=0)
        pairs += zip(source.ravel().tolist(), target.ravel().tolist())
    return pairs


def heads(vision, sentence, vision_map, sentence_map, chunks=3):
    rows, depth = vision.shape
    width = vision_map.shape[1]
    own, step = rows // 2, depth // chunks

    def kernel(v, s, wv, ws, out, vb, sb, wvb, wsb, sems):
        towers = ((v, wv, vb, wvb), (s, ws, sb, wsb))
        copies = []
        for tower, (x, w, xb, wb) in enumerate(towers):
            for c in range(chunks):
                cut = pl.ds(c * step, step)
                pair = (
                    pltpu.make_async_copy(x.at[:, cut], xb.at[:, cut], sems.at[tower, c, 0]),
                    pltpu.make_async_copy(w.at[cut], wb.at[cut], sems.at[tower, c, 1]),
                )
                for copy in pair:
                    copy.start()
                copies.append(pair)
        for tower, (_, _, xb, wb) in enumerate(towers):
            total = None
            for c in range(chunks):
                for copy in copies[tower * chunks + c]:
                    copy.wait()
                cut = slice(c * step, (c + 1) * step)
                part = jnp.dot(xb[:, cut], wb[cut], preferred_element_type=F32)
                total = part if total is None else total + part
            total = total.astype(BF)
            for half in range(2):
                out[half, :, tower * width : (tower + 1) * width] = total[half * own : (half + 1) * own]

    return pl.pallas_call(
        kernel,
        out_shape=pltpu.VMEM((2, own, 2 * width), BF),
        in_specs=[HBM] * 4,
        out_specs=VMEM,
        scratch_shapes=[
            pltpu.VMEM((rows, depth), BF),
            pltpu.VMEM((rows, depth), BF),
            pltpu.VMEM((depth, width), BF),
            pltpu.VMEM((depth, width), BF),
            pltpu.SemaphoreType.DMA((2, chunks, 2)),
        ],
        compiler_params=pltpu.CompilerParams(vmem_limit_bytes=63 * MIB),
        name="heads",
    )(vision, sentence, vision_map, sentence_map)


def chip_sums(parts):
    _, _, own, width = parts.shape

    def kernel(parts_ref, given_ref, kept_ref):
        for yhi in range(2):

            @pl.when(lax.axis_index("yhi") == yhi)
            def _():
                total = [parts_ref[0, h].astype(F32) + parts_ref[1, h].astype(F32) for h in (yhi, 1 - yhi)]
                kept_ref[...] = total[0]
                given_ref[...] = total[1].astype(BF)

    return pl.pallas_call(
        kernel,
        out_shape=[pltpu.VMEM((own, width), BF), pltpu.VMEM((own, width), F32)],
        in_specs=[VMEM],
        out_specs=[VMEM, VMEM],
        compiler_params=pltpu.CompilerParams(vmem_limit_bytes=20 * MIB),
        name="chip_sums",
    )(parts)


def units(kept, got, peers):
    own, width = kept.shape[0], kept.shape[1] // 2

    def kernel(kept_ref, got_ref, wide_ref, line_ref, embed_ref, mine, sems):
        towers = [slice(0, width), slice(width, 2 * width)]
        for yhi in range(2):
            for core in range(2):

                @pl.when((lax.axis_index("yhi") == yhi) & (lax.axis_index("core") == core))
                def _():
                    embed = [kept_ref[:, cut] + got_ref[1 - yhi, :, cut].astype(F32) for cut in towers]
                    embed_ref[...] = embed[core]
                    mine[...] = normalize(embed[core])[1].astype(BF)
                    line_ref[...] = normalize(embed[1 - core])[1].astype(BF)

        copies = [pltpu.make_async_copy(mine, wide_ref.at[peer], sems.at[peer]) for peer in range(peers)]
        for copy in copies:
            copy.start()
        for copy in copies:
            copy.wait()

    return pl.pallas_call(
        kernel,
        out_shape=[
            jax.ShapeDtypeStruct((peers, own, width), BF),
            pltpu.VMEM((own, width), BF),
            pltpu.VMEM((own, width), F32),
        ],
        in_specs=[VMEM] * 2,
        out_specs=[HBM, VMEM, VMEM],
        scratch_shapes=[pltpu.VMEM((own, width), BF), pltpu.SemaphoreType.DMA((peers,))],
        compiler_params=pltpu.CompilerParams(vmem_limit_bytes=20 * MIB),
        name="units",
    )(kept, got)


def tile(sharpness, offset, mine, others, total, own, positives=False, final=False, block=256):
    n, width = mine.shape
    m = others[0].shape[0]
    blocks = n // block

    def kernel(t_ref, b_ref, mine_ref, *rest):
        out_ref = rest[-1]
        t = t_ref[0]
        slope, start = -LOG2E * t, -LOG2E * b_ref[0]
        zhi, last = lax.axis_index("zhi"), lax.axis_size("zhi") - 1
        plane, most = lax.axis_index(PLANE), lax.axis_size(PLANE) - 1
        mine_at = jnp.where(lax.axis_index("core") == 0, plane, most - plane) * own
        other_at = jnp.where(lax.axis_index("core") == 0, zhi, last - zhi) * own
        for i in range(blocks):
            at = pl.multiple_of(lax.rem(mine_at // block + 1 + i, blocks) * block, block)
            sums = None if total is None else rest[len(others)][pl.ds(at, block)]
            for other_ref in rest[: len(others)]:
                dots = lax.dot_general(
                    mine_ref[pl.ds(at, block)], other_ref[...], (((1,), (1,)), ((), ())), preferred_element_type=F32
                )
                e = jnp.exp2(dots * slope + start)
                coef = pl.reciprocal(1.0 + e)
                if positives and i == blocks - 1:
                    row = lax.broadcasted_iota(jnp.int32, (block, 1), 0) + (at - mine_at)
                    row = jnp.where((row >= 0) & (row < own), row, -m)
                    col = lax.broadcasted_iota(jnp.int32, (1, m), 1) - other_at
                    coef = jnp.where(row == col, -e, 1.0) * coef
                part = jnp.dot(coef.astype(BF), other_ref[...], preferred_element_type=F32)
                sums = part if sums is None else sums + part
            out_ref[pl.ds(at, block)] = (t * sums).astype(BF) if final else sums

    totals = [] if total is None else [total]
    return pl.pallas_call(
        kernel,
        out_shape=pltpu.VMEM((n, width), BF if final else F32),
        in_specs=[SMEM, SMEM, VMEM] + [VMEM] * (len(others) + len(totals)),
        out_specs=VMEM,
        compiler_params=pltpu.CompilerParams(vmem_limit_bytes=30 * MIB),
        cost_estimate=pl.CostEstimate(
            flops=4 * n * m * width * len(others),
            bytes_accessed=2 * width * (n + m * len(others)),
            transcendentals=2 * n * m * len(others),
        ),
        name="tile",
    )(sharpness, offset, mine, *others, *totals)


def finish(sums, embed):
    def kernel(sums_ref, embed_ref, out_ref):
        inv, unit = normalize(embed_ref[...])
        grad = jnp.sum(sums_ref[...].astype(F32), axis=0)
        along = jnp.sum(grad * unit, axis=1, keepdims=True)
        out_ref[...] = (inv * (grad - along * unit)).astype(BF)

    return pl.pallas_call(
        kernel,
        out_shape=pltpu.VMEM(embed.shape, BF),
        in_specs=[VMEM] * 2,
        out_specs=VMEM,
        compiler_params=pltpu.CompilerParams(vmem_limit_bytes=20 * MIB),
        name="finish",
    )(sums, embed)


def heads_back(delta, vision_map, sentence_map, chunks=3):
    own, width = delta.shape[1:]
    rows, depth = 2 * own, vision_map.shape[0]
    step = depth // chunks

    def kernel(d, wv, ws, image, text, buf, sems):
        copies = []
        for tower, (w, out) in enumerate(((wv, image), (ws, text))):
            x = jnp.concatenate([d[tower], d[2 + tower]], axis=0)
            for c in range(chunks):
                cut = slice(c * step, (c + 1) * step)
                part = lax.dot_general(x, w[cut], (((1,), (1,)), ((), ())), preferred_element_type=F32)
                buf[tower, :, cut] = part.astype(BF)
                copy = pltpu.make_async_copy(buf.at[tower, :, cut], out.at[:, cut], sems.at[tower, c])
                copy.start()
                copies.append(copy)
        for copy in copies:
            copy.wait()

    return pl.pallas_call(
        kernel,
        out_shape=[jax.ShapeDtypeStruct((rows, depth), BF)] * 2,
        in_specs=[VMEM] * 3,
        out_specs=[HBM] * 2,
        scratch_shapes=[pltpu.VMEM((2, rows, depth), BF), pltpu.SemaphoreType.DMA((2, chunks))],
        compiler_params=pltpu.CompilerParams(vmem_limit_bytes=20 * MIB),
        name="heads_back",
    )(delta, vision_map, sentence_map)


def shards(vision, sentence, vision_map, sentence_map, sharpness, offset):
    width = vision_map.shape[1]
    own = vision.shape[0] // 2
    sizes = [lax.axis_size(a) for a in AXES]
    peers = lax.axis_size(PLANE)

    def meet(x):
        return lax.all_to_all(x, AXES, 0, 0, axis_index_groups=opposite_groups(sizes, PLANE))

    parts = lax.all_gather(heads(vision, sentence, vision_map, sentence_map), "core", axis=0)
    given, kept = chip_sums(parts)
    wide, line, embed = units(kept, lax.all_gather(given, "yhi", axis=0), peers)

    wide, line = lax.optimization_barrier((wide, line))
    mine = meet(wide).reshape(peers * own, width)
    line = lax.all_gather(line, AXES, axis=0, tiled=True, axis_index_groups=opposite_groups(sizes, ("zhi",)))
    first, second, third = (
        lax.ppermute(line, AXES, from_line(sizes, steps)) for steps in ((1, 1), (-1, -1), (2, -2))
    )
    grad = tile(sharpness, offset, mine, [line], None, own, positives=True)
    grad = tile(sharpness, offset, mine, [third], grad, own)
    grad = tile(sharpness, offset, mine, [first, second], grad, own, final=True)

    grad = meet(grad.reshape(peers, own, width))
    delta = lax.all_gather(finish(grad, embed), GROUP, axis=0)
    return tuple(heads_back(delta, vision_map, sentence_map))


def solution(mesh):
    x, ylo, zlo = 4, 2, 4
    zhi = mesh.shape["dp"] // (x * ylo * zlo)
    fine = Mesh(mesh.devices.reshape(ylo, zhi, zlo, x, 2, 2), AXES)
    dp, mp = ("ylo", "zhi", "zlo", "x"), ("yhi", "core")
    in_specs = (P(dp, mp), P(dp, mp), P(mp, None), P(mp, None), P(), P())
    out_specs = (P(dp, mp), P(dp, mp))
    return jax.shard_map(shards, mesh=fine, in_specs=in_specs, out_specs=out_specs, check_vma=False)
```

```python
import math

import jax
import jax.numpy as jnp
import numpy as np
from jax import lax
from jax.experimental import pallas as pl
from jax.experimental.pallas import tpu as pltpu
from jax.sharding import Mesh
from jax.sharding import PartitionSpec as P

EPS = 1e-06
LOG2E = math.log2(math.e)
BF = jnp.bfloat16
F32 = jnp.float32
MIB = 2**20
AXES = ("ylo", "zhi", "zlo", "x", "yhi", "core")
LINE = ("zhi", "zlo")
PLANE = ("ylo", "x", "yhi")
GROUP = ("yhi", "core")

VMEM = pl.BlockSpec(memory_space=pltpu.VMEM)
SMEM = pl.BlockSpec(memory_space=pltpu.SMEM)
HBM = pl.BlockSpec(memory_space=pltpu.MemorySpace.HBM)


def normalize(embed):
    inv = lax.rsqrt(jnp.sum(embed * embed, axis=1, keepdims=True) + EPS)
    return (inv, embed * inv)


def far_groups(sizes):
    ids = np.arange(math.prod(sizes)).reshape(sizes)
    groups = []
    for core in range(2):
        part = np.moveaxis(ids[..., core], 1, -1).reshape(-1, sizes[1])
        groups += (part[:, ::-1] if core == 1 else part).tolist()
    return groups


def from_line(sizes, steps):
    ids = np.arange(math.prod(sizes)).reshape(sizes)
    pairs = []
    for core, step in enumerate(steps):
        target = ids[..., core].transpose(1, 2, 0, 3, 4).reshape(sizes[1] * sizes[2], -1)
        source = np.roll(target, -step, axis=0)
        pairs += zip(source.ravel().tolist(), target.ravel().tolist())
    return pairs


def heads(vision, sentence, vision_map, sentence_map, chunks=3):
    rows, depth = vision.shape
    width = vision_map.shape[1]
    own, step = rows // 2, depth // chunks

    def kernel(v, s, wv, ws, out, vb, sb, wvb, wsb, sems):
        towers = ((v, wv, vb, wvb), (s, ws, sb, wsb))
        copies = []
        for tower, (x, w, xb, wb) in enumerate(towers):
            for c in range(chunks):
                cut = pl.ds(c * step, step)
                pair = (
                    pltpu.make_async_copy(x.at[:, cut], xb.at[:, cut], sems.at[tower, c, 0]),
                    pltpu.make_async_copy(w.at[cut], wb.at[cut], sems.at[tower, c, 1]),
                )
                for copy in pair:
                    copy.start()
                copies.append(pair)
        for tower, (_, _, xb, wb) in enumerate(towers):
            total = None
            for c in range(chunks):
                for copy in copies[tower * chunks + c]:
                    copy.wait()
                cut = slice(c * step, (c + 1) * step)
                part = jnp.dot(xb[:, cut], wb[cut], preferred_element_type=F32)
                total = part if total is None else total + part
            total = total.astype(BF)
            for half in range(2):
                out[half, :, tower * width : (tower + 1) * width] = total[half * own : (half + 1) * own]

    return pl.pallas_call(
        kernel,
        out_shape=pltpu.VMEM((2, own, 2 * width), BF),
        in_specs=[HBM] * 4,
        out_specs=VMEM,
        scratch_shapes=[
            pltpu.VMEM((rows, depth), BF),
            pltpu.VMEM((rows, depth), BF),
            pltpu.VMEM((depth, width), BF),
            pltpu.VMEM((depth, width), BF),
            pltpu.SemaphoreType.DMA((2, chunks, 2)),
        ],
        compiler_params=pltpu.CompilerParams(vmem_limit_bytes=63 * MIB),
        name="heads",
    )(vision, sentence, vision_map, sentence_map)


def chip_sums(parts):
    _, _, own, width = parts.shape

    def kernel(parts_ref, given_ref, kept_ref):
        for yhi in range(2):

            @pl.when(lax.axis_index("yhi") == yhi)
            def _():
                total = [parts_ref[0, h].astype(F32) + parts_ref[1, h].astype(F32) for h in (yhi, 1 - yhi)]
                kept_ref[...] = total[0]
                given_ref[...] = total[1].astype(BF)

    return pl.pallas_call(
        kernel,
        out_shape=[pltpu.VMEM((own, width), BF), pltpu.VMEM((own, width), F32)],
        in_specs=[VMEM],
        out_specs=[VMEM, VMEM],
        compiler_params=pltpu.CompilerParams(vmem_limit_bytes=20 * MIB),
        name="chip_sums",
    )(parts)


def units(kept, got, peers):
    own, width = kept.shape[0], kept.shape[1] // 2

    def kernel(kept_ref, got_ref, wide_ref, line_ref, embed_ref, mine, sems):
        towers = [slice(0, width), slice(width, 2 * width)]
        for yhi in range(2):
            for core in range(2):

                @pl.when((lax.axis_index("yhi") == yhi) & (lax.axis_index("core") == core))
                def _():
                    embed = [kept_ref[:, cut] + got_ref[1 - yhi, :, cut].astype(F32) for cut in towers]
                    embed_ref[...] = embed[core]
                    mine[...] = normalize(embed[core])[1].astype(BF)
                    line_ref[...] = normalize(embed[1 - core])[1].astype(BF)

        copies = [pltpu.make_async_copy(mine, wide_ref.at[peer], sems.at[peer]) for peer in range(peers)]
        for copy in copies:
            copy.start()
        for copy in copies:
            copy.wait()

    return pl.pallas_call(
        kernel,
        out_shape=[
            jax.ShapeDtypeStruct((peers, own, width), BF),
            pltpu.VMEM((own, width), BF),
            pltpu.VMEM((own, width), F32),
        ],
        in_specs=[VMEM] * 2,
        out_specs=[HBM, VMEM, VMEM],
        scratch_shapes=[pltpu.VMEM((own, width), BF), pltpu.SemaphoreType.DMA((peers,))],
        compiler_params=pltpu.CompilerParams(vmem_limit_bytes=20 * MIB),
        name="units",
    )(kept, got)


def tile(sharpness, offset, mine, others, total, own, positives=False, final=False, block=256):
    n, width = mine.shape
    m = others[0].shape[0]
    blocks = n // block

    def kernel(t_ref, b_ref, mine_ref, *rest):
        out_ref = rest[-1]
        t = t_ref[0]
        slope, start = -LOG2E * t, -LOG2E * b_ref[0]
        zhi, last = lax.axis_index("zhi"), lax.axis_size("zhi") - 1
        mine_at = lax.axis_index(PLANE) * own
        other_at = jnp.where(lax.axis_index("core") == 0, zhi, last - zhi) * own
        for i in range(blocks):
            at = pl.multiple_of(lax.rem(mine_at // block + 1 + i, blocks) * block, block)
            sums = None if total is None else rest[len(others)][pl.ds(at, block)]
            for other_ref in rest[: len(others)]:
                dots = lax.dot_general(
                    mine_ref[pl.ds(at, block)], other_ref[...], (((1,), (1,)), ((), ())), preferred_element_type=F32
                )
                e = jnp.exp2(dots * slope + start)
                coef = pl.reciprocal(1.0 + e)
                if positives and i == blocks - 1:
                    row = lax.broadcasted_iota(jnp.int32, (block, 1), 0) + (at - mine_at)
                    row = jnp.where((row >= 0) & (row < own), row, -m)
                    col = lax.broadcasted_iota(jnp.int32, (1, m), 1) - other_at
                    coef = jnp.where(row == col, -e, 1.0) * coef
                part = jnp.dot(coef.astype(BF), other_ref[...], preferred_element_type=F32)
                sums = part if sums is None else sums + part
            out_ref[pl.ds(at, block)] = (t * sums).astype(BF) if final else sums

    totals = [] if total is None else [total]
    return pl.pallas_call(
        kernel,
        out_shape=pltpu.VMEM((n, width), BF if final else F32),
        in_specs=[SMEM, SMEM, VMEM] + [VMEM] * (len(others) + len(totals)),
        out_specs=VMEM,
        compiler_params=pltpu.CompilerParams(vmem_limit_bytes=30 * MIB),
        cost_estimate=pl.CostEstimate(
            flops=4 * n * m * width * len(others),
            bytes_accessed=2 * width * (n + m * len(others)),
            transcendentals=2 * n * m * len(others),
        ),
        name="tile",
    )(sharpness, offset, mine, *others, *totals)


def finish(sums, embed):
    def kernel(sums_ref, embed_ref, out_ref):
        inv, unit = normalize(embed_ref[...])
        grad = jnp.sum(sums_ref[...].astype(F32), axis=0)
        along = jnp.sum(grad * unit, axis=1, keepdims=True)
        out_ref[...] = (inv * (grad - along * unit)).astype(BF)

    return pl.pallas_call(
        kernel,
        out_shape=pltpu.VMEM(embed.shape, BF),
        in_specs=[VMEM] * 2,
        out_specs=VMEM,
        compiler_params=pltpu.CompilerParams(vmem_limit_bytes=20 * MIB),
        name="finish",
    )(sums, embed)


def heads_back(delta, vision_map, sentence_map, chunks=3):
    own, width = delta.shape[1:]
    rows, depth = 2 * own, vision_map.shape[0]
    step = depth // chunks

    def kernel(d, wv, ws, image, text, buf, sems):
        copies = []
        for tower, (w, out) in enumerate(((wv, image), (ws, text))):
            x = jnp.concatenate([d[tower], d[2 + tower]], axis=0)
            for c in range(chunks):
                cut = slice(c * step, (c + 1) * step)
                part = lax.dot_general(x, w[cut], (((1,), (1,)), ((), ())), preferred_element_type=F32)
                buf[tower, :, cut] = part.astype(BF)
                copy = pltpu.make_async_copy(buf.at[tower, :, cut], out.at[:, cut], sems.at[tower, c])
                copy.start()
                copies.append(copy)
        for copy in copies:
            copy.wait()

    return pl.pallas_call(
        kernel,
        out_shape=[jax.ShapeDtypeStruct((rows, depth), BF)] * 2,
        in_specs=[VMEM] * 3,
        out_specs=[HBM] * 2,
        scratch_shapes=[pltpu.VMEM((2, rows, depth), BF), pltpu.SemaphoreType.DMA((2, chunks))],
        compiler_params=pltpu.CompilerParams(vmem_limit_bytes=20 * MIB),
        name="heads_back",
    )(delta, vision_map, sentence_map)


def shards(vision, sentence, vision_map, sentence_map, sharpness, offset):
    width = vision_map.shape[1]
    own = vision.shape[0] // 2
    sizes = [lax.axis_size(a) for a in AXES]
    peers = lax.axis_size(PLANE)

    parts = lax.all_gather(heads(vision, sentence, vision_map, sentence_map), "core", axis=0)
    given, kept = chip_sums(parts)
    wide, line, embed = units(kept, lax.all_gather(given, "yhi", axis=0), peers)

    wide, line = lax.optimization_barrier((wide, line))
    mine = lax.all_to_all(wide, PLANE, 0, 0).reshape(peers * own, width)
    line = lax.all_gather(line, AXES, axis=0, tiled=True, axis_index_groups=far_groups(sizes))
    first, second, third = (
        lax.ppermute(line, AXES, from_line(sizes, steps)) for steps in ((1, 1), (-1, -1), (-2, 2))
    )
    grad = tile(sharpness, offset, mine, [line], None, own, positives=True)
    grad = tile(sharpness, offset, mine, [third], grad, own)
    grad = tile(sharpness, offset, mine, [first, second], grad, own, final=True)

    grad = lax.all_to_all(grad.reshape(peers, own, width), PLANE, 0, 0)
    delta = lax.all_gather(finish(grad, embed), GROUP, axis=0)
    return tuple(heads_back(delta, vision_map, sentence_map))


def solution(mesh):
    x, ylo, zlo = 4, 2, 4
    zhi = mesh.shape["dp"] // (x * ylo * zlo)
    fine = Mesh(mesh.devices.reshape(ylo, zhi, zlo, x, 2, 2), AXES)
    dp, mp = ("ylo", "zhi", "zlo", "x"), ("yhi", "core")
    in_specs = (P(dp, mp), P(dp, mp), P(mp, None), P(mp, None), P(), P())
    out_specs = (P(dp, mp), P(dp, mp))
    return jax.shard_map(shards, mesh=fine, in_specs=in_specs, out_specs=out_specs, check_vma=False)
```

```python
import math

import jax
import jax.numpy as jnp
import numpy as np
from jax import lax
from jax.experimental import pallas as pl
from jax.experimental.pallas import tpu as pltpu
from jax.sharding import Mesh
from jax.sharding import PartitionSpec as P

EPS = 1e-06
LOG2E = math.log2(math.e)
BF = jnp.bfloat16
F32 = jnp.float32
MIB = 2**20
AXES = ("ylo", "zhi", "zlo", "x", "yhi", "core")
LINE = ("zhi", "zlo")
PLANE = ("ylo", "x", "yhi")
GROUP = ("yhi", "core")

VMEM = pl.BlockSpec(memory_space=pltpu.VMEM)
SMEM = pl.BlockSpec(memory_space=pltpu.SMEM)
HBM = pl.BlockSpec(memory_space=pltpu.MemorySpace.HBM)


def normalize(embed):
    inv = lax.rsqrt(jnp.sum(embed * embed, axis=1, keepdims=True) + EPS)
    return (inv, embed * inv)


def from_line(sizes, steps):
    ids = np.arange(math.prod(sizes)).reshape(sizes)
    pairs = []
    for core, step in enumerate(steps):
        target = ids[..., core].transpose(1, 2, 0, 3, 4).reshape(sizes[1] * sizes[2], -1)
        source = np.roll(target, -step, axis=0)
        pairs += zip(source.ravel().tolist(), target.ravel().tolist())
    return pairs


def heads(vision, sentence, vision_map, sentence_map, chunks=3):
    rows, depth = vision.shape
    width = vision_map.shape[1]
    own, step = rows // 2, depth // chunks

    def kernel(v, s, wv, ws, out, vb, sb, wvb, wsb, sems):
        towers = ((v, wv, vb, wvb), (s, ws, sb, wsb))
        copies = []
        for tower, (x, w, xb, wb) in enumerate(towers):
            for c in range(chunks):
                cut = pl.ds(c * step, step)
                pair = (
                    pltpu.make_async_copy(x.at[:, cut], xb.at[:, cut], sems.at[tower, c, 0]),
                    pltpu.make_async_copy(w.at[cut], wb.at[cut], sems.at[tower, c, 1]),
                )
                for copy in pair:
                    copy.start()
                copies.append(pair)
        for tower, (_, _, xb, wb) in enumerate(towers):
            total = None
            for c in range(chunks):
                for copy in copies[tower * chunks + c]:
                    copy.wait()
                cut = slice(c * step, (c + 1) * step)
                part = jnp.dot(xb[:, cut], wb[cut], preferred_element_type=F32)
                total = part if total is None else total + part
            total = total.astype(BF)
            for half in range(2):
                out[half, :, tower * width : (tower + 1) * width] = total[half * own : (half + 1) * own]

    return pl.pallas_call(
        kernel,
        out_shape=pltpu.VMEM((2, own, 2 * width), BF),
        in_specs=[HBM] * 4,
        out_specs=VMEM,
        scratch_shapes=[
            pltpu.VMEM((rows, depth), BF),
            pltpu.VMEM((rows, depth), BF),
            pltpu.VMEM((depth, width), BF),
            pltpu.VMEM((depth, width), BF),
            pltpu.SemaphoreType.DMA((2, chunks, 2)),
        ],
        compiler_params=pltpu.CompilerParams(vmem_limit_bytes=63 * MIB),
        name="heads",
    )(vision, sentence, vision_map, sentence_map)


def chip_sums(parts):
    _, _, own, width = parts.shape

    def kernel(parts_ref, given_ref, kept_ref):
        for yhi in range(2):

            @pl.when(lax.axis_index("yhi") == yhi)
            def _():
                total = [parts_ref[0, h].astype(F32) + parts_ref[1, h].astype(F32) for h in (yhi, 1 - yhi)]
                kept_ref[...] = total[0]
                given_ref[...] = total[1].astype(BF)

    return pl.pallas_call(
        kernel,
        out_shape=[pltpu.VMEM((own, width), BF), pltpu.VMEM((own, width), F32)],
        in_specs=[VMEM],
        out_specs=[VMEM, VMEM],
        compiler_params=pltpu.CompilerParams(vmem_limit_bytes=20 * MIB),
        name="chip_sums",
    )(parts)


def units(kept, got, peers):
    own, width = kept.shape[0], kept.shape[1] // 2

    def kernel(kept_ref, got_ref, wide_ref, line_ref, embed_ref, mine, sems):
        towers = [slice(0, width), slice(width, 2 * width)]
        for yhi in range(2):
            for core in range(2):

                @pl.when((lax.axis_index("yhi") == yhi) & (lax.axis_index("core") == core))
                def _():
                    embed = [kept_ref[:, cut] + got_ref[1 - yhi, :, cut].astype(F32) for cut in towers]
                    embed_ref[...] = embed[core]
                    mine[...] = normalize(embed[core])[1].astype(BF)
                    line_ref[...] = normalize(embed[1 - core])[1].astype(BF)

        copies = [pltpu.make_async_copy(mine, wide_ref.at[peer], sems.at[peer]) for peer in range(peers)]
        for copy in copies:
            copy.start()
        for copy in copies:
            copy.wait()

    return pl.pallas_call(
        kernel,
        out_shape=[
            jax.ShapeDtypeStruct((peers, own, width), BF),
            pltpu.VMEM((own, width), BF),
            pltpu.VMEM((own, width), F32),
        ],
        in_specs=[VMEM] * 2,
        out_specs=[HBM, VMEM, VMEM],
        scratch_shapes=[pltpu.VMEM((own, width), BF), pltpu.SemaphoreType.DMA((peers,))],
        compiler_params=pltpu.CompilerParams(vmem_limit_bytes=20 * MIB),
        name="units",
    )(kept, got)


def tile(sharpness, offset, mine, others, total, own, positives=False, final=False, block=256):
    n, width = mine.shape
    m = others[0].shape[0]
    blocks = n // block

    def kernel(t_ref, b_ref, mine_ref, *rest):
        out_ref = rest[-1]
        t = t_ref[0]
        slope, start = -LOG2E * t, -LOG2E * b_ref[0]
        mine_at, other_at = lax.axis_index(PLANE) * own, lax.axis_index("zhi") * own
        for i in range(blocks):
            at = pl.multiple_of(lax.rem(mine_at // block + 1 + i, blocks) * block, block)
            sums = None if total is None else rest[len(others)][pl.ds(at, block)]
            for other_ref in rest[: len(others)]:
                dots = lax.dot_general(
                    mine_ref[pl.ds(at, block)], other_ref[...], (((1,), (1,)), ((), ())), preferred_element_type=F32
                )
                e = jnp.exp2(dots * slope + start)
                coef = pl.reciprocal(1.0 + e)
                if positives and i == blocks - 1:
                    row = lax.broadcasted_iota(jnp.int32, (block, 1), 0) + (at - mine_at)
                    row = jnp.where((row >= 0) & (row < own), row, -m)
                    col = lax.broadcasted_iota(jnp.int32, (1, m), 1) - other_at
                    coef = jnp.where(row == col, -e, 1.0) * coef
                part = jnp.dot(coef.astype(BF), other_ref[...], preferred_element_type=F32)
                sums = part if sums is None else sums + part
            out_ref[pl.ds(at, block)] = (t * sums).astype(BF) if final else sums

    totals = [] if total is None else [total]
    return pl.pallas_call(
        kernel,
        out_shape=pltpu.VMEM((n, width), BF if final else F32),
        in_specs=[SMEM, SMEM, VMEM] + [VMEM] * (len(others) + len(totals)),
        out_specs=VMEM,
        compiler_params=pltpu.CompilerParams(vmem_limit_bytes=30 * MIB),
        cost_estimate=pl.CostEstimate(
            flops=4 * n * m * width * len(others),
            bytes_accessed=2 * width * (n + m * len(others)),
            transcendentals=2 * n * m * len(others),
        ),
        name="tile",
    )(sharpness, offset, mine, *others, *totals)


def finish(sums, embed):
    def kernel(sums_ref, embed_ref, out_ref):
        inv, unit = normalize(embed_ref[...])
        grad = jnp.sum(sums_ref[...].astype(F32), axis=0)
        along = jnp.sum(grad * unit, axis=1, keepdims=True)
        out_ref[...] = (inv * (grad - along * unit)).astype(BF)

    return pl.pallas_call(
        kernel,
        out_shape=pltpu.VMEM(embed.shape, BF),
        in_specs=[VMEM] * 2,
        out_specs=VMEM,
        compiler_params=pltpu.CompilerParams(vmem_limit_bytes=20 * MIB),
        name="finish",
    )(sums, embed)


def heads_back(delta, vision_map, sentence_map, chunks=3):
    own, width = delta.shape[1:]
    rows, depth = 2 * own, vision_map.shape[0]
    step = depth // chunks

    def kernel(d, wv, ws, image, text, buf, sems):
        copies = []
        for tower, (w, out) in enumerate(((wv, image), (ws, text))):
            x = jnp.concatenate([d[tower], d[2 + tower]], axis=0)
            for c in range(chunks):
                cut = slice(c * step, (c + 1) * step)
                part = lax.dot_general(x, w[cut], (((1,), (1,)), ((), ())), preferred_element_type=F32)
                buf[tower, :, cut] = part.astype(BF)
                copy = pltpu.make_async_copy(buf.at[tower, :, cut], out.at[:, cut], sems.at[tower, c])
                copy.start()
                copies.append(copy)
        for copy in copies:
            copy.wait()

    return pl.pallas_call(
        kernel,
        out_shape=[jax.ShapeDtypeStruct((rows, depth), BF)] * 2,
        in_specs=[VMEM] * 3,
        out_specs=[HBM] * 2,
        scratch_shapes=[pltpu.VMEM((2, rows, depth), BF), pltpu.SemaphoreType.DMA((2, chunks))],
        compiler_params=pltpu.CompilerParams(vmem_limit_bytes=20 * MIB),
        name="heads_back",
    )(delta, vision_map, sentence_map)


def shards(vision, sentence, vision_map, sentence_map, sharpness, offset):
    width = vision_map.shape[1]
    own = vision.shape[0] // 2
    sizes = [lax.axis_size(a) for a in AXES]
    peers = lax.axis_size(PLANE)

    parts = lax.all_gather(heads(vision, sentence, vision_map, sentence_map), "core", axis=0)
    given, kept = chip_sums(parts)
    wide, line, embed = units(kept, lax.all_gather(given, "yhi", axis=0), peers)

    wide, line = lax.optimization_barrier((wide, line))
    mine = lax.all_to_all(wide, PLANE, 0, 0).reshape(peers * own, width)
    line = lax.all_gather(line, "zhi", axis=0, tiled=True)
    first, second, third = (
        lax.ppermute(line, AXES, from_line(sizes, steps)) for steps in ((1, 1), (-1, -1), (2, -2))
    )
    grad = tile(sharpness, offset, mine, [line], None, own, positives=True)
    grad = tile(sharpness, offset, mine, [third], grad, own)
    grad = tile(sharpness, offset, mine, [first, second], grad, own, final=True)

    grad = lax.all_to_all(grad.reshape(peers, own, width), PLANE, 0, 0)
    delta = lax.all_gather(finish(grad, embed), GROUP, axis=0)
    return tuple(heads_back(delta, vision_map, sentence_map))


def solution(mesh):
    x, ylo, zlo = 4, 2, 4
    zhi = mesh.shape["dp"] // (x * ylo * zlo)
    fine = Mesh(mesh.devices.reshape(ylo, zhi, zlo, x, 2, 2), AXES)
    dp, mp = ("ylo", "zhi", "zlo", "x"), ("yhi", "core")
    in_specs = (P(dp, mp), P(dp, mp), P(mp, None), P(mp, None), P(), P())
    out_specs = (P(dp, mp), P(dp, mp))
    return jax.shard_map(shards, mesh=fine, in_specs=in_specs, out_specs=out_specs, check_vma=False)
```

```python
import math

import jax
import jax.numpy as jnp
import numpy as np
from jax import lax
from jax.experimental import pallas as pl
from jax.experimental.pallas import tpu as pltpu
from jax.sharding import Mesh
from jax.sharding import PartitionSpec as P

EPS = 1e-06
LOG2E = math.log2(math.e)
BF = jnp.bfloat16
F32 = jnp.float32
MIB = 2**20
AXES = ("ylo", "zhi", "zlo", "x", "yhi", "core")
LINE = ("zhi", "zlo")
PLANE = ("ylo", "x", "yhi")
GROUP = ("yhi", "core")

VMEM = pl.BlockSpec(memory_space=pltpu.VMEM)
SMEM = pl.BlockSpec(memory_space=pltpu.SMEM)
HBM = pl.BlockSpec(memory_space=pltpu.MemorySpace.HBM)


def normalize(embed):
    inv = lax.rsqrt(jnp.sum(embed * embed, axis=1, keepdims=True) + EPS)
    return (inv, embed * inv)


def from_line(sizes, steps):
    ids = np.arange(math.prod(sizes)).reshape(sizes)
    pairs = []
    for core, step in enumerate(steps):
        target = ids[..., core].transpose(1, 2, 0, 3, 4).reshape(sizes[1] * sizes[2], -1)
        source = np.roll(target, -step, axis=0)
        pairs += zip(source.ravel().tolist(), target.ravel().tolist())
    return pairs


def heads(vision, sentence, vision_map, sentence_map, chunks=3):
    rows, depth = vision.shape
    width = vision_map.shape[1]
    own, step = rows // 2, depth // chunks

    def kernel(v, s, wv, ws, out, vb, sb, wvb, wsb, sems):
        towers = ((v, wv, vb, wvb), (s, ws, sb, wsb))
        copies = []
        for tower, (x, w, xb, wb) in enumerate(towers):
            for c in range(chunks):
                cut = pl.ds(c * step, step)
                pair = (
                    pltpu.make_async_copy(x.at[:, cut], xb.at[:, cut], sems.at[tower, c, 0]),
                    pltpu.make_async_copy(w.at[cut], wb.at[cut], sems.at[tower, c, 1]),
                )
                for copy in pair:
                    copy.start()
                copies.append(pair)
        for tower, (_, _, xb, wb) in enumerate(towers):
            total = None
            for c in range(chunks):
                for copy in copies[tower * chunks + c]:
                    copy.wait()
                cut = slice(c * step, (c + 1) * step)
                part = jnp.dot(xb[:, cut], wb[cut], preferred_element_type=F32)
                total = part if total is None else total + part
            total = total.astype(BF)
            for half in range(2):
                out[half, :, tower * width : (tower + 1) * width] = total[half * own : (half + 1) * own]

    return pl.pallas_call(
        kernel,
        out_shape=pltpu.VMEM((2, own, 2 * width), BF),
        in_specs=[HBM] * 4,
        out_specs=VMEM,
        scratch_shapes=[
            pltpu.VMEM((rows, depth), BF),
            pltpu.VMEM((rows, depth), BF),
            pltpu.VMEM((depth, width), BF),
            pltpu.VMEM((depth, width), BF),
            pltpu.SemaphoreType.DMA((2, chunks, 2)),
        ],
        compiler_params=pltpu.CompilerParams(vmem_limit_bytes=63 * MIB),
        name="heads",
    )(vision, sentence, vision_map, sentence_map)


def chip_sums(parts):
    _, _, own, width = parts.shape

    def kernel(parts_ref, given_ref, kept_ref):
        for yhi in range(2):

            @pl.when(lax.axis_index("yhi") == yhi)
            def _():
                total = [parts_ref[0, h].astype(F32) + parts_ref[1, h].astype(F32) for h in (yhi, 1 - yhi)]
                kept_ref[...] = total[0]
                given_ref[...] = total[1].astype(BF)

    return pl.pallas_call(
        kernel,
        out_shape=[pltpu.VMEM((own, width), BF), pltpu.VMEM((own, width), F32)],
        in_specs=[VMEM],
        out_specs=[VMEM, VMEM],
        compiler_params=pltpu.CompilerParams(vmem_limit_bytes=20 * MIB),
        name="chip_sums",
    )(parts)


def units(kept, got, peers):
    own, width = kept.shape[0], kept.shape[1] // 2

    def kernel(kept_ref, got_ref, wide_ref, line_ref, embed_ref, mine, sems):
        towers = [slice(0, width), slice(width, 2 * width)]
        for yhi in range(2):
            for core in range(2):

                @pl.when((lax.axis_index("yhi") == yhi) & (lax.axis_index("core") == core))
                def _():
                    embed = [kept_ref[:, cut] + got_ref[1 - yhi, :, cut].astype(F32) for cut in towers]
                    embed_ref[...] = embed[core]
                    mine[...] = normalize(embed[core])[1].astype(BF)
                    line_ref[...] = normalize(embed[1 - core])[1].astype(BF)

        copies = [pltpu.make_async_copy(mine, wide_ref.at[peer], sems.at[peer]) for peer in range(peers)]
        for copy in copies:
            copy.start()
        for copy in copies:
            copy.wait()

    return pl.pallas_call(
        kernel,
        out_shape=[
            jax.ShapeDtypeStruct((peers, own, width), BF),
            pltpu.VMEM((own, width), BF),
            pltpu.VMEM((own, width), F32),
        ],
        in_specs=[VMEM] * 2,
        out_specs=[HBM, VMEM, VMEM],
        scratch_shapes=[pltpu.VMEM((own, width), BF), pltpu.SemaphoreType.DMA((peers,))],
        compiler_params=pltpu.CompilerParams(vmem_limit_bytes=20 * MIB),
        name="units",
    )(kept, got)


def tile(sharpness, offset, mine, others, total, own, positives=False, final=False, block=256):
    n, width = mine.shape
    m = others[0].shape[0]
    blocks = n // block

    def kernel(t_ref, b_ref, mine_ref, *rest):
        out_ref = rest[-1]
        t = t_ref[0]
        slope, start = -LOG2E * t, -LOG2E * b_ref[0]
        mine_at, other_at = lax.axis_index(PLANE) * own, lax.axis_index("zhi") * own
        for i in range(blocks):
            at = pl.multiple_of(lax.rem(mine_at // block + 1 + i, blocks) * block, block)
            sums = None if total is None else rest[len(others)][pl.ds(at, block)]
            for other_ref in rest[: len(others)]:
                dots = lax.dot_general(
                    mine_ref[pl.ds(at, block)], other_ref[...], (((1,), (1,)), ((), ())), preferred_element_type=F32
                )
                e = jnp.exp2(dots * slope + start)
                coef = pl.reciprocal(1.0 + e)
                if positives and i == blocks - 1:
                    row = lax.broadcasted_iota(jnp.int32, (block, 1), 0) + (at - mine_at)
                    row = jnp.where((row >= 0) & (row < own), row, -m)
                    col = lax.broadcasted_iota(jnp.int32, (1, m), 1) - other_at
                    coef = jnp.where(row == col, -e, 1.0) * coef
                part = jnp.dot(coef.astype(BF), other_ref[...], preferred_element_type=F32)
                sums = part if sums is None else sums + part
            out_ref[pl.ds(at, block)] = (t * sums).astype(BF) if final else sums

    totals = [] if total is None else [total]
    return pl.pallas_call(
        kernel,
        out_shape=pltpu.VMEM((n, width), BF if final else F32),
        in_specs=[SMEM, SMEM, VMEM] + [VMEM] * (len(others) + len(totals)),
        out_specs=VMEM,
        compiler_params=pltpu.CompilerParams(vmem_limit_bytes=30 * MIB),
        cost_estimate=pl.CostEstimate(
            flops=4 * n * m * width * len(others),
            bytes_accessed=2 * width * (n + m * len(others)),
            transcendentals=2 * n * m * len(others),
        ),
        name="tile",
    )(sharpness, offset, mine, *others, *totals)


def finish(sums, embed):
    def kernel(sums_ref, embed_ref, out_ref):
        inv, unit = normalize(embed_ref[...])
        grad = jnp.sum(sums_ref[...].astype(F32), axis=0)
        along = jnp.sum(grad * unit, axis=1, keepdims=True)
        out_ref[...] = (inv * (grad - along * unit)).astype(BF)

    return pl.pallas_call(
        kernel,
        out_shape=pltpu.VMEM(embed.shape, BF),
        in_specs=[VMEM] * 2,
        out_specs=VMEM,
        compiler_params=pltpu.CompilerParams(vmem_limit_bytes=20 * MIB),
        name="finish",
    )(sums, embed)


def heads_back(delta, vision_map, sentence_map, chunks=3):
    own, width = delta.shape[1:]
    rows, depth = 2 * own, vision_map.shape[0]
    step = depth // chunks

    def kernel(d, wv, ws, image, text, buf, sems):
        copies = []
        for tower, (w, out) in enumerate(((wv, image), (ws, text))):
            x = jnp.concatenate([d[tower], d[2 + tower]], axis=0)
            for c in range(chunks):
                cut = slice(c * step, (c + 1) * step)
                part = lax.dot_general(x, w[cut], (((1,), (1,)), ((), ())), preferred_element_type=F32)
                buf[tower, :, cut] = part.astype(BF)
                copy = pltpu.make_async_copy(buf.at[tower, :, cut], out.at[:, cut], sems.at[tower, c])
                copy.start()
                copies.append(copy)
        for copy in copies:
            copy.wait()

    return pl.pallas_call(
        kernel,
        out_shape=[jax.ShapeDtypeStruct((rows, depth), BF)] * 2,
        in_specs=[VMEM] * 3,
        out_specs=[HBM] * 2,
        scratch_shapes=[pltpu.VMEM((2, rows, depth), BF), pltpu.SemaphoreType.DMA((2, chunks))],
        compiler_params=pltpu.CompilerParams(vmem_limit_bytes=20 * MIB),
        name="heads_back",
    )(delta, vision_map, sentence_map)


def shards(vision, sentence, vision_map, sentence_map, sharpness, offset):
    width = vision_map.shape[1]
    own = vision.shape[0] // 2
    sizes = [lax.axis_size(a) for a in AXES]
    peers = lax.axis_size(PLANE)

    parts = lax.all_gather(heads(vision, sentence, vision_map, sentence_map), "core", axis=0)
    given, kept = chip_sums(parts)
    wide, line, embed = units(kept, lax.all_gather(given, "yhi", axis=0), peers)

    line = lax.all_gather(line, "zhi", axis=0, tiled=True)
    wide, line = lax.optimization_barrier((wide, line))
    mine = lax.all_to_all(wide, PLANE, 0, 0).reshape(peers * own, width)
    first, second, third = (
        lax.ppermute(line, AXES, from_line(sizes, steps)) for steps in ((1, 1), (-1, -1), (2, -2))
    )
    grad = tile(sharpness, offset, mine, [line], None, own, positives=True)
    grad = tile(sharpness, offset, mine, [third], grad, own)
    grad = tile(sharpness, offset, mine, [first, second], grad, own, final=True)

    grad = lax.all_to_all(grad.reshape(peers, own, width), PLANE, 0, 0)
    delta = lax.all_gather(finish(grad, embed), GROUP, axis=0)
    return tuple(heads_back(delta, vision_map, sentence_map))


def solution(mesh):
    x, ylo, zlo = 4, 2, 4
    zhi = mesh.shape["dp"] // (x * ylo * zlo)
    fine = Mesh(mesh.devices.reshape(ylo, zhi, zlo, x, 2, 2), AXES)
    dp, mp = ("ylo", "zhi", "zlo", "x"), ("yhi", "core")
    in_specs = (P(dp, mp), P(dp, mp), P(mp, None), P(mp, None), P(), P())
    out_specs = (P(dp, mp), P(dp, mp))
    return jax.shard_map(shards, mesh=fine, in_specs=in_specs, out_specs=out_specs, check_vma=False)
```

```python
import math

import jax
import jax.numpy as jnp
import numpy as np
from jax import lax
from jax.experimental import pallas as pl
from jax.experimental.pallas import tpu as pltpu
from jax.sharding import Mesh
from jax.sharding import PartitionSpec as P

EPS = 1e-06
LOG2E = math.log2(math.e)
BF = jnp.bfloat16
F32 = jnp.float32
MIB = 2**20
AXES = ("ylo", "zhi", "zlo", "x", "yhi", "core")
LINE = ("zhi", "zlo")
PLANE = ("ylo", "x", "yhi")
GROUP = ("yhi", "core")

VMEM = pl.BlockSpec(memory_space=pltpu.VMEM)
SMEM = pl.BlockSpec(memory_space=pltpu.SMEM)
HBM = pl.BlockSpec(memory_space=pltpu.MemorySpace.HBM)


def normalize(embed):
    inv = lax.rsqrt(jnp.sum(embed * embed, axis=1, keepdims=True) + EPS)
    return (inv, embed * inv)


def from_line(sizes, steps):
    ids = np.arange(math.prod(sizes)).reshape(sizes)
    pairs = []
    for core, step in enumerate(steps):
        target = ids[..., core].transpose(1, 2, 0, 3, 4).reshape(sizes[1] * sizes[2], -1)
        source = np.roll(target, -step, axis=0)
        pairs += zip(source.ravel().tolist(), target.ravel().tolist())
    return pairs


def heads(vision, sentence, vision_map, sentence_map, chunks=3):
    rows, depth = vision.shape
    width = vision_map.shape[1]
    own, step = rows // 2, depth // chunks

    def kernel(v, s, wv, ws, out, vb, sb, wvb, wsb, sems):
        towers = ((v, wv, vb, wvb), (s, ws, sb, wsb))
        copies = []
        for tower, (x, w, xb, wb) in enumerate(towers):
            for c in range(chunks):
                cut = pl.ds(c * step, step)
                pair = (
                    pltpu.make_async_copy(x.at[:, cut], xb.at[:, cut], sems.at[tower, c, 0]),
                    pltpu.make_async_copy(w.at[cut], wb.at[cut], sems.at[tower, c, 1]),
                )
                for copy in pair:
                    copy.start()
                copies.append(pair)
        for tower, (_, _, xb, wb) in enumerate(towers):
            total = None
            for c in range(chunks):
                for copy in copies[tower * chunks + c]:
                    copy.wait()
                cut = slice(c * step, (c + 1) * step)
                part = jnp.dot(xb[:, cut], wb[cut], preferred_element_type=F32)
                total = part if total is None else total + part
            total = total.astype(BF)
            for half in range(2):
                out[half, :, tower * width : (tower + 1) * width] = total[half * own : (half + 1) * own]

    return pl.pallas_call(
        kernel,
        out_shape=pltpu.VMEM((2, own, 2 * width), BF),
        in_specs=[HBM] * 4,
        out_specs=VMEM,
        scratch_shapes=[
            pltpu.VMEM((rows, depth), BF),
            pltpu.VMEM((rows, depth), BF),
            pltpu.VMEM((depth, width), BF),
            pltpu.VMEM((depth, width), BF),
            pltpu.SemaphoreType.DMA((2, chunks, 2)),
        ],
        compiler_params=pltpu.CompilerParams(vmem_limit_bytes=63 * MIB),
        name="heads",
    )(vision, sentence, vision_map, sentence_map)


def chip_sums(parts):
    _, _, own, width = parts.shape

    def kernel(parts_ref, given_ref, kept_ref):
        for yhi in range(2):

            @pl.when(lax.axis_index("yhi") == yhi)
            def _():
                total = [parts_ref[0, h].astype(F32) + parts_ref[1, h].astype(F32) for h in (yhi, 1 - yhi)]
                kept_ref[...] = total[0]
                given_ref[...] = total[1].astype(BF)

    return pl.pallas_call(
        kernel,
        out_shape=[pltpu.VMEM((own, width), BF), pltpu.VMEM((own, width), F32)],
        in_specs=[VMEM],
        out_specs=[VMEM, VMEM],
        compiler_params=pltpu.CompilerParams(vmem_limit_bytes=20 * MIB),
        name="chip_sums",
    )(parts)


def units(kept, got, peers):
    own, width = kept.shape[0], kept.shape[1] // 2

    def kernel(kept_ref, got_ref, wide_ref, line_ref, embed_ref):
        towers = [slice(0, width), slice(width, 2 * width)]
        for yhi in range(2):
            for core in range(2):

                @pl.when((lax.axis_index("yhi") == yhi) & (lax.axis_index("core") == core))
                def _():
                    embed = [kept_ref[:, cut] + got_ref[1 - yhi, :, cut].astype(F32) for cut in towers]
                    embed_ref[...] = embed[core]
                    mine = normalize(embed[core])[1].astype(BF)
                    for peer in range(peers):
                        wide_ref[peer] = mine
                    line_ref[...] = normalize(embed[1 - core])[1].astype(BF)

    return pl.pallas_call(
        kernel,
        out_shape=[
            pltpu.VMEM((peers, own, width), BF),
            pltpu.VMEM((own, width), BF),
            pltpu.VMEM((own, width), F32),
        ],
        in_specs=[VMEM] * 2,
        out_specs=[VMEM] * 3,
        compiler_params=pltpu.CompilerParams(vmem_limit_bytes=20 * MIB),
        name="units",
    )(kept, got)


def tile(sharpness, offset, mine, others, total, own, positives=False, final=False, block=256):
    n, width = mine.shape
    m = others[0].shape[0]
    blocks = n // block

    def kernel(t_ref, b_ref, mine_ref, *rest):
        out_ref = rest[-1]
        t = t_ref[0]
        slope, start = -LOG2E * t, -LOG2E * b_ref[0]
        mine_at, other_at = lax.axis_index(PLANE) * own, lax.axis_index("zhi") * own
        for i in range(blocks):
            at = pl.multiple_of(lax.rem(mine_at // block + 1 + i, blocks) * block, block)
            sums = None if total is None else rest[len(others)][pl.ds(at, block)]
            for other_ref in rest[: len(others)]:
                dots = lax.dot_general(
                    mine_ref[pl.ds(at, block)], other_ref[...], (((1,), (1,)), ((), ())), preferred_element_type=F32
                )
                e = jnp.exp2(dots * slope + start)
                coef = pl.reciprocal(1.0 + e)
                if positives and i == blocks - 1:
                    row = lax.broadcasted_iota(jnp.int32, (block, 1), 0) + (at - mine_at)
                    row = jnp.where((row >= 0) & (row < own), row, -m)
                    col = lax.broadcasted_iota(jnp.int32, (1, m), 1) - other_at
                    coef = jnp.where(row == col, -e, 1.0) * coef
                part = jnp.dot(coef.astype(BF), other_ref[...], preferred_element_type=F32)
                sums = part if sums is None else sums + part
            out_ref[pl.ds(at, block)] = (t * sums).astype(BF) if final else sums

    totals = [] if total is None else [total]
    return pl.pallas_call(
        kernel,
        out_shape=pltpu.VMEM((n, width), BF if final else F32),
        in_specs=[SMEM, SMEM, VMEM] + [VMEM] * (len(others) + len(totals)),
        out_specs=VMEM,
        compiler_params=pltpu.CompilerParams(vmem_limit_bytes=30 * MIB),
        cost_estimate=pl.CostEstimate(
            flops=4 * n * m * width * len(others),
            bytes_accessed=2 * width * (n + m * len(others)),
            transcendentals=2 * n * m * len(others),
        ),
        name="tile",
    )(sharpness, offset, mine, *others, *totals)


def finish(sums, embed):
    def kernel(sums_ref, embed_ref, out_ref):
        inv, unit = normalize(embed_ref[...])
        grad = jnp.sum(sums_ref[...].astype(F32), axis=0)
        along = jnp.sum(grad * unit, axis=1, keepdims=True)
        out_ref[...] = (inv * (grad - along * unit)).astype(BF)

    return pl.pallas_call(
        kernel,
        out_shape=pltpu.VMEM(embed.shape, BF),
        in_specs=[VMEM] * 2,
        out_specs=VMEM,
        compiler_params=pltpu.CompilerParams(vmem_limit_bytes=20 * MIB),
        name="finish",
    )(sums, embed)


def heads_back(delta, vision_map, sentence_map, chunks=3):
    own, width = delta.shape[1:]
    rows, depth = 2 * own, vision_map.shape[0]
    step = depth // chunks

    def kernel(d, wv, ws, image, text, buf, sems):
        copies = []
        for tower, (w, out) in enumerate(((wv, image), (ws, text))):
            x = jnp.concatenate([d[tower], d[2 + tower]], axis=0)
            for c in range(chunks):
                cut = slice(c * step, (c + 1) * step)
                part = lax.dot_general(x, w[cut], (((1,), (1,)), ((), ())), preferred_element_type=F32)
                buf[tower, :, cut] = part.astype(BF)
                copy = pltpu.make_async_copy(buf.at[tower, :, cut], out.at[:, cut], sems.at[tower, c])
                copy.start()
                copies.append(copy)
        for copy in copies:
            copy.wait()

    return pl.pallas_call(
        kernel,
        out_shape=[jax.ShapeDtypeStruct((rows, depth), BF)] * 2,
        in_specs=[VMEM] * 3,
        out_specs=[HBM] * 2,
        scratch_shapes=[pltpu.VMEM((2, rows, depth), BF), pltpu.SemaphoreType.DMA((2, chunks))],
        compiler_params=pltpu.CompilerParams(vmem_limit_bytes=20 * MIB),
        name="heads_back",
    )(delta, vision_map, sentence_map)


def shards(vision, sentence, vision_map, sentence_map, sharpness, offset):
    width = vision_map.shape[1]
    own = vision.shape[0] // 2
    sizes = [lax.axis_size(a) for a in AXES]
    peers = lax.axis_size(PLANE)

    parts = lax.all_gather(heads(vision, sentence, vision_map, sentence_map), "core", axis=0)
    given, kept = chip_sums(parts)
    wide, line, embed = units(kept, lax.all_gather(given, "yhi", axis=0), peers)

    wide, line = lax.optimization_barrier((wide, line))
    mine = lax.all_to_all(wide, PLANE, 0, 0).reshape(peers * own, width)
    line = lax.all_gather(line, "zhi", axis=0, tiled=True)
    first, second, third = (
        lax.ppermute(line, AXES, from_line(sizes, steps)) for steps in ((1, 1), (-1, -1), (2, -2))
    )
    grad = tile(sharpness, offset, mine, [line], None, own, positives=True)
    grad = tile(sharpness, offset, mine, [third], grad, own)
    grad = tile(sharpness, offset, mine, [first, second], grad, own, final=True, block=1024)

    grad = lax.all_to_all(grad.reshape(peers, own, width), PLANE, 0, 0)
    delta = lax.all_gather(finish(grad, embed), GROUP, axis=0)
    return tuple(heads_back(delta, vision_map, sentence_map))


def solution(mesh):
    x, ylo, zlo = 4, 2, 4
    zhi = mesh.shape["dp"] // (x * ylo * zlo)
    fine = Mesh(mesh.devices.reshape(ylo, zhi, zlo, x, 2, 2), AXES)
    dp, mp = ("ylo", "zhi", "zlo", "x"), ("yhi", "core")
    in_specs = (P(dp, mp), P(dp, mp), P(mp, None), P(mp, None), P(), P())
    out_specs = (P(dp, mp), P(dp, mp))
    return jax.shard_map(shards, mesh=fine, in_specs=in_specs, out_specs=out_specs, check_vma=False)
```
